32 devices in a mesh: expert: 16 (over z, y, core), blk: 2 (over x).
Axes of the slice: x: 2, y: 2, z: 4, core: 2. Of those that a mesh axis runs over, the one named last changes fastest.
Arguments:
- tokens: bfloat16 [2048, 7168], P(('expert', 'blk')), may hold values from -6 to 6
- expert_ids: int32 [2048, 8], P(('expert', 'blk')), may hold values from 0 to 255, all different within a row; in each aligned block of 64 rows (0 to 63, 64 to 127, ...) at most 4 rows name the same one
- gate_weights: bfloat16 [2048, 8], P(('expert', 'blk')), may hold values from 0.099609375 to 1
- w_gate: bfloat16 [16, 7168, 2048], P('expert', None, 'blk'), may hold values from -0.0625 to 0.0625
- w_up: bfloat16 [16, 7168, 2048], P('expert', None, 'blk'), may hold values from -0.0625 to 0.0625
- w_down: bfloat16 [16, 2048, 7168], P('expert', None, 'blk'), may hold values from -0.125 to 0.125
Outputs:
- mixed_out: bfloat16 [2048, 7168], P(('expert', 'blk'))
The draws below stay inside these ranges and needn't reach their ends.
Inputs may be any that keep to these rules, and one draw needn't show every extreme that they name: `expert_ids`: each row names 8 different experts; among the 64 rows of one device no expert is named more than 4 times, a bound that some block reaches.
All inputs are finite; a program needn't handle non-finite values.
Results may differ from the reference program's by a relative error of at most 0.0057.
Values may be sent and summed in bfloat16 or wider, within the bound.
No kernel may reach another device: no remote copies, remote signals or barrier semaphores. Data moves between devices by JAX's collectives and lax.ppermute only.
A program may use at most 128 MiB of HBM per device.

```python
import math
import jax
import jax.numpy as jnp
import numpy as np
from jax import lax

D = 7168
FF = 2048
ROUTED = 256
TOP = 8
TOK_DEV = 64
CAP = 4
EXPERTS = 16
TOKENS = 2048
N_EXPERT = 16
N_BLK = 2


def levels(key, shape, shards, smallest, largest):
    gain, own = 1.0, jax.random.fold_in(key, 6)
    for dim, shards_of in shards:
        draws = jnp.exp(jax.random.uniform(jax.random.fold_in(own, dim), (shards_of,), jnp.float32, smallest / len(shards), largest / len(shards)))
        gain = gain * jnp.repeat(draws, shape[dim] // shards_of).reshape([-1 if axis == dim else 1 for axis in range(len(shape))])
    return gain


def routed_block(rng, own, number, rows, count, top, bound, lean):
    order = jax.random.permutation(rng, count)
    packed, common = portions_of(count, rows * top, bound, lean, True), portions_of(count, rows * top, bound, lean, False)
    places = jnp.arange(count)

    def named(tallies, rotation):
        used = int((tallies > 0).sum())
        fixed = max(1, used // 4)
        shifted = fixed + (places - fixed + rotation * (used - fixed)) % max(1, count - fixed)
        return jnp.zeros((count,), jnp.int32).at[order[jnp.where(places < fixed, places, shifted)]].set(jnp.asarray(tallies, jnp.int32))

    tallies = jnp.where(number % 4 == 0, named(packed, number // 4), named(common, number - number // 4 - 1))
    mixed = jax.random.permutation(jax.random.fold_in(own, 3), count)
    source_of, receiver = mixed[0:count // 2 * 2:2], mixed[1:count // 2 * 2:2]
    room = jnp.minimum(tallies[source_of] - 1, bound - tallies[receiver]) // 2
    room = jnp.where((source_of == order[0]) | (receiver == order[0]) | (tallies[receiver] == 0), 0, jnp.maximum(room, 0))
    shifted = jax.random.randint(jax.random.fold_in(own, 4), (count // 2,), 0, 1 << 20) % (room + 1)
    tallies = tallies.at[source_of].add(-shifted).at[receiver].add(shifted)
    members = jnp.searchsorted(jnp.cumsum(tallies), jnp.arange(rows * top), side="right").astype(jnp.int32)
    table = members.reshape(top, rows).T
    table = table[jax.random.permutation(jax.random.fold_in(own, 1), rows)]
    rotation = jax.random.randint(jax.random.fold_in(own, 2), (rows, 1), 0, top)
    return jnp.take_along_axis(table, (jnp.arange(top)[None, :] + rotation) % top, axis=1)


def portions_of(count, total, bound, skew, full):
    weights = [(1 << 20) // math.isqrt(standing ** skew) + 1 for standing in range(1, count + 1)]
    largest = bound if full else min(bound, max(-(-total // count), total * weights[0] // sum(weights)))
    least = 1 if total - largest >= count - 1 else 0
    holding, rest = [largest] + [least] * (count - 1), total - largest - least * (count - 1)
    while rest > 0:
        candidates = [i for i in range(1, count) if holding[i] < largest] or [i for i in range(1, count) if holding[i] < bound]
        mass, remaining = sum([weights[i] for i in candidates]), rest
        for i in candidates:
            addition = min(bound - holding[i], max(1, remaining * weights[i] // mass), rest)
            holding[i] = holding[i] + addition
            rest = rest - addition
    return np.array(holding)


def gaussian(own_key, dims, width, most, pieces=(), kind=jnp.bfloat16):
    level = levels(own_key, dims, pieces, -0.22, 0.18) if pieces else 1.0
    drawn = jax.random.normal(own_key, dims, jnp.float32) * width * level
    return jnp.minimum(jnp.maximum(drawn, -most), most).astype(kind)


def setup_inputs(seed: int = 0) -> dict:
    keys = jax.random.split(jax.random.key(seed), 7)
    tokens = gaussian(keys[0], (TOKENS, D), 1.0, 6.0, ((0, 32),))
    expert_ids_keys = jax.random.split(jax.random.fold_in(keys[1], 1), TOKENS // TOK_DEV)
    expert_ids_turns = jax.random.permutation(jax.random.fold_in(keys[1], 3), TOKENS // TOK_DEV)
    expert_ids = jax.vmap(lambda own, number: routed_block(jax.random.fold_in(keys[1], 2), own, number, TOK_DEV, ROUTED, TOP, CAP, 2))(expert_ids_keys, expert_ids_turns).reshape((TOKENS, TOP))
    gate_weights = jnp.clip(jnp.exp(math.log(1.0) - 2.306499 * jax.random.uniform(keys[2], (TOKENS, TOP), jnp.float32) ** levels(keys[2], (TOKENS, TOP), ((0, 32),), -0.2, 0.2)), 0.099609375, 1.0).astype(jnp.bfloat16)
    w_gate = gaussian(keys[3], (EXPERTS, D, FF), D ** -0.5, 0.0625, ((0, 16), (2, 2)))
    w_up = gaussian(keys[4], (EXPERTS, D, FF), D ** -0.5, 0.0625, ((0, 16), (2, 2)))
    w_down = gaussian(keys[5], (EXPERTS, FF, D), FF ** -0.5, 0.125, ((0, 16), (2, 2)))
    return {"tokens": tokens, "expert_ids": expert_ids, "gate_weights": gate_weights, "w_gate": w_gate, "w_up": w_up, "w_down": w_down}


def reference(tokens, expert_ids, gate_weights, w_gate, w_up, w_down):
    most_rows = N_EXPERT * N_BLK * CAP
    tokens_wide = tokens.astype(jnp.float32)
    labels = jnp.arange(EXPERTS, dtype=jnp.int32)

    def one_expert(running, inputs):
        expert_label, gate_mat, up_mat, down_mat = inputs
        matches = expert_ids == expert_label
        chosen = jnp.any(matches, axis=1)
        weights = jnp.sum(jnp.where(matches, gate_weights.astype(jnp.float32), 0.0), axis=1)
        row_index = jnp.nonzero(chosen, size=most_rows, fill_value=0)[0].astype(jnp.int32)
        valid_rows = jnp.arange(most_rows) < jnp.sum(chosen.astype(jnp.int32))
        row_block = tokens_wide[row_index]
        gate_part = jnp.dot(row_block, gate_mat.astype(jnp.float32), precision=lax.Precision.HIGHEST)
        up_part = jnp.dot(row_block, up_mat.astype(jnp.float32), precision=lax.Precision.HIGHEST)
        hidden = (jax.nn.silu(gate_part) * up_part).astype(jnp.bfloat16)
        hidden = lax.optimization_barrier(hidden).astype(jnp.float32)
        outputs = jnp.dot(hidden, down_mat.astype(jnp.float32), precision=lax.Precision.HIGHEST).astype(jnp.bfloat16)
        outputs = lax.optimization_barrier(outputs).astype(jnp.float32)
        scale = jnp.where(valid_rows, weights[row_index], 0.0)
        contribution = scale[:, None] * outputs
        running = running.at[row_index].add(contribution)
        return running, None

    start = jnp.zeros(tokens.shape, jnp.float32)
    running, unused = lax.scan(one_expert, start, (labels, w_gate, w_up, w_down))
    return running.astype(jnp.bfloat16)
```

```python
import jax
import jax.numpy as jnp
from jax import lax
from jax.sharding import PartitionSpec as P

CAP = 4
CHUNKS = 4


def slot_tables(id_rows, gate_rows, experts, capacity):
    labels = jnp.arange(experts, dtype=jnp.int32)
    matches = id_rows[:, :, None] == labels[None, None, :]
    chosen = jnp.any(matches, axis=1)
    weights = jnp.sum(jnp.where(matches, gate_rows.astype(jnp.float32)[:, :, None], 0.0), axis=1)
    counts = chosen.astype(jnp.int32)
    before = jnp.cumsum(counts, axis=0) - counts
    places = jnp.arange(capacity, dtype=jnp.int32)
    selected = chosen[:, :, None] & (before[:, :, None] == places[None, None, :])
    selector = selected.astype(jnp.bfloat16)
    weighting = jnp.where(selected, weights[:, :, None], 0.0).astype(jnp.bfloat16)
    return (selector, weighting)


def shifted(block, axis, steps):
    size = lax.axis_size(axis)
    return lax.ppermute(block, axis, [(i, (i + steps) % size) for i in range(size)])


def matmul(left, right):
    return jnp.dot(left, right, preferred_element_type=jnp.float32)


def by_owner(parts, owner_of_first, step):
    size = len(parts)
    if size == 2:
        first = owner_of_first == 0
        return [jnp.where(first, parts[0], parts[1]), jnp.where(first, parts[1], parts[0])]
    stacked = jnp.stack(parts)
    order = (step * (jnp.arange(size) - owner_of_first)) % size
    ordered = jnp.take(stacked, order, axis=0)
    return [ordered[k] for k in range(size)]


def on_device(tokens, expert_ids, gate_weights, w_gate, w_up, w_down):
    gate_mat, up_mat, down_mat = w_gate[0], w_up[0], w_down[0]
    experts, blocks = lax.axis_size("expert"), lax.axis_size("blk")
    mine = lax.axis_index("blk")
    width = tokens.shape[1]
    selector, weighting = slot_tables(expert_ids, gate_weights, experts, CAP)

    step = width // CHUNKS
    gate_sum, up_sum = 0.0, 0.0
    for c in range(CHUNKS):
        columns = slice(c * step, (c + 1) * step)
        outgoing = jnp.einsum(
            "tec,td->ecd", selector, tokens[:, columns], preferred_element_type=jnp.float32
        ).astype(jnp.bfloat16)
        received = lax.all_to_all(outgoing, "expert", split_axis=0, concat_axis=0, tiled=True)
        rows = received.reshape(-1, step)
        rows = jnp.concatenate([rows] + [shifted(rows, "blk", k) for k in range(1, blocks)], axis=0)
        gate_sum = gate_sum + matmul(rows, gate_mat[columns])
        up_sum = up_sum + matmul(rows, up_mat[columns])
    hidden = (jax.nn.silu(gate_sum) * up_sum).astype(jnp.bfloat16)

    slots = experts * CAP
    parts = [hidden]
    for k in range(1, blocks):
        parts.append(jnp.roll(shifted(hidden, "blk", k), k * slots, axis=0))
    whole = jnp.concatenate(by_owner(parts, mine, -1), axis=1)
    slices = matmul(whole, down_mat).astype(jnp.bfloat16)

    mixed = []
    for k in range(blocks):
        piece = slices[k * slots:(k + 1) * slots]
        if k:
            piece = shifted(piece, "blk", blocks - k)
        piece = piece.reshape(experts, CAP, -1)
        returned = lax.all_to_all(piece, "expert", split_axis=0, concat_axis=0, tiled=True)
        mixed.append(jnp.einsum(
            "tec,ecd->td", weighting, returned, preferred_element_type=jnp.float32
        ).astype(jnp.bfloat16))
    return jnp.concatenate(by_owner(mixed, mine, 1), axis=1)


def solution(mesh):
    return jax.shard_map(
        on_device,
        mesh=mesh,
        in_specs=(
            P(("expert", "blk"), None),
            P(("expert", "blk"), None),
            P(("expert", "blk"), None),
            P("expert", None, "blk"),
            P("expert", None, "blk"),
            P("expert", None, "blk"),
        ),
        out_specs=P(("expert", "blk"), None),
        check_vma=False,
    )
```

```python
import jax
import jax.numpy as jnp
from jax import lax
from jax.sharding import PartitionSpec as P

CAP = 4
GROUPS = 4
MOST_PAIRS = 16


def slot_tables(id_rows, gate_rows, labels, capacity):
    matches = id_rows[:, :, None] == labels[None, None, :]
    chosen = jnp.any(matches, axis=1)
    weights = jnp.sum(jnp.where(matches, gate_rows.astype(jnp.float32)[:, :, None], 0.0), axis=1)
    counts = chosen.astype(jnp.int32)
    before = jnp.cumsum(counts, axis=0) - counts
    places = jnp.arange(capacity, dtype=jnp.int32)
    selected = chosen[:, :, None] & (before[:, :, None] == places[None, None, :])
    selector = selected.astype(jnp.bfloat16)
    weighting = jnp.where(selected, weights[:, :, None], 0.0).astype(jnp.bfloat16)
    return (selector, weighting)


def partner(index, turn, size):
    return index ^ turn if size & (size - 1) == 0 else (index + turn) % size


def partners(size):
    order = jnp.arange(size, dtype=jnp.int32)
    return order if size > MOST_PAIRS else partner(lax.axis_index("expert"), order, size)


def to_partners(pieces, back=False):
    size = len(pieces)
    if size > MOST_PAIRS:
        swapped = lax.all_to_all(jnp.stack(pieces), "expert", split_axis=0, concat_axis=0, tiled=True)
        return [swapped[r] for r in range(size)]
    received = list(pieces)
    for turn in sorted(range(1, size), reverse=True):
        pairs = [(i, partner(i, turn, size)) for i in range(size)]
        if back:
            pairs = [(to, i) for i, to in pairs]
        received[turn] = lax.ppermute(pieces[turn], "expert", pairs)
    return received


def shifted(block, axis, steps):
    size = lax.axis_size(axis)
    return lax.ppermute(block, axis, [(i, (i + steps) % size) for i in range(size)])


def matmul(left, right):
    return jnp.dot(left, right, preferred_element_type=jnp.float32)


def by_owner(parts, owner_of_first, step):
    size = len(parts)
    if size == 2:
        first = owner_of_first == 0
        return [jnp.where(first, parts[0], parts[1]), jnp.where(first, parts[1], parts[0])]
    stacked = jnp.stack(parts)
    order = (step * (jnp.arange(size) - owner_of_first)) % size
    ordered = jnp.take(stacked, order, axis=0)
    return [ordered[k] for k in range(size)]


def on_device(tokens, expert_ids, gate_weights, w_gate, w_up, w_down):
    gate_mat, up_mat, down_mat = w_gate[0], w_up[0], w_down[0]
    experts, blocks = lax.axis_size("expert"), lax.axis_size("blk")
    mine = lax.axis_index("blk")
    selector, weighting = slot_tables(expert_ids, gate_weights, partners(experts), CAP)

    outgoing = jnp.einsum(
        "tec,td->ecd", selector, tokens, preferred_element_type=jnp.float32
    ).astype(jnp.bfloat16)
    received = to_partners([outgoing[r] for r in range(experts)])
    group = experts // GROUPS
    own, others = [], [[] for k in range(1, blocks)]
    for g in range(GROUPS):
        rows = jnp.concatenate(received[g * group:(g + 1) * group], axis=0)
        own.append(rows)
        for k in range(1, blocks):
            others[k - 1].append(shifted(rows, "blk", k))
    rows = jnp.concatenate(own + sum(others, []), axis=0)
    gate_sum = matmul(rows, gate_mat)
    up_sum = matmul(rows, up_mat)
    hidden = (jax.nn.silu(gate_sum) * up_sum).astype(jnp.bfloat16)

    slots = experts * CAP
    parts = [hidden]
    for k in range(1, blocks):
        parts.append(jnp.roll(shifted(hidden, "blk", k), k * slots, axis=0))
    whole = jnp.concatenate(by_owner(parts, mine, -1), axis=1)
    slices = matmul(whole, down_mat).astype(jnp.bfloat16)

    mixed = []
    for k in range(blocks):
        piece = slices[k * slots:(k + 1) * slots]
        if k:
            piece = shifted(piece, "blk", blocks - k)
        piece = piece.reshape(experts, CAP, -1)
        returned = jnp.stack(to_partners([piece[r] for r in range(experts)], back=True))
        mixed.append(jnp.einsum(
            "tec,ecd->td", weighting, returned, preferred_element_type=jnp.float32
        ).astype(jnp.bfloat16))
    return jnp.concatenate(by_owner(mixed, mine, 1), axis=1)


def solution(mesh):
    return jax.shard_map(
        on_device,
        mesh=mesh,
        in_specs=(
            P(("expert", "blk"), None),
            P(("expert", "blk"), None),
            P(("expert", "blk"), None),
            P("expert", None, "blk"),
            P("expert", None, "blk"),
            P("expert", None, "blk"),
        ),
        out_specs=P(("expert", "blk"), None),
        check_vma=False,
    )
```

```python
import functools

import jax
import jax.numpy as jnp
from jax import lax
from jax.experimental import pallas as pl
from jax.experimental.pallas import tpu as pltpu
from jax.sharding import PartitionSpec as P

CAP = 4
CORE, ROW = 1, 2
MIB = 1 << 20


def exchanged(block, mask):
    size = lax.axis_size("expert")
    return lax.ppermute(block, "expert", [(i, i ^ mask) for i in range(size)])


def shifted(block, steps):
    size = lax.axis_size("blk")
    return lax.ppermute(block, "blk", [(i, (i + steps) % size) for i in range(size)])


def matmul(left, right):
    return jnp.dot(left, right, preferred_element_type=jnp.float32)


def slots_of(id_rows, labels):
    matches = id_rows[:, :, None] == labels[None, None, :]
    chosen = jnp.any(matches, axis=1)
    counts = chosen.astype(jnp.int32)
    before = jnp.cumsum(counts, axis=0) - counts
    places = jnp.arange(CAP, dtype=jnp.int32)
    return chosen[:, :, None] & (before[:, :, None] == places[None, None, :])


def weights_of(id_rows, gate_rows, labels):
    matches = id_rows[:, :, None] == labels[None, None, :]
    return jnp.sum(jnp.where(matches, gate_rows.astype(jnp.float32)[:, :, None], 0.0), axis=1)


def side_by_side(first, second):
    return jnp.stack([first, second], axis=2).reshape(first.shape[0], -1)


def hidden_kernel(count, *refs):
    pieces, (gate_ref, up_ref, out_ref, gate_sum, up_sum) = refs[:count], refs[count:]
    rows = jnp.concatenate([piece[...].astype(jnp.float32) for piece in pieces], axis=0)
    rows = rows.astype(jnp.bfloat16)
    step = pl.program_id(0)

    @pl.when(step == 0)
    def _():
        gate_sum[...] = jnp.zeros_like(gate_sum)
        up_sum[...] = jnp.zeros_like(up_sum)

    gate_sum[...] += matmul(rows, gate_ref[0])
    up_sum[...] += matmul(rows, up_ref[0])

    @pl.when(step == pl.num_programs(0) - 1)
    def _():
        out_ref[...] = (jax.nn.silu(gate_sum[...]) * up_sum[...]).astype(out_ref.dtype)


def hidden_units(pieces, w_gate, w_up):
    depth, units = w_gate.shape[1:]
    rows = sum(piece.shape[0] for piece in pieces)
    tile = max(t for t in range(128, depth + 1, 128) if depth % t == 0 and t * units <= MIB)
    return pl.pallas_call(
        functools.partial(hidden_kernel, len(pieces)),
        grid=(depth // tile,),
        in_specs=[pl.BlockSpec((piece.shape[0], tile), lambda i: (0, i)) for piece in pieces]
        + [pl.BlockSpec((1, tile, units), lambda i: (0, i, 0))] * 2,
        out_specs=pl.BlockSpec((rows, units), lambda i: (0, 0)),
        out_shape=jax.ShapeDtypeStruct((rows, units), jnp.bfloat16),
        scratch_shapes=[pltpu.VMEM((rows, units), jnp.float32)] * 2,
        compiler_params=pltpu.CompilerParams(vmem_limit_bytes=24 * MIB),
        cost_estimate=pl.CostEstimate(
            flops=4 * rows * depth * units,
            bytes_accessed=2 * (2 * depth * units + rows * (depth + units)),
            transcendentals=rows * units,
        ),
    )(*pieces, w_gate, w_up)


def by_owner(parts, owner_of_first, step):
    size = len(parts)
    if size == 2:
        first = owner_of_first == 0
        return [jnp.where(first, parts[0], parts[1]), jnp.where(first, parts[1], parts[0])]
    stacked = jnp.stack(parts)
    order = (step * (jnp.arange(size) - owner_of_first)) % size
    ordered = jnp.take(stacked, order, axis=0)
    return [ordered[k] for k in range(size)]


def on_device(tokens, expert_ids, gate_weights, w_gate, w_up, w_down):
    experts, blocks = lax.axis_size("expert"), lax.axis_size("blk")
    me, mine = lax.axis_index("expert"), lax.axis_index("blk")
    levels = experts // 4
    unit = 2 * CAP
    half = levels * unit
    down_mat = w_down[0]

    turns = jnp.arange(2 * levels, dtype=jnp.int32)
    turns = (turns // levels) * ROW + (turns % levels) * (2 * ROW)
    near, far = me ^ turns, me ^ CORE ^ turns

    other_ids = exchanged(expert_ids, CORE)
    other_tokens = exchanged(tokens, CORE)
    own_slots, far_slots = slots_of(expert_ids, near), slots_of(expert_ids, far)
    nothing = jnp.zeros_like(own_slots)
    pick = side_by_side(own_slots, nothing).astype(jnp.bfloat16)
    pick_other = side_by_side(nothing, slots_of(other_ids, near)).astype(jnp.bfloat16)
    chosen = (matmul(pick.T, tokens) + matmul(pick_other.T, other_tokens)).astype(jnp.bfloat16)

    groups = [chosen[:half], exchanged(chosen[half:], ROW)]
    outputs = []
    for rows in groups:
        own = [rows[:unit]]
        crossed = [[shifted(own[0], k)] for k in range(1, blocks)]
        for z in range(levels - 1, 0, -1):
            own.insert(1, exchanged(rows[z * unit:(z + 1) * unit], z * 2 * ROW))
        rest = jnp.concatenate(own[1:], axis=0)
        for k in range(1, blocks):
            crossed[k - 1].append(shifted(rest, k))
        hidden = hidden_units([own[0], rest] + sum(crossed, []), w_gate, w_up)

        parts = [hidden]
        for k in range(1, blocks):
            parts.append(jnp.roll(shifted(hidden, k), k * half, axis=0))
        whole = jnp.concatenate(by_owner(parts, mine, -1), axis=1)
        outputs.append(matmul(whole, down_mat).astype(jnp.bfloat16))

    returned = []
    for number, output in enumerate(outputs):
        pieces = [output[:half]]
        for k in range(1, blocks):
            pieces.append(shifted(output[k * half:(k + 1) * half], blocks - k))
        pieces = jnp.stack(pieces)
        if number == 1:
            pieces = exchanged(pieces, ROW)
        back = [pieces[:, :unit]]
        for z in range(levels - 1, 0, -1):
            back.insert(1, exchanged(pieces[:, z * unit:(z + 1) * unit], z * 2 * ROW))
        back = jnp.concatenate(back, axis=1)
        returned.append((back, exchanged(back, CORE)))

    own_weights = jnp.where(own_slots, weights_of(expert_ids, gate_weights, near)[:, :, None], 0.0)
    far_weights = jnp.where(far_slots, weights_of(expert_ids, gate_weights, far)[:, :, None], 0.0)
    zeros = jnp.zeros_like(own_weights)
    weighting = [
        side_by_side(own_weights, zeros).astype(jnp.bfloat16),
        side_by_side(zeros, far_weights).astype(jnp.bfloat16),
    ]
    mixed = []
    for k in range(blocks):
        total = 0.0
        for number, sides in enumerate(returned):
            for side, rows in enumerate(sides):
                total = total + matmul(weighting[side][:, number * half:(number + 1) * half], rows[k])
        mixed.append(total.astype(jnp.bfloat16))
    return jnp.concatenate(by_owner(mixed, mine, 1), axis=1)


def solution(mesh):
    return jax.shard_map(
        on_device,
        mesh=mesh,
        in_specs=(
            P(("expert", "blk"), None),
            P(("expert", "blk"), None),
            P(("expert", "blk"), None),
            P("expert", None, "blk"),
            P("expert", None, "blk"),
            P("expert", None, "blk"),
        ),
        out_specs=P(("expert", "blk"), None),
        check_vma=False,
    )
```

```python
import functools

import jax
import jax.numpy as jnp
from jax import lax
from jax.experimental import pallas as pl
from jax.experimental.pallas import tpu as pltpu
from jax.sharding import PartitionSpec as P

CAP = 4
CORE, ROW = 1, 2
MIB = 1 << 20
PARTS = 4


def exchanged(block, mask):
    size = lax.axis_size("expert")
    return lax.ppermute(block, "expert", [(i, i ^ mask) for i in range(size)])


def shifted(block, steps):
    size = lax.axis_size("blk")
    return lax.ppermute(block, "blk", [(i, (i + steps) % size) for i in range(size)])


def matmul(left, right):
    return jnp.dot(left, right, preferred_element_type=jnp.float32)


def slots_of(id_rows, labels):
    matches = id_rows[:, :, None] == labels[None, None, :]
    chosen = jnp.any(matches, axis=1)
    counts = chosen.astype(jnp.int32)
    before = jnp.cumsum(counts, axis=0) - counts
    places = jnp.arange(CAP, dtype=jnp.int32)
    return chosen[:, :, None] & (before[:, :, None] == places[None, None, :])


def weights_of(id_rows, gate_rows, labels):
    matches = id_rows[:, :, None] == labels[None, None, :]
    return jnp.sum(jnp.where(matches, gate_rows.astype(jnp.float32)[:, :, None], 0.0), axis=1)


def side_by_side(first, second):
    return jnp.stack([first, second], axis=2).reshape(first.shape[0], -1)


def tile_of(size, most):
    return max(t for t in range(128, most + 1, 128) if size % t == 0)


def load_kernel(count, *refs):
    sources, targets, sem = refs[:count], refs[count:-1], refs[-1]
    copies = []
    for source, target in zip(sources, targets):
        step = source.shape[1] // PARTS
        for p in range(PARTS):
            part = (0, pl.ds(p * step, step))
            copies.append(pltpu.make_async_copy(source.at[part], target.at[part], sem.at[len(copies)]))
    for copy in copies:
        copy.start()
    for copy in copies:
        copy.wait()


def loaded(*weights):
    count = len(weights)
    size = sum(w.size * w.dtype.itemsize for w in weights)
    return pl.pallas_call(
        functools.partial(load_kernel, count),
        in_specs=[pl.BlockSpec(memory_space=pltpu.HBM)] * count,
        out_specs=[pl.BlockSpec(memory_space=pltpu.VMEM)] * count,
        out_shape=[pltpu.VMEM(w.shape, w.dtype) for w in weights],
        scratch_shapes=[pltpu.SemaphoreType.DMA((count * PARTS,))],
        compiler_params=pltpu.CompilerParams(vmem_limit_bytes=2 * MIB),
        cost_estimate=pl.CostEstimate(flops=0, bytes_accessed=2 * size, transcendentals=0),
    )(*[pltpu.with_memory_space_constraint(w, pltpu.HBM) for w in weights])


def in_vmem(weight):
    return pltpu.with_memory_space_constraint(weight, pltpu.VMEM)


def hidden_kernel(count, *refs):
    pieces, (gate_ref, up_ref, out_ref, rows_ref) = refs[:count], refs[count:]
    rows = jnp.concatenate([piece[...].astype(jnp.float32) for piece in pieces], axis=0)
    rows_ref[...] = rows.astype(jnp.bfloat16)
    tile = tile_of(out_ref.shape[1], 256)

    @pl.loop(0, out_ref.shape[1] // tile)
    def _(n):
        columns = pl.ds(pl.multiple_of(n * tile, tile), tile)
        gate_part = matmul(rows_ref[...], gate_ref[0, :, columns])
        up_part = matmul(rows_ref[...], up_ref[0, :, columns])
        out_ref[:, columns] = (jax.nn.silu(gate_part) * up_part).astype(out_ref.dtype)


def hidden_units(pieces, w_gate, w_up):
    depth, units = w_gate.shape[1:]
    rows = sum(piece.shape[0] for piece in pieces)
    return pl.pallas_call(
        functools.partial(hidden_kernel, len(pieces)),
        in_specs=[pl.BlockSpec(memory_space=pltpu.VMEM)] * (len(pieces) + 2),
        out_specs=pl.BlockSpec(memory_space=pltpu.VMEM),
        out_shape=jax.ShapeDtypeStruct((rows, units), jnp.bfloat16),
        scratch_shapes=[pltpu.VMEM((rows, depth), jnp.bfloat16)],
        compiler_params=pltpu.CompilerParams(vmem_limit_bytes=10 * rows * depth + 2 * MIB),
        cost_estimate=pl.CostEstimate(
            flops=4 * rows * depth * units,
            bytes_accessed=2 * (2 * depth * units + rows * (depth + units)),
            transcendentals=rows * units,
        ),
    )(*pieces, in_vmem(w_gate), in_vmem(w_up))


def down_kernel(half, *refs):
    place, parts, (weight_ref, out_ref) = refs[0], refs[1:-2], refs[-2:]
    size, units = len(parts), parts[0].shape[1]
    tile = tile_of(out_ref.shape[1], 512)

    @pl.loop(0, out_ref.shape[1] // tile)
    def _(n):
        columns = pl.ds(pl.multiple_of(n * tile, tile), tile)
        total = jnp.zeros((out_ref.shape[0], tile), jnp.float32)
        for k, part in enumerate(parts):
            owner = lax.rem(place[0] + (size - k), size)
            rows = pl.ds(pl.multiple_of(owner * units, units), units)
            left = part[...]
            if k:
                left = jnp.concatenate([left[-k * half:], left[:-k * half]], axis=0)
            total += matmul(left, weight_ref[0, rows, columns])
        out_ref[:, columns] = total.astype(out_ref.dtype)


def down_slices(parts, half, place, w_down):
    units, width = w_down.shape[1:]
    rows = parts[0].shape[0]
    return pl.pallas_call(
        functools.partial(down_kernel, half),
        in_specs=[pl.BlockSpec(memory_space=pltpu.SMEM)]
        + [pl.BlockSpec(memory_space=pltpu.VMEM)] * (len(parts) + 1),
        out_specs=pl.BlockSpec(memory_space=pltpu.VMEM),
        out_shape=jax.ShapeDtypeStruct((rows, width), jnp.bfloat16),
        compiler_params=pltpu.CompilerParams(vmem_limit_bytes=8 * rows * (units + width) + 2 * MIB),
        cost_estimate=pl.CostEstimate(
            flops=2 * rows * units * width,
            bytes_accessed=2 * (units * width + rows * (units + width)),
            transcendentals=0,
        ),
    )(place, *parts, in_vmem(w_down))


def mix_kernel(blocks, *refs):
    place, weights, pieces, out_ref = refs[0], refs[1], refs[2:-1], refs[-1]
    width = out_ref.shape[1] // blocks
    tile = tile_of(width, 512)
    for k in range(blocks):
        start = lax.rem(place[0] + k, blocks) * width
        for n in range(0, width, tile):
            rows = jnp.concatenate([piece[k, :, n:n + tile] for piece in pieces], axis=0)
            columns = pl.ds(pl.multiple_of(start + n, 128), tile)
            out_ref[:, columns] = matmul(weights[...], rows).astype(out_ref.dtype)


def mixed_rows(weights, pieces, place):
    blocks, half, width = pieces[0].shape
    tokens = weights.shape[0]
    return pl.pallas_call(
        functools.partial(mix_kernel, blocks),
        in_specs=[pl.BlockSpec(memory_space=pltpu.SMEM)]
        + [pl.BlockSpec(memory_space=pltpu.VMEM)] * (len(pieces) + 1),
        out_specs=pl.BlockSpec(memory_space=pltpu.VMEM),
        out_shape=jax.ShapeDtypeStruct((tokens, blocks * width), jnp.bfloat16),
        compiler_params=pltpu.CompilerParams(
            vmem_limit_bytes=4 * blocks * width * (len(pieces) * half + tokens) + 2 * MIB
        ),
    )(place, weights, *pieces)


def on_device(tokens, expert_ids, gate_weights, w_gate, w_up, w_down):
    experts, blocks = lax.axis_size("expert"), lax.axis_size("blk")
    me, mine = lax.axis_index("expert"), lax.axis_index("blk")
    levels = experts // 4
    unit = 2 * CAP
    half = levels * unit
    down_mat = w_down[0]

    turns = jnp.arange(2 * levels, dtype=jnp.int32)
    turns = (turns // levels) * ROW + (turns % levels) * (2 * ROW)
    near, far = me ^ turns, me ^ CORE ^ turns

    other_ids = exchanged(expert_ids, CORE)
    other_tokens = exchanged(tokens, CORE)
    own_slots, far_slots = slots_of(expert_ids, near), slots_of(expert_ids, far)
    nothing = jnp.zeros_like(own_slots)
    pick = side_by_side(own_slots, nothing).astype(jnp.bfloat16)
    pick_other = side_by_side(nothing, slots_of(other_ids, near)).astype(jnp.bfloat16)
    chosen = (matmul(pick.T, tokens) + matmul(pick_other.T, other_tokens)).astype(jnp.bfloat16)

    place = mine.reshape(1).astype(jnp.int32)
    w_gate, w_up, w_down, chosen = lax.optimization_barrier((w_gate, w_up, w_down, chosen))

    def over_z(rows):
        pieces = [rows[:unit]]
        for z in range(levels - 1, 0, -1):
            pieces.insert(1, exchanged(rows[z * unit:(z + 1) * unit], z * 2 * ROW))
        return pieces

    def over_blk(piece):
        return [shifted(piece, k) for k in range(1, blocks)]

    stay = over_z(chosen[:half])
    first_stay = over_blk(stay[0])
    leave = exchanged(chosen[half:], ROW)
    w_gate, w_up = loaded(w_gate, w_up)
    rest = jnp.concatenate(stay[1:], axis=0)
    rest, leave, w_gate, w_up, w_down = lax.optimization_barrier((rest, leave, w_gate, w_up, w_down))
    rest_stay = over_blk(rest)
    leave = over_z(leave)
    first_leave = over_blk(leave[0])
    w_down, = loaded(w_down)
    stay = [stay[0], rest] + sum([[a, b] for a, b in zip(first_stay, rest_stay)], [])
    leave, stay, w_down = lax.optimization_barrier((leave, stay, w_down))
    rest = jnp.concatenate(leave[1:], axis=0)
    rest_leave = over_blk(rest)
    leave = [leave[0], rest] + sum([[a, b] for a, b in zip(first_leave, rest_leave)], [])

    outputs = []
    for pieces in (stay, leave):
        hidden = hidden_units(pieces, w_gate, w_up)
        outputs.append(down_slices([hidden] + over_blk(hidden), half, place, w_down))

    def slices(output):
        return [output[:half]] + [
            shifted(output[k * half:(k + 1) * half], blocks - k) for k in range(1, blocks)
        ]

    stay = jnp.stack([jnp.concatenate(over_z(part), axis=0) for part in slices(outputs[0])])
    leave = exchanged(jnp.stack(slices(outputs[1])), ROW)
    back = [leave[:, :unit]]
    for z in range(levels - 1, 0, -1):
        back.insert(1, exchanged(leave[:, z * unit:(z + 1) * unit], z * 2 * ROW))
    leave = jnp.concatenate(back, axis=1)
    returned = [stay, exchanged(stay, CORE), leave, exchanged(leave, CORE)]

    own_weights = jnp.where(own_slots, weights_of(expert_ids, gate_weights, near)[:, :, None], 0.0)
    far_weights = jnp.where(far_slots, weights_of(expert_ids, gate_weights, far)[:, :, None], 0.0)
    zeros = jnp.zeros_like(own_weights)
    own_weights, far_weights = side_by_side(own_weights, zeros), side_by_side(zeros, far_weights)
    weighting = jnp.concatenate(
        [own_weights[:, :half], far_weights[:, :half], own_weights[:, half:], far_weights[:, half:]], axis=1
    )
    return mixed_rows(weighting.astype(jnp.bfloat16), returned, place)


def solution(mesh):
    return jax.shard_map(
        on_device,
        mesh=mesh,
        in_specs=(
            P(("expert", "blk"), None),
            P(("expert", "blk"), None),
            P(("expert", "blk"), None),
            P("expert", None, "blk"),
            P("expert", None, "blk"),
            P("expert", None, "blk"),
        ),
        out_specs=P(("expert", "blk"), None),
        check_vma=False,
    )
```

```python
import functools

import jax
import jax.numpy as jnp
from jax import lax
from jax.experimental import pallas as pl
from jax.experimental.pallas import tpu as pltpu
from jax.sharding import PartitionSpec as P

CAP = 4
CORE, ROW = 1, 2
MIB = 1 << 20
PARTS = 4


def exchanged(block, mask, name):
    size = lax.axis_size("expert")
    with jax.named_scope(f"{name}_{mask}"):
        return lax.ppermute(block, "expert", [(i, i ^ mask) for i in range(size)])


def shifted(block, steps, name):
    size = lax.axis_size("blk")
    with jax.named_scope(f"{name}_{steps}"):
        return lax.ppermute(block, "blk", [(i, (i + steps) % size) for i in range(size)])


def matmul(left, right):
    return jnp.dot(left, right, preferred_element_type=jnp.float32)


def slots_of(id_rows, labels):
    matches = id_rows[:, :, None] == labels[None, None, :]
    chosen = jnp.any(matches, axis=1)
    counts = chosen.astype(jnp.int32)
    before = jnp.cumsum(counts, axis=0) - counts
    places = jnp.arange(CAP, dtype=jnp.int32)
    return chosen[:, :, None] & (before[:, :, None] == places[None, None, :])


def weights_of(id_rows, gate_rows, labels):
    matches = id_rows[:, :, None] == labels[None, None, :]
    return jnp.sum(jnp.where(matches, gate_rows.astype(jnp.float32)[:, :, None], 0.0), axis=1)


def side_by_side(first, second):
    return jnp.stack([first, second], axis=2).reshape(first.shape[0], -1)


def tile_of(size, most):
    return max(t for t in range(128, most + 1, 128) if size % t == 0)


def load_kernel(source, target, sem):
    step = source.shape[1] // PARTS
    parts = [(0, pl.ds(p * step, step)) for p in range(PARTS)]
    copies = [pltpu.make_async_copy(source.at[part], target.at[part], sem.at[p]) for p, part in enumerate(parts)]
    for copy in copies:
        copy.start()
    for copy in copies:
        copy.wait()


def loaded(weight):
    return pl.pallas_call(
        load_kernel,
        in_specs=[pl.BlockSpec(memory_space=pltpu.HBM)],
        out_specs=pl.BlockSpec(memory_space=pltpu.VMEM),
        out_shape=pltpu.VMEM(weight.shape, weight.dtype),
        scratch_shapes=[pltpu.SemaphoreType.DMA((PARTS,))],
        compiler_params=pltpu.CompilerParams(vmem_limit_bytes=2 * MIB),
        cost_estimate=pl.CostEstimate(
            flops=0, bytes_accessed=weight.size * weight.dtype.itemsize, transcendentals=0
        ),
    )(pltpu.with_memory_space_constraint(weight, pltpu.HBM))


def in_vmem(weight):
    return pltpu.with_memory_space_constraint(weight, pltpu.VMEM)


def hidden_kernel(count, *refs):
    pieces, (gate_ref, up_ref, out_ref, rows_ref) = refs[:count], refs[count:]
    rows = jnp.concatenate([piece[...].astype(jnp.float32) for piece in pieces], axis=0)
    rows_ref[...] = rows.astype(jnp.bfloat16)
    tile = tile_of(out_ref.shape[1], 256)

    @pl.loop(0, out_ref.shape[1] // tile)
    def _(n):
        columns = pl.ds(pl.multiple_of(n * tile, tile), tile)
        gate_part = matmul(rows_ref[...], gate_ref[0, :, columns])
        up_part = matmul(rows_ref[...], up_ref[0, :, columns])
        out_ref[:, columns] = (jax.nn.silu(gate_part) * up_part).astype(out_ref.dtype)


def hidden_units(pieces, w_gate, w_up):
    depth, units = w_gate.shape[1:]
    rows = sum(piece.shape[0] for piece in pieces)
    return pl.pallas_call(
        functools.partial(hidden_kernel, len(pieces)),
        in_specs=[pl.BlockSpec(memory_space=pltpu.VMEM)] * (len(pieces) + 2),
        out_specs=pl.BlockSpec(memory_space=pltpu.VMEM),
        out_shape=jax.ShapeDtypeStruct((rows, units), jnp.bfloat16),
        scratch_shapes=[pltpu.VMEM((rows, depth), jnp.bfloat16)],
        compiler_params=pltpu.CompilerParams(vmem_limit_bytes=10 * rows * depth + 2 * MIB),
        cost_estimate=pl.CostEstimate(
            flops=4 * rows * depth * units,
            bytes_accessed=2 * rows * (depth + units),
            transcendentals=rows * units,
        ),
    )(*pieces, in_vmem(w_gate), in_vmem(w_up))


def down_kernel(half, *refs):
    place, parts, (weight_ref, out_ref) = refs[0], refs[1:-2], refs[-2:]
    size, units = len(parts), parts[0].shape[1]
    total = jnp.zeros(out_ref.shape, jnp.float32)
    for k, part in enumerate(parts):
        owner = lax.rem(place[0] + (size - k), size)
        rows = pl.ds(pl.multiple_of(owner * units, units), units)
        left = part[...]
        if k:
            left = jnp.concatenate([left[-k * half:], left[:-k * half]], axis=0)
        total += matmul(left, weight_ref[0, rows, :])
    out_ref[...] = total.astype(out_ref.dtype)


def down_slices(parts, half, place, w_down):
    units, width = w_down.shape[1:]
    rows = parts[0].shape[0]
    tile = tile_of(width, 512)
    return pl.pallas_call(
        functools.partial(down_kernel, half),
        grid=(width // tile,),
        in_specs=[pl.BlockSpec(memory_space=pltpu.SMEM)]
        + [pl.BlockSpec(part.shape, lambda i: (0, 0)) for part in parts]
        + [pl.BlockSpec((1, units, tile), lambda i: (0, 0, i))],
        out_specs=pl.BlockSpec((rows, tile), lambda i: (0, i)),
        out_shape=jax.ShapeDtypeStruct((rows, width), jnp.bfloat16),
        compiler_params=pltpu.CompilerParams(vmem_limit_bytes=8 * (rows + tile) * units + 4 * MIB),
        cost_estimate=pl.CostEstimate(
            flops=2 * rows * units * width,
            bytes_accessed=2 * (units * width + rows * (units + width)),
            transcendentals=0,
        ),
    )(place, *parts, pltpu.with_memory_space_constraint(w_down, pltpu.HBM))


def mix_kernel(blocks, *refs):
    place, weights, pieces, out_ref = refs[0], refs[1], refs[2:-1], refs[-1]
    width = out_ref.shape[1] // blocks
    tile = tile_of(width, 512)
    for k in range(blocks):
        start = lax.rem(place[0] + k, blocks) * width
        for n in range(0, width, tile):
            rows = jnp.concatenate([piece[k, :, n:n + tile] for piece in pieces], axis=0)
            columns = pl.ds(pl.multiple_of(start + n, 128), tile)
            out_ref[:, columns] = matmul(weights[...], rows).astype(out_ref.dtype)


def mixed_rows(weights, pieces, place):
    blocks, half, width = pieces[0].shape
    tokens = weights.shape[0]
    return pl.pallas_call(
        functools.partial(mix_kernel, blocks),
        in_specs=[pl.BlockSpec(memory_space=pltpu.SMEM)]
        + [pl.BlockSpec(memory_space=pltpu.VMEM)] * (len(pieces) + 1),
        out_specs=pl.BlockSpec(memory_space=pltpu.VMEM),
        out_shape=jax.ShapeDtypeStruct((tokens, blocks * width), jnp.bfloat16),
        compiler_params=pltpu.CompilerParams(
            vmem_limit_bytes=4 * blocks * width * (len(pieces) * half + tokens) + 2 * MIB
        ),
    )(place, weights, *pieces)


def on_device(tokens, expert_ids, gate_weights, w_gate, w_up, w_down):
    experts, blocks = lax.axis_size("expert"), lax.axis_size("blk")
    me, mine = lax.axis_index("expert"), lax.axis_index("blk")
    levels = experts // 4
    unit = 2 * CAP
    half = levels * unit
    down_mat = w_down[0]

    turns = jnp.arange(2 * levels, dtype=jnp.int32)
    turns = (turns // levels) * ROW + (turns % levels) * (2 * ROW)
    near, far = me ^ turns, me ^ CORE ^ turns

    other_ids = exchanged(expert_ids, CORE, "ids")
    other_tokens = exchanged(tokens, CORE, "tokens")
    own_slots, far_slots = slots_of(expert_ids, near), slots_of(expert_ids, far)
    nothing = jnp.zeros_like(own_slots)
    pick = side_by_side(own_slots, nothing).astype(jnp.bfloat16)
    pick_other = side_by_side(nothing, slots_of(other_ids, near)).astype(jnp.bfloat16)
    chosen = (matmul(pick.T, tokens) + matmul(pick_other.T, other_tokens)).astype(jnp.bfloat16)

    place = mine.reshape(1).astype(jnp.int32)
    w_gate, chosen = lax.optimization_barrier((w_gate, chosen))

    def split(rows):
        return [rows[..., z * unit:(z + 1) * unit, :] for z in range(levels)]

    def routed(pieces, turn, name):
        masks = [z * 2 * ROW + turn for z in range(levels)]
        received = list(pieces)
        for z in sorted(range(levels), reverse=True):
            if masks[z]:
                received[z] = exchanged(pieces[z], masks[z], name)
        return received

    def over_blk(piece, name):
        return [shifted(piece, k, name) for k in range(1, blocks)]

    stay, leave = routed(split(chosen[:half]), 0, "go_stay"), split(chosen[half:])
    first_stay = over_blk(stay[0], "first_stay")
    w_gate = loaded(w_gate)
    leave[1:], w_gate = lax.optimization_barrier((leave[1:], w_gate))
    leave = routed(leave, ROW, "go_leave")
    rest, first, w_gate, w_up = lax.optimization_barrier(
        (jnp.concatenate(stay[1:], axis=0), leave[0], w_gate, w_up)
    )
    middle = over_blk(jnp.concatenate([rest, first], axis=0), "middle")
    rest_stay, first_leave = [m[:-unit] for m in middle], [m[-unit:] for m in middle]
    w_up = loaded(w_up)
    stay = [stay[0], rest] + sum([[a, b] for a, b in zip(first_stay, rest_stay)], [])
    rest, first_leave, stay, w_up = lax.optimization_barrier(
        (jnp.concatenate(leave[1:], axis=0), first_leave, stay, w_up)
    )
    rest_leave = over_blk(rest, "rest_leave")
    leave = [first, rest] + sum([[a, b] for a, b in zip(first_leave, rest_leave)], [])

    hidden = hidden_units(stay, w_gate, w_up)
    stay = [hidden] + over_blk(hidden, "hidden_stay")
    hidden = hidden_units(leave, w_gate, w_up)
    stay, hidden = lax.optimization_barrier((stay, hidden))
    leave = [hidden] + over_blk(hidden, "hidden_leave")
    outputs = [down_slices(parts, half, place, w_down) for parts in (stay, leave)]

    def slices(output):
        return [output[:half]] + [
            shifted(output[k * half:(k + 1) * half], blocks - k, "slices") for k in range(1, blocks)
        ]

    stay = jnp.stack([jnp.concatenate(routed(split(part), 0, "back_stay"), axis=0) for part in slices(outputs[0])])
    leave = jnp.concatenate(routed(split(jnp.stack(slices(outputs[1]))), ROW, "back_leave"), axis=1)
    returned = [stay, exchanged(stay, CORE, "pair_stay"), leave, exchanged(leave, CORE, "pair_leave")]

    own_weights = jnp.where(own_slots, weights_of(expert_ids, gate_weights, near)[:, :, None], 0.0)
    far_weights = jnp.where(far_slots, weights_of(expert_ids, gate_weights, far)[:, :, None], 0.0)
    zeros = jnp.zeros_like(own_weights)
    own_weights, far_weights = side_by_side(own_weights, zeros), side_by_side(zeros, far_weights)
    weighting = jnp.concatenate(
        [own_weights[:, :half], far_weights[:, :half], own_weights[:, half:], far_weights[:, half:]], axis=1
    )
    return mixed_rows(weighting.astype(jnp.bfloat16), returned, place)


def solution(mesh):
    return jax.shard_map(
        on_device,
        mesh=mesh,
        in_specs=(
            P(("expert", "blk"), None),
            P(("expert", "blk"), None),
            P(("expert", "blk"), None),
            P("expert", None, "blk"),
            P("expert", None, "blk"),
            P("expert", None, "blk"),
        ),
        out_specs=P(("expert", "blk"), None),
        check_vma=False,
    )
```

```python
import functools

import jax
import jax.numpy as jnp
from jax import lax
from jax.experimental import pallas as pl
from jax.experimental.pallas import tpu as pltpu
from jax.sharding import PartitionSpec as P

CAP = 4
CORE, ROW = 1, 2
MIB = 1 << 20
PARTS = 4


def exchanged(block, mask, name):
    size = lax.axis_size("expert")
    with jax.named_scope(f"{name}_{mask}"):
        return lax.ppermute(block, "expert", [(i, i ^ mask) for i in range(size)])


def shifted(block, steps, name):
    size = lax.axis_size("blk")
    with jax.named_scope(f"{name}_{steps}"):
        return lax.ppermute(block, "blk", [(i, (i + steps) % size) for i in range(size)])


def matmul(left, right):
    return jnp.dot(left, right, preferred_element_type=jnp.float32)


def slots_of(id_rows, labels):
    matches = id_rows[:, :, None] == labels[None, None, :]
    chosen = jnp.any(matches, axis=1)
    counts = chosen.astype(jnp.int32)
    before = jnp.cumsum(counts, axis=0) - counts
    places = jnp.arange(CAP, dtype=jnp.int32)
    return chosen[:, :, None] & (before[:, :, None] == places[None, None, :])


def weights_of(id_rows, gate_rows, labels):
    matches = id_rows[:, :, None] == labels[None, None, :]
    return jnp.sum(jnp.where(matches, gate_rows.astype(jnp.float32)[:, :, None], 0.0), axis=1)


def side_by_side(first, second):
    return jnp.stack([first, second], axis=2).reshape(first.shape[0], -1)


def tile_of(size, most):
    return max(t for t in range(128, most + 1, 128) if size % t == 0)


def load_kernel(count, *refs):
    sources, targets, sem = refs[:count], refs[count:-1], refs[-1]
    copies = []
    for source, target in zip(sources, targets):
        step = source.shape[1] // PARTS
        for p in range(PARTS):
            part = (0, pl.ds(p * step, step))
            copies.append(pltpu.make_async_copy(source.at[part], target.at[part], sem.at[len(copies)]))
    for copy in copies:
        copy.start()
    for copy in copies:
        copy.wait()


def loaded(*weights):
    count = len(weights)
    return pl.pallas_call(
        functools.partial(load_kernel, count),
        in_specs=[pl.BlockSpec(memory_space=pltpu.HBM)] * count,
        out_specs=[pl.BlockSpec(memory_space=pltpu.VMEM)] * count,
        out_shape=[pltpu.VMEM(weight.shape, weight.dtype) for weight in weights],
        scratch_shapes=[pltpu.SemaphoreType.DMA((count * PARTS,))],
        compiler_params=pltpu.CompilerParams(vmem_limit_bytes=2 * MIB),
        cost_estimate=pl.CostEstimate(
            flops=0, bytes_accessed=sum(w.size * w.dtype.itemsize for w in weights), transcendentals=0
        ),
    )(*[pltpu.with_memory_space_constraint(weight, pltpu.HBM) for weight in weights])


def in_vmem(weight):
    return pltpu.with_memory_space_constraint(weight, pltpu.VMEM)


def hidden_kernel(count, *refs):
    pieces, (gate_ref, up_ref, out_ref, rows_ref) = refs[:count], refs[count:]
    rows = jnp.concatenate([piece[...].astype(jnp.float32) for piece in pieces], axis=0)
    rows_ref[...] = rows.astype(jnp.bfloat16)
    tile = tile_of(out_ref.shape[1], 256)

    @pl.loop(0, out_ref.shape[1] // tile)
    def _(n):
        columns = pl.ds(pl.multiple_of(n * tile, tile), tile)
        gate_part = matmul(rows_ref[...], gate_ref[0, :, columns])
        up_part = matmul(rows_ref[...], up_ref[0, :, columns])
        out_ref[:, columns] = (jax.nn.silu(gate_part) * up_part).astype(out_ref.dtype)


def hidden_units(pieces, w_gate, w_up):
    depth, units = w_gate.shape[1:]
    rows = sum(piece.shape[0] for piece in pieces)
    return pl.pallas_call(
        functools.partial(hidden_kernel, len(pieces)),
        in_specs=[pl.BlockSpec(memory_space=pltpu.VMEM)] * (len(pieces) + 2),
        out_specs=pl.BlockSpec(memory_space=pltpu.VMEM),
        out_shape=jax.ShapeDtypeStruct((rows, units), jnp.bfloat16),
        scratch_shapes=[pltpu.VMEM((rows, depth), jnp.bfloat16)],
        compiler_params=pltpu.CompilerParams(vmem_limit_bytes=10 * rows * depth + 2 * MIB),
        cost_estimate=pl.CostEstimate(
            flops=4 * rows * depth * units,
            bytes_accessed=2 * rows * (depth + units),
            transcendentals=rows * units,
        ),
    )(*pieces, in_vmem(w_gate), in_vmem(w_up))


def down_kernel(half, *refs):
    place, parts, (weight_ref, out_ref) = refs[0], refs[1:-2], refs[-2:]
    size, units = len(parts), parts[0].shape[1]
    tile = tile_of(out_ref.shape[1], 512)

    @pl.loop(0, out_ref.shape[1] // tile)
    def _(n):
        columns = pl.ds(pl.multiple_of(n * tile, tile), tile)
        total = jnp.zeros((out_ref.shape[0], tile), jnp.float32)
        for k, part in enumerate(parts):
            owner = lax.rem(place[0] + (size - k), size)
            rows = pl.ds(pl.multiple_of(owner * units, units), units)
            left = part[...]
            if k:
                left = jnp.concatenate([left[-k * half:], left[:-k * half]], axis=0)
            total += matmul(left, weight_ref[0, rows, columns])
        out_ref[:, columns] = total.astype(out_ref.dtype)


def down_slices(parts, half, place, w_down):
    units, width = w_down.shape[1:]
    rows = parts[0].shape[0]
    return pl.pallas_call(
        functools.partial(down_kernel, half),
        in_specs=[pl.BlockSpec(memory_space=pltpu.SMEM)]
        + [pl.BlockSpec(memory_space=pltpu.VMEM)] * (len(parts) + 1),
        out_specs=pl.BlockSpec(memory_space=pltpu.VMEM),
        out_shape=jax.ShapeDtypeStruct((rows, width), jnp.bfloat16),
        compiler_params=pltpu.CompilerParams(vmem_limit_bytes=8 * rows * (units + width) + 2 * MIB),
        cost_estimate=pl.CostEstimate(
            flops=2 * rows * units * width,
            bytes_accessed=2 * rows * (units + width),
            transcendentals=0,
        ),
    )(place, *parts, in_vmem(w_down))


def mix_kernel(blocks, *refs):
    place, weights, pieces, out_ref = refs[0], refs[1], refs[2:-1], refs[-1]
    width = out_ref.shape[1] // blocks
    tile = tile_of(width, 512)
    for k in range(blocks):
        start = lax.rem(place[0] + k, blocks) * width
        for n in range(0, width, tile):
            rows = jnp.concatenate([piece[k, :, n:n + tile] for piece in pieces], axis=0)
            columns = pl.ds(pl.multiple_of(start + n, 128), tile)
            out_ref[:, columns] = matmul(weights[...], rows).astype(out_ref.dtype)


def mixed_rows(weights, pieces, place):
    blocks, half, width = pieces[0].shape
    tokens = weights.shape[0]
    return pl.pallas_call(
        functools.partial(mix_kernel, blocks),
        in_specs=[pl.BlockSpec(memory_space=pltpu.SMEM)]
        + [pl.BlockSpec(memory_space=pltpu.VMEM)] * (len(pieces) + 1),
        out_specs=pl.BlockSpec(memory_space=pltpu.VMEM),
        out_shape=jax.ShapeDtypeStruct((tokens, blocks * width), jnp.bfloat16),
        compiler_params=pltpu.CompilerParams(
            vmem_limit_bytes=4 * blocks * width * (len(pieces) * half + tokens) + 2 * MIB
        ),
    )(place, weights, *pieces)


def on_device(tokens, expert_ids, gate_weights, w_gate, w_up, w_down):
    experts, blocks = lax.axis_size("expert"), lax.axis_size("blk")
    me, mine = lax.axis_index("expert"), lax.axis_index("blk")
    levels = experts // 4
    unit = 2 * CAP
    half = levels * unit
    down_mat = w_down[0]

    turns = jnp.arange(2 * levels, dtype=jnp.int32)
    turns = (turns // levels) * ROW + (turns % levels) * (2 * ROW)
    near, far = me ^ turns, me ^ CORE ^ turns

    other_ids = exchanged(expert_ids, CORE, "ids")
    other_tokens = exchanged(tokens, CORE, "tokens")
    own_slots, far_slots = slots_of(expert_ids, near), slots_of(expert_ids, far)
    nothing = jnp.zeros_like(own_slots)
    pick = side_by_side(own_slots, nothing).astype(jnp.bfloat16)
    pick_other = side_by_side(nothing, slots_of(other_ids, near)).astype(jnp.bfloat16)
    chosen = (matmul(pick.T, tokens) + matmul(pick_other.T, other_tokens)).astype(jnp.bfloat16)

    own_weights = jnp.where(own_slots, weights_of(expert_ids, gate_weights, near)[:, :, None], 0.0)
    far_weights = jnp.where(far_slots, weights_of(expert_ids, gate_weights, far)[:, :, None], 0.0)
    zeros = jnp.zeros_like(own_weights)
    own_weights, far_weights = side_by_side(own_weights, zeros), side_by_side(zeros, far_weights)
    weighting = jnp.concatenate(
        [own_weights[:, :half], far_weights[:, :half], own_weights[:, half:], far_weights[:, half:]], axis=1
    )
    weighting = weighting.astype(jnp.bfloat16)
    place = mine.reshape(1).astype(jnp.int32)
    w_gate, weighting, place, _ = lax.optimization_barrier((w_gate, weighting, place, chosen))

    def split(rows):
        return [rows[..., z * unit:(z + 1) * unit, :] for z in range(levels)]

    def routed(pieces, turn, name):
        masks = [z * 2 * ROW + turn for z in range(levels)]
        received = list(pieces)
        for z in sorted(range(levels), reverse=True):
            if masks[z]:
                received[z] = exchanged(pieces[z], masks[z], name)
        return received

    def over_blk(piece, name):
        return [shifted(piece, k, name) for k in range(1, blocks)]

    stay, leave = routed(split(chosen[:half]), 0, "go_stay"), split(chosen[half:])
    first_stay = over_blk(stay[0], "first_stay")
    w_gate, = loaded(w_gate)
    leave[1:], w_gate = lax.optimization_barrier((leave[1:], w_gate))
    leave = routed(leave, ROW, "go_leave")
    rest, first, w_gate, w_up, w_down = lax.optimization_barrier(
        (jnp.concatenate(stay[1:], axis=0), leave[0], w_gate, w_up, w_down)
    )
    middle = over_blk(jnp.concatenate([rest, first], axis=0), "middle")
    rest_stay, first_leave = [m[:-unit] for m in middle], [m[-unit:] for m in middle]
    w_up, w_down = loaded(w_up, w_down)
    stay = [stay[0], rest] + sum([[a, b] for a, b in zip(first_stay, rest_stay)], [])
    rest, first_leave, stay, w_up, w_down = lax.optimization_barrier(
        (jnp.concatenate(leave[1:], axis=0), first_leave, stay, w_up, w_down)
    )
    rest_leave = over_blk(rest, "rest_leave")
    leave = [first, rest] + sum([[a, b] for a, b in zip(first_leave, rest_leave)], [])

    hidden = hidden_units(stay, w_gate, w_up)
    stay = [hidden] + over_blk(hidden, "hidden_stay")
    hidden = hidden_units(leave, w_gate, w_up)
    stay, hidden = lax.optimization_barrier((stay, hidden))
    leave = [hidden] + over_blk(hidden, "hidden_leave")
    stay, leave = lax.optimization_barrier((down_slices(stay, half, place, w_down), leave))
    outputs = [stay, down_slices(leave, half, place, w_down)]

    def slices(output):
        return [output[:half]] + [
            shifted(output[k * half:(k + 1) * half], blocks - k, "slices") for k in range(1, blocks)
        ]

    stay = jnp.stack([jnp.concatenate(routed(split(part), 0, "back_stay"), axis=0) for part in slices(outputs[0])])
    leave = jnp.concatenate(routed(split(jnp.stack(slices(outputs[1]))), ROW, "back_leave"), axis=1)
    returned = [stay, exchanged(stay, CORE, "pair_stay"), leave, exchanged(leave, CORE, "pair_leave")]

    return mixed_rows(weighting, returned, place)


def solution(mesh):
    return jax.shard_map(
        on_device,
        mesh=mesh,
        in_specs=(
            P(("expert", "blk"), None),
            P(("expert", "blk"), None),
            P(("expert", "blk"), None),
            P("expert", None, "blk"),
            P("expert", None, "blk"),
            P("expert", None, "blk"),
        ),
        out_specs=P(("expert", "blk"), None),
        check_vma=False,
    )
```

```python
import functools

import jax
import jax.numpy as jnp
from jax import lax
from jax.experimental import pallas as pl
from jax.experimental.pallas import tpu as pltpu
from jax.sharding import PartitionSpec as P

CAP = 4
CORE, ROW = 1, 2
MIB = 1 << 20
PARTS = 4


def exchanged(block, mask, name):
    size = lax.axis_size("expert")
    with jax.named_scope(f"{name}_{mask}"):
        return lax.ppermute(block, "expert", [(i, i ^ mask) for i in range(size)])


def shifted(block, steps, name):
    size = lax.axis_size("blk")
    with jax.named_scope(f"{name}_{steps}"):
        return lax.ppermute(block, "blk", [(i, (i + steps) % size) for i in range(size)])


def crossed(block, mask, steps, name):
    size, wide = lax.axis_size("expert"), lax.axis_size("blk")
    pairs = [(e * wide + b, (e ^ mask) * wide + (b - steps) % wide) for e in range(size) for b in range(wide)]
    with jax.named_scope(f"{name}_{mask}_{steps}"):
        return lax.ppermute(block, ("expert", "blk"), pairs)


def matmul(left, right):
    return jnp.dot(left, right, preferred_element_type=jnp.float32)


def slots_of(id_rows, labels):
    matches = id_rows[:, :, None] == labels[None, None, :]
    chosen = jnp.any(matches, axis=1)
    counts = chosen.astype(jnp.int32)
    before = jnp.cumsum(counts, axis=0) - counts
    places = jnp.arange(CAP, dtype=jnp.int32)
    return chosen[:, :, None] & (before[:, :, None] == places[None, None, :])


def weights_of(id_rows, gate_rows, labels):
    matches = id_rows[:, :, None] == labels[None, None, :]
    return jnp.sum(jnp.where(matches, gate_rows.astype(jnp.float32)[:, :, None], 0.0), axis=1)


def side_by_side(first, second):
    return jnp.stack([first, second], axis=2).reshape(first.shape[0], -1)


def tile_of(size, most):
    return max(t for t in range(128, most + 1, 128) if size % t == 0)


def parts_of(size, unit):
    return max(p for p in range(1, PARTS + 1) if size % (p * unit) == 0)


def copies_of(source, target, sem, dim):
    count = parts_of(source.shape[dim], 128)
    step = source.shape[dim] // count
    copies = []
    for p in range(count):
        part = (0, pl.ds(p * step, step)) if dim == 1 else (0, slice(None), pl.ds(p * step, step))
        copies.append(pltpu.make_async_copy(source.at[part], target.at[part], sem.at[p]))
    return copies


def load_kernel(source, target, sem):
    copies = copies_of(source, target, sem, 1)
    for copy in copies:
        copy.start()
    for copy in copies:
        copy.wait()


def loaded(weight):
    return pl.pallas_call(
        load_kernel,
        in_specs=[pl.BlockSpec(memory_space=pltpu.HBM)],
        out_specs=pl.BlockSpec(memory_space=pltpu.VMEM),
        out_shape=pltpu.VMEM(weight.shape, weight.dtype),
        scratch_shapes=[pltpu.SemaphoreType.DMA((PARTS,))],
        compiler_params=pltpu.CompilerParams(vmem_limit_bytes=2 * MIB),
        cost_estimate=pl.CostEstimate(
            flops=0, bytes_accessed=weight.size * weight.dtype.itemsize, transcendentals=0
        ),
    )(pltpu.with_memory_space_constraint(weight, pltpu.HBM))


def in_vmem(weight):
    return pltpu.with_memory_space_constraint(weight, pltpu.VMEM)


def gathered(pieces, rows_ref):
    rows = jnp.concatenate([piece[...].astype(jnp.float32) for piece in pieces], axis=0)
    rows_ref[...] = rows.astype(jnp.bfloat16)


def first_hidden_kernel(count, *refs):
    pieces, (gate_ref, up_hbm, out_ref, up_ref, rows_ref, gate_part, sem) = refs[:count], refs[count:]
    copies = copies_of(up_hbm, up_ref, sem, 2)
    for copy in copies:
        copy.start()
    gathered(pieces, rows_ref)
    tile = out_ref.shape[1] // len(copies)
    parts = [slice(p * tile, (p + 1) * tile) for p in range(len(copies))]
    for columns in parts:
        gate_part[:, columns] = jax.nn.silu(matmul(rows_ref[...], gate_ref[0, :, columns]))
    for columns, copy in zip(parts, copies):
        copy.wait()
        up_part = matmul(rows_ref[...], up_ref[0, :, columns])
        out_ref[:, columns] = (gate_part[:, columns] * up_part).astype(out_ref.dtype)


def hidden_kernel(count, *refs):
    pieces, (gate_ref, up_ref, out_ref, rows_ref) = refs[:count], refs[count:]
    gathered(pieces, rows_ref)
    tile = tile_of(out_ref.shape[1], 256)

    @pl.loop(0, out_ref.shape[1] // tile)
    def _(n):
        columns = pl.ds(pl.multiple_of(n * tile, tile), tile)
        gate_part = matmul(rows_ref[...], gate_ref[0, :, columns])
        up_part = matmul(rows_ref[...], up_ref[0, :, columns])
        out_ref[:, columns] = (jax.nn.silu(gate_part) * up_part).astype(out_ref.dtype)


def hidden_units(pieces, w_gate, w_up, first):
    depth, units = w_gate.shape[1:]
    rows = sum(piece.shape[0] for piece in pieces)
    vmem = pl.BlockSpec(memory_space=pltpu.VMEM)
    place = pltpu.HBM if first else pltpu.VMEM
    out_shape = [jax.ShapeDtypeStruct((rows, units), jnp.bfloat16)]
    scratch = [pltpu.VMEM((rows, depth), jnp.bfloat16)]
    if first:
        out_shape.append(pltpu.VMEM(w_up.shape, w_up.dtype))
        scratch += [pltpu.VMEM((rows, units), jnp.float32), pltpu.SemaphoreType.DMA((PARTS,))]
    return pl.pallas_call(
        functools.partial(first_hidden_kernel if first else hidden_kernel, len(pieces)),
        in_specs=[vmem] * (len(pieces) + 1) + [pl.BlockSpec(memory_space=place)],
        out_specs=[vmem] * len(out_shape),
        out_shape=out_shape,
        scratch_shapes=scratch,
        compiler_params=pltpu.CompilerParams(vmem_limit_bytes=10 * rows * (depth + units) + 2 * MIB),
        cost_estimate=pl.CostEstimate(
            flops=4 * rows * depth * units,
            bytes_accessed=2 * rows * (depth + units),
            transcendentals=rows * units,
        ),
    )(*pieces, in_vmem(w_gate), pltpu.with_memory_space_constraint(w_up, place))


def down_columns(half, place, parts, weight_ref, out_ref, columns):
    size, units = len(parts), parts[0].shape[1]
    total = 0.0
    for k, part in enumerate(parts):
        owner = lax.rem(place[0] + (size - k), size)
        rows = pl.ds(pl.multiple_of(owner * units, units), units)
        left = part[...]
        if k:
            left = jnp.concatenate([left[-k * half:], left[:-k * half]], axis=0)
        total += matmul(left, weight_ref[0, rows, columns])
    out_ref[:, columns] = total.astype(out_ref.dtype)


def first_down_kernel(half, count, place, *refs):
    parts, (weight_hbm, out_ref, weight_ref, sem) = refs[:count], refs[count:]
    copies = copies_of(weight_hbm, weight_ref, sem, 2)
    for copy in copies:
        copy.start()
    tile = out_ref.shape[1] // len(copies)
    for p, copy in enumerate(copies):
        copy.wait()
        down_columns(half, place, parts, weight_ref, out_ref, slice(p * tile, (p + 1) * tile))


def down_kernel(half, count, place, *refs):
    parts, (weight_ref, out_ref) = refs[:count], refs[count:]
    tile = tile_of(out_ref.shape[1], 512)

    @pl.loop(0, out_ref.shape[1] // tile)
    def _(n):
        columns = pl.ds(pl.multiple_of(n * tile, tile), tile)
        down_columns(half, place, parts, weight_ref, out_ref, columns)


def down_slices(parts, half, place, w_down, first):
    units, width = w_down.shape[1:]
    rows = parts[0].shape[0]
    vmem = pl.BlockSpec(memory_space=pltpu.VMEM)
    weight_place = pltpu.HBM if first else pltpu.VMEM
    out_shape = [jax.ShapeDtypeStruct((rows, width), jnp.bfloat16)]
    if first:
        out_shape.append(pltpu.VMEM(w_down.shape, w_down.dtype))
    return pl.pallas_call(
        functools.partial(first_down_kernel if first else down_kernel, half, len(parts)),
        in_specs=[pl.BlockSpec(memory_space=pltpu.SMEM)]
        + [vmem] * len(parts)
        + [pl.BlockSpec(memory_space=weight_place)],
        out_specs=[vmem] * len(out_shape),
        out_shape=out_shape,
        scratch_shapes=[pltpu.SemaphoreType.DMA((PARTS,))] * first,
        compiler_params=pltpu.CompilerParams(vmem_limit_bytes=8 * rows * (units + width) + 2 * MIB),
        cost_estimate=pl.CostEstimate(
            flops=2 * rows * units * width,
            bytes_accessed=2 * rows * (units + width),
            transcendentals=0,
        ),
    )(place, *parts, pltpu.with_memory_space_constraint(w_down, weight_place))


def mix_kernel(blocks, *refs):
    place, weights, pieces, out_ref = refs[0], refs[1], refs[2:-1], refs[-1]
    width = out_ref.shape[1] // blocks
    tile = tile_of(width, 512)
    for k in range(blocks):
        start = lax.rem(place[0] + k, blocks) * width
        for n in range(0, width, tile):
            rows = jnp.concatenate([piece[k, :, n:n + tile] for piece in pieces], axis=0)
            columns = pl.ds(pl.multiple_of(start + n, 128), tile)
            out_ref[:, columns] = matmul(weights[...], rows).astype(out_ref.dtype)


def mixed_rows(weights, pieces, place):
    blocks, half, width = pieces[0].shape
    tokens = weights.shape[0]
    return pl.pallas_call(
        functools.partial(mix_kernel, blocks),
        in_specs=[pl.BlockSpec(memory_space=pltpu.SMEM)]
        + [pl.BlockSpec(memory_space=pltpu.VMEM)] * (len(pieces) + 1),
        out_specs=pl.BlockSpec(memory_space=pltpu.VMEM),
        out_shape=jax.ShapeDtypeStruct((tokens, blocks * width), jnp.bfloat16),
        compiler_params=pltpu.CompilerParams(
            vmem_limit_bytes=4 * blocks * width * (len(pieces) * half + tokens) + 2 * MIB
        ),
    )(place, weights, *pieces)


def on_device(tokens, expert_ids, gate_weights, w_gate, w_up, w_down):
    experts, blocks = lax.axis_size("expert"), lax.axis_size("blk")
    me, mine = lax.axis_index("expert"), lax.axis_index("blk")
    levels = experts // 4
    unit = 2 * CAP
    half = levels * unit
    down_mat = w_down[0]

    turns = jnp.arange(2 * levels, dtype=jnp.int32)
    turns = (turns // levels) * ROW + (turns % levels) * (2 * ROW)
    near, far = me ^ turns, me ^ CORE ^ turns

    other_ids = exchanged(expert_ids, CORE, "ids")
    other_tokens = exchanged(tokens, CORE, "tokens")
    own_slots, far_slots = slots_of(expert_ids, near), slots_of(expert_ids, far)
    nothing = jnp.zeros_like(own_slots)
    pick = side_by_side(own_slots, nothing).astype(jnp.bfloat16)
    pick_other = side_by_side(nothing, slots_of(other_ids, near)).astype(jnp.bfloat16)
    chosen = (matmul(pick.T, tokens) + matmul(pick_other.T, other_tokens)).astype(jnp.bfloat16)

    own_weights = jnp.where(own_slots, weights_of(expert_ids, gate_weights, near)[:, :, None], 0.0)
    far_weights = jnp.where(far_slots, weights_of(expert_ids, gate_weights, far)[:, :, None], 0.0)
    zeros = jnp.zeros_like(own_weights)
    own_weights, far_weights = side_by_side(own_weights, zeros), side_by_side(zeros, far_weights)
    weighting = jnp.concatenate(
        [own_weights[:, :half], far_weights[:, :half], own_weights[:, half:], far_weights[:, half:]], axis=1
    )
    weighting = weighting.astype(jnp.bfloat16)
    place = mine.reshape(1).astype(jnp.int32)
    w_gate, weighting, place, _ = lax.optimization_barrier((w_gate, weighting, place, chosen))

    def split(rows):
        return [rows[z * unit:(z + 1) * unit] for z in range(levels)]

    def over_blk(piece, name):
        return [shifted(piece, k, name) for k in range(1, blocks)]

    stay, leave = split(chosen[:half]), split(chosen[half:])
    for z in range(levels - 1, 0, -1):
        stay[z] = exchanged(stay[z], z * 2 * ROW, "go_stay")
    first_stay = over_blk(stay[0], "first_stay")
    leave[0] = exchanged(leave[0], ROW, "go_leave")
    w_gate = loaded(w_gate)
    leave[1:], w_gate = lax.optimization_barrier((leave[1:], w_gate))
    for z in range(levels - 1, 0, -1):
        leave[z] = exchanged(leave[z], z * 2 * ROW + ROW, "go_leave")
    first, rest = leave[0], jnp.concatenate(stay[1:], axis=0)
    middle = over_blk(jnp.concatenate([rest, first], axis=0), "middle")
    stay = [stay[0], rest] + sum([[a, b[:-unit]] for a, b in zip(first_stay, middle)], [])
    rest = jnp.concatenate(leave[1:], axis=0)
    rest_leave = over_blk(rest, "rest_leave")
    rest, stay = lax.optimization_barrier((rest, stay))
    leave = [first, rest] + sum([[a[-unit:], b] for a, b in zip(middle, rest_leave)], [])

    hidden, w_up = hidden_units(stay, w_gate, w_up, True)
    stay = [hidden] + over_blk(hidden, "hidden_stay")
    hidden, = hidden_units(leave, w_gate, w_up, False)
    stay, hidden, w_down = lax.optimization_barrier((stay, hidden, w_down))
    leave = [hidden] + over_blk(hidden, "hidden_leave")
    stay, w_down = down_slices(stay, half, place, w_down, True)
    stay, leave = lax.optimization_barrier((stay, leave))

    def back(output, turn, name):
        received = [split(output[k * half:(k + 1) * half]) for k in range(blocks)]
        for k in range(blocks):
            for z in range(levels - 1, -1, -1):
                mask = z * 2 * ROW + turn
                if k:
                    received[k][z] = crossed(received[k][z], mask, k, name)
                elif mask:
                    received[k][z] = exchanged(received[k][z], mask, name)
        return received

    stay = back(stay, 0, "back_stay")
    stay[-1][0], leave, w_down = lax.optimization_barrier((stay[-1][0], leave, w_down))
    leave, = down_slices(leave, half, place, w_down, False)
    leave = back(leave, ROW, "back_leave")
    returned = []
    for pieces, name in ((stay, "pair_stay"), (leave, "pair_leave")):
        rows = jnp.stack([jnp.concatenate(part, axis=0) for part in pieces])
        returned += [rows, exchanged(rows, CORE, name)]
    return mixed_rows(weighting, returned, place)


def solution(mesh):
    return jax.shard_map(
        on_device,
        mesh=mesh,
        in_specs=(
            P(("expert", "blk"), None),
            P(("expert", "blk"), None),
            P(("expert", "blk"), None),
            P("expert", None, "blk"),
            P("expert", None, "blk"),
            P("expert", None, "blk"),
        ),
        out_specs=P(("expert", "blk"), None),
        check_vma=False,
    )
```

```python
import functools

import jax
import jax.numpy as jnp
from jax import lax
from jax.experimental import pallas as pl
from jax.experimental.pallas import tpu as pltpu
from jax.sharding import PartitionSpec as P

CAP = 4
CORE, ROW = 1, 2
MIB = 1 << 20
PARTS = 4
ROOM = 13 * MIB


def exchanged(block, mask, name):
    size = lax.axis_size("expert")
    with jax.named_scope(f"{name}_{mask}"):
        return lax.ppermute(block, "expert", [(i, i ^ mask) for i in range(size)])


def shifted(block, steps, name):
    size = lax.axis_size("blk")
    with jax.named_scope(f"{name}_{steps}"):
        return lax.ppermute(block, "blk", [(i, (i + steps) % size) for i in range(size)])


def matmul(left, right):
    return jnp.dot(left, right, preferred_element_type=jnp.float32)


def slots_of(id_rows, labels):
    matches = id_rows[:, :, None] == labels[None, None, :]
    chosen = jnp.any(matches, axis=1)
    counts = chosen.astype(jnp.int32)
    before = jnp.cumsum(counts, axis=0) - counts
    places = jnp.arange(CAP, dtype=jnp.int32)
    return chosen[:, :, None] & (before[:, :, None] == places[None, None, :])


def weights_of(id_rows, gate_rows, labels):
    matches = id_rows[:, :, None] == labels[None, None, :]
    return jnp.sum(jnp.where(matches, gate_rows.astype(jnp.float32)[:, :, None], 0.0), axis=1)


def side_by_side(first, second):
    return jnp.stack([first, second], axis=2).reshape(first.shape[0], -1)


def tile_of(size, most):
    return max(t for t in range(128, most + 1, 128) if size % t == 0)


def parts_of(size, unit):
    return max(p for p in range(1, PARTS + 1) if size % (p * unit) == 0)


def copies_of(source, target, sem, dim):
    count = parts_of(source.shape[dim], 128)
    step = source.shape[dim] // count
    copies = []
    for p in range(count):
        part = (0, pl.ds(p * step, step)) if dim == 1 else (0, slice(None), pl.ds(p * step, step))
        copies.append(pltpu.make_async_copy(source.at[part], target.at[part], sem.at[p]))
    return copies


def load_kernel(source, target, sem):
    copies = copies_of(source, target, sem, 1)
    for copy in copies:
        copy.start()
    for copy in copies:
        copy.wait()


def loaded(weight):
    return pl.pallas_call(
        load_kernel,
        in_specs=[pl.BlockSpec(memory_space=pltpu.HBM)],
        out_specs=pl.BlockSpec(memory_space=pltpu.VMEM),
        out_shape=pltpu.VMEM(weight.shape, weight.dtype),
        scratch_shapes=[pltpu.SemaphoreType.DMA((PARTS,))],
        compiler_params=pltpu.CompilerParams(vmem_limit_bytes=ROOM),
        cost_estimate=pl.CostEstimate(
            flops=0, bytes_accessed=weight.size * weight.dtype.itemsize, transcendentals=0
        ),
    )(pltpu.with_memory_space_constraint(weight, pltpu.HBM))


def in_vmem(weight):
    return pltpu.with_memory_space_constraint(weight, pltpu.VMEM)


def gathered(pieces, ranges, rows_ref):
    rows = [piece[...].astype(jnp.float32)[start:stop] for piece, (start, stop) in zip(pieces, ranges)]
    rows_ref[...] = jnp.concatenate(rows, axis=0).astype(jnp.bfloat16)


def first_hidden_kernel(ranges, *refs):
    count = len(ranges)
    pieces, (gate_ref, up_hbm, out_ref, up_ref, rows_ref, gate_part, sem) = refs[:count], refs[count:]
    copies = copies_of(up_hbm, up_ref, sem, 2)
    for copy in copies:
        copy.start()
    gathered(pieces, ranges, rows_ref)
    tile = out_ref.shape[1] // len(copies)
    parts = [slice(p * tile, (p + 1) * tile) for p in range(len(copies))]
    for columns in parts:
        gate_part[:, columns] = jax.nn.silu(matmul(rows_ref[...], gate_ref[0, :, columns]))
    for columns, copy in zip(parts, copies):
        copy.wait()
        up_part = matmul(rows_ref[...], up_ref[0, :, columns])
        out_ref[:, columns] = (gate_part[:, columns] * up_part).astype(out_ref.dtype)


def hidden_kernel(ranges, *refs):
    count = len(ranges)
    pieces, (gate_ref, up_ref, out_ref, rows_ref) = refs[:count], refs[count:]
    gathered(pieces, ranges, rows_ref)
    tile = tile_of(out_ref.shape[1], 256)

    @pl.loop(0, out_ref.shape[1] // tile)
    def _(n):
        columns = pl.ds(pl.multiple_of(n * tile, tile), tile)
        gate_part = matmul(rows_ref[...], gate_ref[0, :, columns])
        up_part = matmul(rows_ref[...], up_ref[0, :, columns])
        out_ref[:, columns] = (jax.nn.silu(gate_part) * up_part).astype(out_ref.dtype)


def hidden_units(pieces, w_gate, w_up, first):
    depth, units = w_gate.shape[1:]
    ranges = [(start, stop) for _, start, stop in pieces]
    pieces = [piece for piece, _, _ in pieces]
    rows = sum(stop - start for start, stop in ranges)
    vmem = pl.BlockSpec(memory_space=pltpu.VMEM)
    place = pltpu.HBM if first else pltpu.VMEM
    out_shape = [jax.ShapeDtypeStruct((rows, units), jnp.bfloat16)]
    scratch = [pltpu.VMEM((rows, depth), jnp.bfloat16)]
    if first:
        out_shape.append(pltpu.VMEM(w_up.shape, w_up.dtype))
        scratch += [pltpu.VMEM((rows, units), jnp.float32), pltpu.SemaphoreType.DMA((PARTS,))]
    return pl.pallas_call(
        functools.partial(first_hidden_kernel if first else hidden_kernel, ranges),
        in_specs=[vmem] * (len(pieces) + 1) + [pl.BlockSpec(memory_space=place)],
        out_specs=[vmem] * len(out_shape),
        out_shape=out_shape,
        scratch_shapes=scratch,
        compiler_params=pltpu.CompilerParams(vmem_limit_bytes=max(ROOM, 10 * rows * (depth + units) + 2 * MIB)),
        cost_estimate=pl.CostEstimate(
            flops=4 * rows * depth * units,
            bytes_accessed=2 * rows * (depth + units),
            transcendentals=rows * units,
        ),
    )(*pieces, in_vmem(w_gate), pltpu.with_memory_space_constraint(w_up, place))


def down_columns(half, place, parts, weight_ref, out_ref, columns):
    size, units = len(parts), parts[0].shape[1]
    total = 0.0
    for k, part in enumerate(parts):
        owner = lax.rem(place[0] + (size - k), size)
        rows = pl.ds(pl.multiple_of(owner * units, units), units)
        left = part[...]
        if k:
            left = jnp.concatenate([left[-k * half:], left[:-k * half]], axis=0)
        total += matmul(left, weight_ref[0, rows, columns])
    out_ref[:, columns] = total.astype(out_ref.dtype)


def first_down_kernel(half, count, place, *refs):
    parts, (weight_hbm, out_ref, weight_ref, sem) = refs[:count], refs[count:]
    copies = copies_of(weight_hbm, weight_ref, sem, 2)
    for copy in copies:
        copy.start()
    tile = out_ref.shape[1] // len(copies)
    for p, copy in enumerate(copies):
        copy.wait()
        down_columns(half, place, parts, weight_ref, out_ref, slice(p * tile, (p + 1) * tile))


def down_kernel(half, count, place, *refs):
    parts, (weight_ref, out_ref) = refs[:count], refs[count:]
    tile = tile_of(out_ref.shape[1], 512)

    @pl.loop(0, out_ref.shape[1] // tile)
    def _(n):
        columns = pl.ds(pl.multiple_of(n * tile, tile), tile)
        down_columns(half, place, parts, weight_ref, out_ref, columns)


def down_slices(parts, half, place, w_down, first):
    units, width = w_down.shape[1:]
    rows = parts[0].shape[0]
    vmem = pl.BlockSpec(memory_space=pltpu.VMEM)
    weight_place = pltpu.HBM if first else pltpu.VMEM
    out_shape = [jax.ShapeDtypeStruct((rows, width), jnp.bfloat16)]
    if first:
        out_shape.append(pltpu.VMEM(w_down.shape, w_down.dtype))
    return pl.pallas_call(
        functools.partial(first_down_kernel if first else down_kernel, half, len(parts)),
        in_specs=[pl.BlockSpec(memory_space=pltpu.SMEM)]
        + [vmem] * len(parts)
        + [pl.BlockSpec(memory_space=weight_place)],
        out_specs=[vmem] * len(out_shape),
        out_shape=out_shape,
        scratch_shapes=[pltpu.SemaphoreType.DMA((PARTS,))] * first,
        compiler_params=pltpu.CompilerParams(vmem_limit_bytes=max(ROOM, 8 * rows * (units + width) + 2 * MIB)),
        cost_estimate=pl.CostEstimate(
            flops=2 * rows * units * width,
            bytes_accessed=2 * rows * (units + width),
            transcendentals=0,
        ),
    )(place, *parts, pltpu.with_memory_space_constraint(w_down, weight_place))


def mix_kernel(blocks, *refs):
    place, weights, pieces, out_ref = refs[0], refs[1], refs[2:-1], refs[-1]
    width = out_ref.shape[1] // blocks
    tile = tile_of(width, 512)
    for k in range(blocks):
        start = lax.rem(place[0] + k, blocks) * width
        for n in range(0, width, tile):
            rows = jnp.concatenate([piece[k, :, n:n + tile] for piece in pieces], axis=0)
            columns = pl.ds(pl.multiple_of(start + n, 128), tile)
            out_ref[:, columns] = matmul(weights[...], rows).astype(out_ref.dtype)


def mixed_rows(weights, pieces, place):
    blocks, half, width = pieces[0].shape
    tokens = weights.shape[0]
    return pl.pallas_call(
        functools.partial(mix_kernel, blocks),
        in_specs=[pl.BlockSpec(memory_space=pltpu.SMEM)]
        + [pl.BlockSpec(memory_space=pltpu.VMEM)] * (len(pieces) + 1),
        out_specs=pl.BlockSpec(memory_space=pltpu.VMEM),
        out_shape=jax.ShapeDtypeStruct((tokens, blocks * width), jnp.bfloat16),
        compiler_params=pltpu.CompilerParams(
            vmem_limit_bytes=4 * blocks * width * (len(pieces) * half + tokens) + 2 * MIB
        ),
    )(place, weights, *pieces)


def on_device(tokens, expert_ids, gate_weights, w_gate, w_up, w_down):
    experts, blocks = lax.axis_size("expert"), lax.axis_size("blk")
    me, mine = lax.axis_index("expert"), lax.axis_index("blk")
    levels = experts // 4
    unit = 2 * CAP
    half = levels * unit
    down_mat = w_down[0]

    turns = jnp.arange(2 * levels, dtype=jnp.int32)
    turns = (turns // levels) * ROW + (turns % levels) * (2 * ROW)
    near, far = me ^ turns, me ^ CORE ^ turns

    other_ids = exchanged(expert_ids, CORE, "ids")
    other_tokens = exchanged(tokens, CORE, "tokens")
    own_slots, far_slots = slots_of(expert_ids, near), slots_of(expert_ids, far)
    nothing = jnp.zeros_like(own_slots)
    pick = side_by_side(own_slots, nothing).astype(jnp.bfloat16)
    pick_other = side_by_side(nothing, slots_of(other_ids, near)).astype(jnp.bfloat16)
    chosen = (matmul(pick.T, tokens) + matmul(pick_other.T, other_tokens)).astype(jnp.bfloat16)

    own_weights = jnp.where(own_slots, weights_of(expert_ids, gate_weights, near)[:, :, None], 0.0)
    far_weights = jnp.where(far_slots, weights_of(expert_ids, gate_weights, far)[:, :, None], 0.0)
    zeros = jnp.zeros_like(own_weights)
    own_weights, far_weights = side_by_side(own_weights, zeros), side_by_side(zeros, far_weights)
    weighting = jnp.concatenate(
        [own_weights[:, :half], far_weights[:, :half], own_weights[:, half:], far_weights[:, half:]], axis=1
    )
    weighting = weighting.astype(jnp.bfloat16)
    place = mine.reshape(1).astype(jnp.int32)
    w_gate, weighting, place, _ = lax.optimization_barrier((w_gate, weighting, place, chosen))

    def split(rows):
        return [rows[z * unit:(z + 1) * unit] for z in range(levels)]

    def over_blk(piece, name):
        return [shifted(piece, k, name) for k in range(1, blocks)]

    stay, leave = split(chosen[:half]), split(chosen[half:])
    for z in range(levels - 1, 0, -1):
        stay[z] = exchanged(stay[z], z * 2 * ROW, "go_stay")
    first_stay = over_blk(stay[0], "first_stay")
    leave[0] = exchanged(leave[0], ROW, "go_leave")
    w_gate = loaded(w_gate)
    leave[1:], w_gate = lax.optimization_barrier((leave[1:], w_gate))
    for z in range(levels - 1, 0, -1):
        leave[z] = exchanged(leave[z], z * 2 * ROW + ROW, "go_leave")
    first, rest = leave[0], jnp.concatenate(stay[1:], axis=0)
    middle = over_blk(jnp.concatenate([rest, first], axis=0), "middle")
    cut = half - unit
    stay = [(stay[0], 0, unit), (rest, 0, cut)]
    stay += sum([[(a, 0, unit), (b, 0, cut)] for a, b in zip(first_stay, middle)], [])
    rest = jnp.concatenate(leave[1:], axis=0)
    rest_leave = over_blk(rest, "rest_leave")
    arrays, rest = lax.optimization_barrier(([piece for piece, _, _ in stay], rest))
    stay = [(array, start, stop) for array, (_, start, stop) in zip(arrays, stay)]
    leave = [(first, 0, unit), (rest, 0, cut)]
    leave += sum([[(a, cut, half), (b, 0, cut)] for a, b in zip(middle, rest_leave)], [])

    hidden, w_up = hidden_units(stay, w_gate, w_up, True)
    stay = [hidden] + over_blk(hidden, "hidden_stay")
    hidden, = hidden_units(leave, w_gate, w_up, False)
    stay, hidden, w_down = lax.optimization_barrier((stay, hidden, w_down))
    leave = [hidden] + over_blk(hidden, "hidden_leave")
    stay, w_down = down_slices(stay, half, place, w_down, True)
    stay, leave = lax.optimization_barrier((stay, leave))

    def back(pieces, turn, name):
        received = [pieces[:, z * unit:(z + 1) * unit] for z in range(levels)]
        for z in range(levels - 1, -1, -1):
            mask = z * 2 * ROW + turn
            if mask:
                received[z] = exchanged(received[z], mask, name)
        return jnp.concatenate(received, axis=1)

    def to_owners(slices, name):
        return jnp.stack([slices[0]] + [shifted(slices[k], blocks - k, name) for k in range(1, blocks)])

    def by_blk(output):
        return output.reshape(blocks, half, output.shape[1])

    stay = to_owners(back(by_blk(stay), 0, "back_stay"), "own_stay")
    leave, = down_slices(leave, half, place, w_down, False)
    leave = back(to_owners(by_blk(leave), "own_leave"), ROW, "back_leave")
    returned = [stay, exchanged(stay, CORE, "pair_stay"), leave, exchanged(leave, CORE, "pair_leave")]
    return mixed_rows(weighting, returned, place)


def solution(mesh):
    return jax.shard_map(
        on_device,
        mesh=mesh,
        in_specs=(
            P(("expert", "blk"), None),
            P(("expert", "blk"), None),
            P(("expert", "blk"), None),
            P("expert", None, "blk"),
            P("expert", None, "blk"),
            P("expert", None, "blk"),
        ),
        out_specs=P(("expert", "blk"), None),
        check_vma=False,
    )
```

```python
import functools

import jax
import jax.numpy as jnp
from jax import lax
from jax.experimental import pallas as pl
from jax.experimental.pallas import tpu as pltpu
from jax.sharding import PartitionSpec as P

CAP = 4
CORE, ROW = 1, 2
MIB = 1 << 20
PARTS = 4
ROOM = 13 * MIB


def exchanged(block, mask, name):
    size = lax.axis_size("expert")
    with jax.named_scope(f"{name}_{mask}"):
        return lax.ppermute(block, "expert", [(i, i ^ mask) for i in range(size)])


def shifted(block, steps, name):
    size = lax.axis_size("blk")
    with jax.named_scope(f"{name}_{steps}"):
        return lax.ppermute(block, "blk", [(i, (i + steps) % size) for i in range(size)])


def matmul(left, right):
    return jnp.dot(left, right, preferred_element_type=jnp.float32)


def slots_of(id_rows, labels):
    matches = id_rows[:, :, None] == labels[None, None, :]
    chosen = jnp.any(matches, axis=1)
    counts = chosen.astype(jnp.int32)
    before = jnp.cumsum(counts, axis=0) - counts
    places = jnp.arange(CAP, dtype=jnp.int32)
    return chosen[:, :, None] & (before[:, :, None] == places[None, None, :])


def weights_of(id_rows, gate_rows, labels):
    matches = id_rows[:, :, None] == labels[None, None, :]
    return jnp.sum(jnp.where(matches, gate_rows.astype(jnp.float32)[:, :, None], 0.0), axis=1)


def side_by_side(first, second):
    return jnp.stack([first, second], axis=2).reshape(first.shape[0], -1)


def tile_of(size, most):
    return max(t for t in range(128, most + 1, 128) if size % t == 0)


def parts_of(size, unit):
    return max(p for p in range(1, PARTS + 1) if size % (p * unit) == 0)


def copies_of(source, target, sem, dim):
    count = parts_of(source.shape[dim], 128)
    step = source.shape[dim] // count
    copies = []
    for p in range(count):
        part = (0, pl.ds(p * step, step)) if dim == 1 else (0, slice(None), pl.ds(p * step, step))
        copies.append(pltpu.make_async_copy(source.at[part], target.at[part], sem.at[p]))
    return copies


def load_kernel(source, target, sem):
    copies = copies_of(source, target, sem, 1)
    for copy in copies:
        copy.start()
    for copy in copies:
        copy.wait()


def loaded(weight):
    return pl.pallas_call(
        load_kernel,
        in_specs=[pl.BlockSpec(memory_space=pltpu.HBM)],
        out_specs=pl.BlockSpec(memory_space=pltpu.VMEM),
        out_shape=pltpu.VMEM(weight.shape, weight.dtype),
        scratch_shapes=[pltpu.SemaphoreType.DMA((PARTS,))],
        compiler_params=pltpu.CompilerParams(vmem_limit_bytes=ROOM),
        cost_estimate=pl.CostEstimate(
            flops=0, bytes_accessed=weight.size * weight.dtype.itemsize, transcendentals=0
        ),
    )(pltpu.with_memory_space_constraint(weight, pltpu.HBM))


def in_vmem(weight):
    return pltpu.with_memory_space_constraint(weight, pltpu.VMEM)


def gathered(pieces, ranges, rows_ref):
    rows = [piece[...].astype(jnp.float32)[start:stop] for piece, (start, stop) in zip(pieces, ranges)]
    rows_ref[...] = jnp.concatenate(rows, axis=0).astype(jnp.bfloat16)


def first_hidden_kernel(ranges, *refs):
    count = len(ranges)
    pieces, (gate_ref, up_hbm, out_ref, up_ref, rows_ref, gate_part, sem) = refs[:count], refs[count:]
    copies = copies_of(up_hbm, up_ref, sem, 2)
    for copy in copies:
        copy.start()
    gathered(pieces, ranges, rows_ref)
    tile = out_ref.shape[1] // len(copies)
    parts = [slice(p * tile, (p + 1) * tile) for p in range(len(copies))]
    for columns in parts:
        gate_part[:, columns] = jax.nn.silu(matmul(rows_ref[...], gate_ref[0, :, columns]))
    for columns, copy in zip(parts, copies):
        copy.wait()
        up_part = matmul(rows_ref[...], up_ref[0, :, columns])
        out_ref[:, columns] = (gate_part[:, columns] * up_part).astype(out_ref.dtype)


def hidden_kernel(ranges, *refs):
    count = len(ranges)
    pieces, (gate_ref, up_ref, out_ref, rows_ref) = refs[:count], refs[count:]
    gathered(pieces, ranges, rows_ref)
    tile = tile_of(out_ref.shape[1], 256)

    @pl.loop(0, out_ref.shape[1] // tile)
    def _(n):
        columns = pl.ds(pl.multiple_of(n * tile, tile), tile)
        gate_part = matmul(rows_ref[...], gate_ref[0, :, columns])
        up_part = matmul(rows_ref[...], up_ref[0, :, columns])
        out_ref[:, columns] = (jax.nn.silu(gate_part) * up_part).astype(out_ref.dtype)


def hidden_units(pieces, w_gate, w_up, first):
    depth, units = w_gate.shape[1:]
    ranges = [(start, stop) for _, start, stop in pieces]
    pieces = [piece for piece, _, _ in pieces]
    rows = sum(stop - start for start, stop in ranges)
    vmem = pl.BlockSpec(memory_space=pltpu.VMEM)
    place = pltpu.HBM if first else pltpu.VMEM
    out_shape = [jax.ShapeDtypeStruct((rows, units), jnp.bfloat16)]
    scratch = [pltpu.VMEM((rows, depth), jnp.bfloat16)]
    if first:
        out_shape.append(pltpu.VMEM(w_up.shape, w_up.dtype))
        scratch += [pltpu.VMEM((rows, units), jnp.float32), pltpu.SemaphoreType.DMA((PARTS,))]
    return pl.pallas_call(
        functools.partial(first_hidden_kernel if first else hidden_kernel, ranges),
        in_specs=[vmem] * (len(pieces) + 1) + [pl.BlockSpec(memory_space=place)],
        out_specs=[vmem] * len(out_shape),
        out_shape=out_shape,
        scratch_shapes=scratch,
        compiler_params=pltpu.CompilerParams(vmem_limit_bytes=max(ROOM, 10 * rows * (depth + units) + 2 * MIB)),
        cost_estimate=pl.CostEstimate(
            flops=4 * rows * depth * units,
            bytes_accessed=2 * rows * (depth + units),
            transcendentals=rows * units,
        ),
    )(*pieces, in_vmem(w_gate), pltpu.with_memory_space_constraint(w_up, place))


def down_columns(half, place, parts, weight_ref, out_ref, columns):
    size, units = len(parts), parts[0].shape[1]
    total = 0.0
    for k, part in enumerate(parts):
        owner = lax.rem(place[0] + (size - k), size)
        rows = pl.ds(pl.multiple_of(owner * units, units), units)
        left = part[...]
        if k:
            left = jnp.concatenate([left[-k * half:], left[:-k * half]], axis=0)
        total += matmul(left, weight_ref[0, rows, columns])
    out_ref[:, columns] = total.astype(out_ref.dtype)


def first_down_kernel(half, count, place, *refs):
    parts, (weight_hbm, out_ref, weight_ref, sem) = refs[:count], refs[count:]
    copies = copies_of(weight_hbm, weight_ref, sem, 2)
    for copy in copies:
        copy.start()
    tile = out_ref.shape[1] // len(copies)
    for p, copy in enumerate(copies):
        copy.wait()
        down_columns(half, place, parts, weight_ref, out_ref, slice(p * tile, (p + 1) * tile))


def down_kernel(half, count, place, *refs):
    parts, (weight_ref, out_ref) = refs[:count], refs[count:]
    tile = tile_of(out_ref.shape[1], 512)

    @pl.loop(0, out_ref.shape[1] // tile)
    def _(n):
        columns = pl.ds(pl.multiple_of(n * tile, tile), tile)
        down_columns(half, place, parts, weight_ref, out_ref, columns)


def down_slices(parts, half, place, w_down, first):
    units, width = w_down.shape[1:]
    rows = parts[0].shape[0]
    vmem = pl.BlockSpec(memory_space=pltpu.VMEM)
    weight_place = pltpu.HBM if first else pltpu.VMEM
    out_shape = [jax.ShapeDtypeStruct((rows, width), jnp.bfloat16)]
    if first:
        out_shape.append(pltpu.VMEM(w_down.shape, w_down.dtype))
    return pl.pallas_call(
        functools.partial(first_down_kernel if first else down_kernel, half, len(parts)),
        in_specs=[pl.BlockSpec(memory_space=pltpu.SMEM)]
        + [vmem] * len(parts)
        + [pl.BlockSpec(memory_space=weight_place)],
        out_specs=[vmem] * len(out_shape),
        out_shape=out_shape,
        scratch_shapes=[pltpu.SemaphoreType.DMA((PARTS,))] * first,
        compiler_params=pltpu.CompilerParams(vmem_limit_bytes=max(ROOM, 8 * rows * (units + width) + 2 * MIB)),
        cost_estimate=pl.CostEstimate(
            flops=2 * rows * units * width,
            bytes_accessed=2 * rows * (units + width),
            transcendentals=0,
        ),
    )(place, *parts, pltpu.with_memory_space_constraint(w_down, weight_place))


def mix_kernel(blocks, *refs):
    place, weights, pieces, out_ref = refs[0], refs[1], refs[2:-1], refs[-1]
    width = out_ref.shape[1] // blocks
    tile = tile_of(width, 512)
    for k in range(blocks):
        start = lax.rem(place[0] + k, blocks) * width
        for n in range(0, width, tile):
            rows = jnp.concatenate([piece[k, :, n:n + tile] for piece in pieces], axis=0)
            columns = pl.ds(pl.multiple_of(start + n, 128), tile)
            out_ref[:, columns] = matmul(weights[...], rows).astype(out_ref.dtype)


def mixed_rows(weights, pieces, place):
    blocks, half, width = pieces[0].shape
    tokens = weights.shape[0]
    return pl.pallas_call(
        functools.partial(mix_kernel, blocks),
        in_specs=[pl.BlockSpec(memory_space=pltpu.SMEM)]
        + [pl.BlockSpec(memory_space=pltpu.VMEM)] * (len(pieces) + 1),
        out_specs=pl.BlockSpec(memory_space=pltpu.VMEM),
        out_shape=jax.ShapeDtypeStruct((tokens, blocks * width), jnp.bfloat16),
        compiler_params=pltpu.CompilerParams(
            vmem_limit_bytes=4 * blocks * width * (len(pieces) * half + tokens) + 2 * MIB
        ),
    )(place, weights, *pieces)


def on_device(tokens, expert_ids, gate_weights, w_gate, w_up, w_down):
    experts, blocks = lax.axis_size("expert"), lax.axis_size("blk")
    me, mine = lax.axis_index("expert"), lax.axis_index("blk")
    levels = experts // 4
    unit = 2 * CAP
    half = levels * unit
    down_mat = w_down[0]

    turns = jnp.arange(2 * levels, dtype=jnp.int32)
    turns = (turns // levels) * ROW + (turns % levels) * (2 * ROW)
    near, far = me ^ turns, me ^ CORE ^ turns

    other_ids = exchanged(expert_ids, CORE, "ids")
    other_tokens = exchanged(tokens, CORE, "tokens")
    own_slots, far_slots = slots_of(expert_ids, near), slots_of(expert_ids, far)
    nothing = jnp.zeros_like(own_slots)
    pick = side_by_side(own_slots, nothing).astype(jnp.bfloat16)
    pick_other = side_by_side(nothing, slots_of(other_ids, near)).astype(jnp.bfloat16)
    chosen = (matmul(pick.T, tokens) + matmul(pick_other.T, other_tokens)).astype(jnp.bfloat16)

    own_weights = jnp.where(own_slots, weights_of(expert_ids, gate_weights, near)[:, :, None], 0.0)
    far_weights = jnp.where(far_slots, weights_of(expert_ids, gate_weights, far)[:, :, None], 0.0)
    zeros = jnp.zeros_like(own_weights)
    own_weights, far_weights = side_by_side(own_weights, zeros), side_by_side(zeros, far_weights)
    weighting = jnp.concatenate(
        [own_weights[:, :half], far_weights[:, :half], own_weights[:, half:], far_weights[:, half:]], axis=1
    )
    weighting = weighting.astype(jnp.bfloat16)
    place = mine.reshape(1).astype(jnp.int32)
    w_gate, weighting, place, _ = lax.optimization_barrier((w_gate, weighting, place, chosen))

    def split(rows):
        return [rows[z * unit:(z + 1) * unit] for z in range(levels)]

    def over_blk(piece, name):
        return [shifted(piece, k, name) for k in range(1, blocks)]

    stay, leave = split(chosen[:half]), split(chosen[half:])
    first = over_blk(stay[0], "blk_first")
    for z in range(levels - 1, 0, -1):
        stay[z] = exchanged(stay[z], z * 2 * ROW, "go_stay")
    leave[0] = exchanged(leave[0], ROW, "go_leave")
    early = jnp.concatenate([stay[1], leave[0]], axis=0)
    leave[1:], early, w_gate = lax.optimization_barrier((leave[1:], early, w_gate))
    for z in range(levels - 1, 0, -1):
        leave[z] = exchanged(leave[z], z * 2 * ROW + ROW, "go_leave")
    w_gate = loaded(w_gate)
    late = jnp.concatenate(stay[2:], axis=0)
    most = jnp.concatenate([leave[1], *leave[3:]], axis=0)
    early_far, late_far = over_blk(early, "blk_early"), over_blk(late, "blk_late")
    most_far, last_far = over_blk(most, "blk_most"), over_blk(leave[2], "blk_last")
    cut = (levels - 2) * unit
    stay = [(stay[0], 0, unit), (early, 0, unit), (late, 0, cut)]
    for k in range(blocks - 1):
        stay += [(first[k], 0, unit), (early_far[k], 0, unit), (late_far[k], 0, cut)]
    order = [1, *range(3, levels)]
    places = [order.index(z) if z != 2 else None for z in range(1, levels)]

    def leaving(head, most, last):
        rows = [(head, unit, 2 * unit)]
        return rows + [(last, 0, unit) if p is None else (most, p * unit, (p + 1) * unit) for p in places]

    leave = sum([leaving(*arrays) for arrays in zip([early, *early_far], [most, *most_far], [leave[2], *last_far])], [])

    hidden, w_up = hidden_units(stay, w_gate, w_up, True)
    stay = [hidden] + over_blk(hidden, "hidden_stay")
    hidden, = hidden_units(leave, w_gate, w_up, False)
    stay, hidden, w_down = lax.optimization_barrier((stay, hidden, w_down))
    leave = [hidden] + over_blk(hidden, "hidden_leave")
    stay, w_down = down_slices(stay, half, place, w_down, True)
    stay, leave = lax.optimization_barrier((stay, leave))

    def back(pieces, turn, name):
        received = [pieces[:, z * unit:(z + 1) * unit] for z in range(levels)]
        for z in range(levels - 1, -1, -1):
            mask = z * 2 * ROW + turn
            if mask:
                received[z] = exchanged(received[z], mask, name)
        return jnp.concatenate(received, axis=1)

    def to_owners(slices, name):
        return jnp.stack([slices[0]] + [shifted(slices[k], blocks - k, name) for k in range(1, blocks)])

    def by_blk(output):
        return output.reshape(blocks, half, output.shape[1])

    stay = to_owners(back(by_blk(stay), 0, "back_stay"), "own_stay")
    leave, = down_slices(leave, half, place, w_down, False)
    leave = back(to_owners(by_blk(leave), "own_leave"), ROW, "back_leave")
    returned = [stay, exchanged(stay, CORE, "pair_stay"), leave, exchanged(leave, CORE, "pair_leave")]
    return mixed_rows(weighting, returned, place)


def solution(mesh):
    return jax.shard_map(
        on_device,
        mesh=mesh,
        in_specs=(
            P(("expert", "blk"), None),
            P(("expert", "blk"), None),
            P(("expert", "blk"), None),
            P("expert", None, "blk"),
            P("expert", None, "blk"),
            P("expert", None, "blk"),
        ),
        out_specs=P(("expert", "blk"), None),
        check_vma=False,
    )
```

```python
import functools

import jax
import jax.numpy as jnp
from jax import lax
from jax.experimental import pallas as pl
from jax.experimental.pallas import tpu as pltpu
from jax.sharding import PartitionSpec as P

CAP = 4
CORE, ROW = 1, 2
MIB = 1 << 20
PARTS = 4
ROOM = 13 * MIB


def exchanged(block, mask, name):
    size = lax.axis_size("expert")
    with jax.named_scope(f"{name}_{mask}"):
        return lax.ppermute(block, "expert", [(i, i ^ mask) for i in range(size)])


def shifted(block, steps, name):
    size = lax.axis_size("blk")
    with jax.named_scope(f"{name}_{steps}"):
        return lax.ppermute(block, "blk", [(i, (i + steps) % size) for i in range(size)])


def matmul(left, right):
    return jnp.dot(left, right, preferred_element_type=jnp.float32)


def slots_of(id_rows, labels):
    matches = id_rows[:, :, None] == labels[None, None, :]
    chosen = jnp.any(matches, axis=1)
    counts = chosen.astype(jnp.int32)
    before = jnp.cumsum(counts, axis=0) - counts
    places = jnp.arange(CAP, dtype=jnp.int32)
    return chosen[:, :, None] & (before[:, :, None] == places[None, None, :])


def weights_of(id_rows, gate_rows, labels):
    matches = id_rows[:, :, None] == labels[None, None, :]
    return jnp.sum(jnp.where(matches, gate_rows.astype(jnp.float32)[:, :, None], 0.0), axis=1)


def side_by_side(first, second):
    return jnp.stack([first, second], axis=2).reshape(first.shape[0], -1)


def tile_of(size, most):
    return max(t for t in range(128, most + 1, 128) if size % t == 0)


def parts_of(size, unit):
    return max(p for p in range(1, PARTS + 1) if size % (p * unit) == 0)


def copies_of(source, target, sem, dim):
    count = parts_of(source.shape[dim], 128)
    step = source.shape[dim] // count
    copies = []
    for p in range(count):
        part = (0, pl.ds(p * step, step)) if dim == 1 else (0, slice(None), pl.ds(p * step, step))
        copies.append(pltpu.make_async_copy(source.at[part], target.at[part], sem.at[p]))
    return copies


def load_kernel(source, target, sem):
    copies = copies_of(source, target, sem, 1)
    for copy in copies:
        copy.start()
    for copy in copies:
        copy.wait()


def loaded(weight):
    return pl.pallas_call(
        load_kernel,
        in_specs=[pl.BlockSpec(memory_space=pltpu.HBM)],
        out_specs=pl.BlockSpec(memory_space=pltpu.VMEM),
        out_shape=pltpu.VMEM(weight.shape, weight.dtype),
        scratch_shapes=[pltpu.SemaphoreType.DMA((PARTS,))],
        compiler_params=pltpu.CompilerParams(vmem_limit_bytes=ROOM),
        cost_estimate=pl.CostEstimate(
            flops=0, bytes_accessed=weight.size * weight.dtype.itemsize, transcendentals=0
        ),
    )(pltpu.with_memory_space_constraint(weight, pltpu.HBM))


def in_vmem(weight):
    return pltpu.with_memory_space_constraint(weight, pltpu.VMEM)


def gathered(pieces, ranges, rows_ref):
    rows = [piece[...].astype(jnp.float32)[start:stop] for piece, (start, stop) in zip(pieces, ranges)]
    rows_ref[...] = jnp.concatenate(rows, axis=0).astype(jnp.bfloat16)


def first_hidden_kernel(ranges, *refs):
    count = len(ranges)
    pieces, (gate_ref, up_hbm, out_ref, up_ref, rows_ref, gate_part, sem) = refs[:count], refs[count:]
    copies = copies_of(up_hbm, up_ref, sem, 2)
    for copy in copies:
        copy.start()
    gathered(pieces, ranges, rows_ref)
    tile = out_ref.shape[1] // len(copies)
    parts = [slice(p * tile, (p + 1) * tile) for p in range(len(copies))]
    for columns in parts:
        gate_part[:, columns] = jax.nn.silu(matmul(rows_ref[...], gate_ref[0, :, columns]))
    for columns, copy in zip(parts, copies):
        copy.wait()
        up_part = matmul(rows_ref[...], up_ref[0, :, columns])
        out_ref[:, columns] = (gate_part[:, columns] * up_part).astype(out_ref.dtype)


def hidden_kernel(ranges, *refs):
    count = len(ranges)
    pieces, (gate_ref, up_ref, out_ref, rows_ref) = refs[:count], refs[count:]
    gathered(pieces, ranges, rows_ref)
    tile = tile_of(out_ref.shape[1], 256)

    @pl.loop(0, out_ref.shape[1] // tile)
    def _(n):
        columns = pl.ds(pl.multiple_of(n * tile, tile), tile)
        gate_part = matmul(rows_ref[...], gate_ref[0, :, columns])
        up_part = matmul(rows_ref[...], up_ref[0, :, columns])
        out_ref[:, columns] = (jax.nn.silu(gate_part) * up_part).astype(out_ref.dtype)


def hidden_units(pieces, w_gate, w_up, first):
    depth, units = w_gate.shape[1:]
    ranges = [(start, stop) for _, start, stop in pieces]
    pieces = [piece for piece, _, _ in pieces]
    rows = sum(stop - start for start, stop in ranges)
    vmem = pl.BlockSpec(memory_space=pltpu.VMEM)
    place = pltpu.HBM if first else pltpu.VMEM
    out_shape = [jax.ShapeDtypeStruct((rows, units), jnp.bfloat16)]
    scratch = [pltpu.VMEM((rows, depth), jnp.bfloat16)]
    if first:
        out_shape.append(pltpu.VMEM(w_up.shape, w_up.dtype))
        scratch += [pltpu.VMEM((rows, units), jnp.float32), pltpu.SemaphoreType.DMA((PARTS,))]
    return pl.pallas_call(
        functools.partial(first_hidden_kernel if first else hidden_kernel, ranges),
        in_specs=[vmem] * (len(pieces) + 1) + [pl.BlockSpec(memory_space=place)],
        out_specs=[vmem] * len(out_shape),
        out_shape=out_shape,
        scratch_shapes=scratch,
        compiler_params=pltpu.CompilerParams(vmem_limit_bytes=max(ROOM, 10 * rows * (depth + units) + 2 * MIB)),
        cost_estimate=pl.CostEstimate(
            flops=4 * rows * depth * units,
            bytes_accessed=2 * rows * (depth + units),
            transcendentals=rows * units,
        ),
    )(*pieces, in_vmem(w_gate), pltpu.with_memory_space_constraint(w_up, place))


def down_kernel(half, groups, place, *refs):
    parts, (weight_ref, out_ref) = refs[:-2], refs[-2:]
    size, units = len(parts) // groups, parts[0].shape[1]
    tile = tile_of(out_ref.shape[1], 512)

    @pl.loop(0, out_ref.shape[1] // tile)
    def _(n):
        columns = pl.ds(pl.multiple_of(n * tile, tile), tile)
        total = jnp.zeros((out_ref.shape[0], tile), jnp.float32)
        for k in range(size):
            owner = lax.rem(place[0] + (size - k), size)
            rows = pl.ds(pl.multiple_of(owner * units, units), units)
            left = []
            for part in parts[k::size]:
                left += [part[-k * half:], part[:-k * half]] if k else [part[...]]
            total += matmul(jnp.concatenate(left, axis=0), weight_ref[0, rows, columns])
        out_ref[:, columns] = total.astype(out_ref.dtype)


def down_slices(groups, half, place, w_down):
    units, width = w_down.shape[1:]
    parts = sum(groups, [])
    rows = sum(parts[0].shape[0] for parts in groups)
    vmem = pl.BlockSpec(memory_space=pltpu.VMEM)
    return pl.pallas_call(
        functools.partial(down_kernel, half, len(groups)),
        in_specs=[pl.BlockSpec(memory_space=pltpu.SMEM)] + [vmem] * (len(parts) + 1),
        out_specs=vmem,
        out_shape=jax.ShapeDtypeStruct((rows, width), jnp.bfloat16),
        compiler_params=pltpu.CompilerParams(vmem_limit_bytes=max(ROOM, 8 * rows * (units + width) + 2 * MIB)),
        cost_estimate=pl.CostEstimate(
            flops=2 * rows * units * width,
            bytes_accessed=2 * rows * (units + width),
            transcendentals=0,
        ),
    )(place, *parts, in_vmem(w_down))


def mix_kernel(blocks, *refs):
    place, weights, pieces, out_ref = refs[0], refs[1], refs[2:-1], refs[-1]
    width = out_ref.shape[1] // blocks
    tile = tile_of(width, 512)
    for k in range(blocks):
        start = lax.rem(place[0] + k, blocks) * width
        for n in range(0, width, tile):
            rows = jnp.concatenate([piece[k, :, n:n + tile] for piece in pieces], axis=0)
            columns = pl.ds(pl.multiple_of(start + n, 128), tile)
            out_ref[:, columns] = matmul(weights[...], rows).astype(out_ref.dtype)


def mixed_rows(weights, pieces, place):
    blocks, half, width = pieces[0].shape
    tokens = weights.shape[0]
    return pl.pallas_call(
        functools.partial(mix_kernel, blocks),
        in_specs=[pl.BlockSpec(memory_space=pltpu.SMEM)]
        + [pl.BlockSpec(memory_space=pltpu.VMEM)] * (len(pieces) + 1),
        out_specs=pl.BlockSpec(memory_space=pltpu.VMEM),
        out_shape=jax.ShapeDtypeStruct((tokens, blocks * width), jnp.bfloat16),
        compiler_params=pltpu.CompilerParams(
            vmem_limit_bytes=4 * blocks * width * (len(pieces) * half + tokens) + 2 * MIB
        ),
    )(place, weights, *pieces)


def on_device(tokens, expert_ids, gate_weights, w_gate, w_up, w_down):
    experts, blocks = lax.axis_size("expert"), lax.axis_size("blk")
    me, mine = lax.axis_index("expert"), lax.axis_index("blk")
    levels = experts // 4
    unit = 2 * CAP
    half = levels * unit
    down_mat = w_down[0]

    turns = jnp.arange(2 * levels, dtype=jnp.int32)
    turns = (turns // levels) * ROW + (turns % levels) * (2 * ROW)
    near, far = me ^ turns, me ^ CORE ^ turns

    other_ids = exchanged(expert_ids, CORE, "ids")
    other_tokens = exchanged(tokens, CORE, "tokens")
    own_slots, far_slots = slots_of(expert_ids, near), slots_of(expert_ids, far)
    nothing = jnp.zeros_like(own_slots)
    pick = side_by_side(own_slots, nothing).astype(jnp.bfloat16)
    pick_other = side_by_side(nothing, slots_of(other_ids, near)).astype(jnp.bfloat16)
    chosen = (matmul(pick.T, tokens) + matmul(pick_other.T, other_tokens)).astype(jnp.bfloat16)

    own_weights = jnp.where(own_slots, weights_of(expert_ids, gate_weights, near)[:, :, None], 0.0)
    far_weights = jnp.where(far_slots, weights_of(expert_ids, gate_weights, far)[:, :, None], 0.0)
    zeros = jnp.zeros_like(own_weights)
    own_weights, far_weights = side_by_side(own_weights, zeros), side_by_side(zeros, far_weights)
    weighting = jnp.concatenate(
        [own_weights[:, :half], far_weights[:, :half], own_weights[:, half:], far_weights[:, half:]], axis=1
    )
    weighting = weighting.astype(jnp.bfloat16)
    place = mine.reshape(1).astype(jnp.int32)
    w_gate, weighting, place, _ = lax.optimization_barrier((w_gate, weighting, place, chosen))

    def split(rows):
        return [rows[z * unit:(z + 1) * unit] for z in range(levels)]

    def over_blk(piece, name):
        return [shifted(piece, k, name) for k in range(1, blocks)]

    stay, leave = split(chosen[:half]), split(chosen[half:])
    first = over_blk(stay[0], "blk_first")
    for z in range(levels - 1, 0, -1):
        stay[z] = exchanged(stay[z], z * 2 * ROW, "go_stay")
    leave[0] = exchanged(leave[0], ROW, "go_leave")
    early = jnp.concatenate([stay[1], leave[0]], axis=0)
    early, w_gate = lax.optimization_barrier((early, w_gate))
    w_gate = loaded(w_gate)
    leave[1:], w_gate = lax.optimization_barrier((leave[1:], w_gate))
    for z in range(levels - 1, 0, -1):
        leave[z] = exchanged(leave[z], z * 2 * ROW + ROW, "go_leave")
    late = jnp.concatenate(stay[2:], axis=0)
    most = jnp.concatenate([leave[1], *leave[3:]], axis=0)
    early_far, late_far = over_blk(early, "blk_early"), over_blk(late, "blk_late")
    most_far, last_far = over_blk(most, "blk_most"), over_blk(leave[2], "blk_last")
    cut = (levels - 2) * unit
    stay = [(stay[0], 0, unit), (early, 0, unit), (late, 0, cut)]
    for k in range(blocks - 1):
        stay += [(first[k], 0, unit), (early_far[k], 0, unit), (late_far[k], 0, cut)]
    order = [1, *range(3, levels)]
    places = [order.index(z) if z != 2 else None for z in range(1, levels)]

    def leaving(head, most, last):
        rows = [(head, unit, 2 * unit)]
        return rows + [(last, 0, unit) if p is None else (most, p * unit, (p + 1) * unit) for p in places]

    leave = sum([leaving(*arrays) for arrays in zip([early, *early_far], [most, *most_far], [leave[2], *last_far])], [])

    hidden, w_up = hidden_units(stay, w_gate, w_up, True)
    stay = [hidden] + over_blk(hidden, "hidden_stay")
    hidden, = hidden_units(leave, w_gate, w_up, False)
    stay, hidden, w_down = lax.optimization_barrier((stay, hidden, w_down))
    leave = [hidden] + over_blk(hidden, "hidden_leave")
    output = down_slices([stay, leave], half, place, loaded(w_down))
    stay, leave = output[:blocks * half], output[blocks * half:]

    def back(pieces, turn, name):
        received = [pieces[:, z * unit:(z + 1) * unit] for z in range(levels)]
        for z in range(levels - 1, -1, -1):
            mask = z * 2 * ROW + turn
            if mask:
                received[z] = exchanged(received[z], mask, name)
        return jnp.concatenate(received, axis=1)

    def to_owners(slices, name):
        return jnp.stack([slices[0]] + [shifted(slices[k], blocks - k, name) for k in range(1, blocks)])

    def by_blk(output):
        return output.reshape(blocks, half, output.shape[1])

    stay = to_owners(back(by_blk(stay), 0, "back_stay"), "own_stay")
    leave = back(to_owners(by_blk(leave), "own_leave"), ROW, "back_leave")
    returned = [stay, exchanged(stay, CORE, "pair_stay"), leave, exchanged(leave, CORE, "pair_leave")]
    return mixed_rows(weighting, returned, place)


def solution(mesh):
    return jax.shard_map(
        on_device,
        mesh=mesh,
        in_specs=(
            P(("expert", "blk"), None),
            P(("expert", "blk"), None),
            P(("expert", "blk"), None),
            P("expert", None, "blk"),
            P("expert", None, "blk"),
            P("expert", None, "blk"),
        ),
        out_specs=P(("expert", "blk"), None),
        check_vma=False,
    )
```

```python
import functools

import jax
import jax.numpy as jnp
from jax import lax
from jax.experimental import pallas as pl
from jax.experimental.pallas import tpu as pltpu
from jax.sharding import PartitionSpec as P

CAP = 4
CORE, ROW = 1, 2
MIB = 1 << 20
PARTS = 4
ROOM = 13 * MIB


def exchanged(block, mask, name):
    size = lax.axis_size("expert")
    with jax.named_scope(f"{name}_{mask}"):
        return lax.ppermute(block, "expert", [(i, i ^ mask) for i in range(size)])


def shifted(block, steps, name):
    size = lax.axis_size("blk")
    with jax.named_scope(f"{name}_{steps}"):
        return lax.ppermute(block, "blk", [(i, (i + steps) % size) for i in range(size)])


def matmul(left, right):
    return jnp.dot(left, right, preferred_element_type=jnp.float32)


def tile_of(size, most):
    return max(t for t in range(128, most + 1, 128) if size % t == 0)


def prepare_kernel(levels, place, ids_ref, other_ids_ref, gates_ref, tokens_ref, other_ref, chosen_ref, weights_ref):
    tokens, rows = tokens_ref.shape[0], chosen_ref.shape[0]
    half = rows // 2
    row = lax.broadcasted_iota(jnp.int32, (rows, tokens), 0)
    slot = lax.rem(row, CAP).astype(jnp.float32)
    other_side = lax.rem(row // CAP, 2) == 1
    near = place[0] ^ ((row // half) * ROW + lax.rem(row // (2 * CAP), levels) * (2 * ROW))
    far = near ^ CORE
    earlier = lax.broadcasted_iota(jnp.int32, (tokens, tokens), 0) < lax.broadcasted_iota(jnp.int32, (tokens, tokens), 1)
    earlier = earlier.astype(jnp.float32).astype(jnp.bfloat16)

    def table(ids, labels):
        hits = jnp.zeros((rows, tokens), jnp.float32)
        weights = jnp.zeros((rows, tokens), jnp.float32)
        for j in range(ids.shape[0]):
            match = ids[j:j + 1, :] == labels
            hits = jnp.where(match, 1.0, hits)
            weights = jnp.where(match, gates_ref[j:j + 1, :].astype(jnp.float32), weights)
        before = matmul(hits.astype(jnp.bfloat16), earlier)
        return (hits > 0) & (before == slot), weights

    own, own_weights = table(ids_ref, near)
    other, _ = table(other_ids_ref, near)
    away, away_weights = table(ids_ref, far)
    own_weights = jnp.where(own & ~other_side, own_weights, 0.0)
    away_weights = jnp.where(away & other_side, away_weights, 0.0)
    weights = [own_weights[:half], away_weights[:half], own_weights[half:], away_weights[half:]]
    weights_ref[...] = jnp.concatenate(weights, axis=0).astype(weights_ref.dtype)
    own = jnp.where(own & ~other_side, 1.0, 0.0).astype(jnp.bfloat16)
    other = jnp.where(other & other_side, 1.0, 0.0).astype(jnp.bfloat16)
    tile = tile_of(tokens_ref.shape[1], 1024)
    for n in range(0, tokens_ref.shape[1], tile):
        columns = slice(n, n + tile)
        picked = matmul(own, tokens_ref[:, columns]) + matmul(other, other_ref[:, columns])
        chosen_ref[:, columns] = picked.astype(chosen_ref.dtype)


def prepared(levels, place, ids, other_ids, gates, tokens, other_tokens):
    rows = 4 * levels * CAP
    vmem = pl.BlockSpec(memory_space=pltpu.VMEM)
    return pl.pallas_call(
        functools.partial(prepare_kernel, levels),
        in_specs=[pl.BlockSpec(memory_space=pltpu.SMEM)] + [vmem] * 5,
        out_specs=[vmem, vmem],
        out_shape=[
            jax.ShapeDtypeStruct((rows, tokens.shape[1]), jnp.bfloat16),
            jax.ShapeDtypeStruct((2 * rows, tokens.shape[0]), jnp.bfloat16),
        ],
        compiler_params=pltpu.CompilerParams(vmem_limit_bytes=ROOM),
        cost_estimate=pl.CostEstimate(
            flops=4 * rows * tokens.size, bytes_accessed=4 * (tokens.size + rows * tokens.shape[1]), transcendentals=0
        ),
    )(place, ids, other_ids, gates, tokens, other_tokens)


def parts_of(size, unit):
    return max(p for p in range(1, PARTS + 1) if size % (p * unit) == 0)


def copies_of(source, target, sem, dim):
    count = parts_of(source.shape[dim], 128)
    step = source.shape[dim] // count
    copies = []
    for p in range(count):
        part = (0, pl.ds(p * step, step)) if dim == 1 else (0, slice(None), pl.ds(p * step, step))
        copies.append(pltpu.make_async_copy(source.at[part], target.at[part], sem.at[p]))
    return copies


def load_kernel(source, target, sem):
    copies = copies_of(source, target, sem, 1)
    for copy in copies:
        copy.start()
    for copy in copies:
        copy.wait()


def loaded(weight):
    return pl.pallas_call(
        load_kernel,
        in_specs=[pl.BlockSpec(memory_space=pltpu.HBM)],
        out_specs=pl.BlockSpec(memory_space=pltpu.VMEM),
        out_shape=pltpu.VMEM(weight.shape, weight.dtype),
        scratch_shapes=[pltpu.SemaphoreType.DMA((PARTS,))],
        compiler_params=pltpu.CompilerParams(vmem_limit_bytes=ROOM),
        cost_estimate=pl.CostEstimate(
            flops=0, bytes_accessed=weight.size * weight.dtype.itemsize, transcendentals=0
        ),
    )(pltpu.with_memory_space_constraint(weight, pltpu.HBM))


def in_vmem(weight):
    return pltpu.with_memory_space_constraint(weight, pltpu.VMEM)


def gathered(pieces, ranges, rows_ref):
    rows = [piece[...].astype(jnp.float32)[start:stop] for piece, (start, stop) in zip(pieces, ranges)]
    rows_ref[...] = jnp.concatenate(rows, axis=0).astype(jnp.bfloat16)


def first_hidden_kernel(ranges, *refs):
    count = len(ranges)
    pieces, (gate_ref, up_hbm, out_ref, up_ref, rows_ref, gate_part, sem) = refs[:count], refs[count:]
    copies = copies_of(up_hbm, up_ref, sem, 2)
    for copy in copies:
        copy.start()
    gathered(pieces, ranges, rows_ref)
    tile = out_ref.shape[1] // len(copies)
    parts = [slice(p * tile, (p + 1) * tile) for p in range(len(copies))]
    for columns in parts:
        gate_part[:, columns] = jax.nn.silu(matmul(rows_ref[...], gate_ref[0, :, columns]))
    for columns, copy in zip(parts, copies):
        copy.wait()
        up_part = matmul(rows_ref[...], up_ref[0, :, columns])
        out_ref[:, columns] = (gate_part[:, columns] * up_part).astype(out_ref.dtype)


def hidden_kernel(ranges, *refs):
    count = len(ranges)
    pieces, (gate_ref, up_ref, out_ref, rows_ref) = refs[:count], refs[count:]
    gathered(pieces, ranges, rows_ref)
    tile = tile_of(out_ref.shape[1], 256)

    @pl.loop(0, out_ref.shape[1] // tile)
    def _(n):
        columns = pl.ds(pl.multiple_of(n * tile, tile), tile)
        gate_part = matmul(rows_ref[...], gate_ref[0, :, columns])
        up_part = matmul(rows_ref[...], up_ref[0, :, columns])
        out_ref[:, columns] = (jax.nn.silu(gate_part) * up_part).astype(out_ref.dtype)


def hidden_units(pieces, w_gate, w_up, first):
    depth, units = w_gate.shape[1:]
    ranges = [(start, stop) for _, start, stop in pieces]
    pieces = [piece for piece, _, _ in pieces]
    rows = sum(stop - start for start, stop in ranges)
    vmem = pl.BlockSpec(memory_space=pltpu.VMEM)
    place = pltpu.HBM if first else pltpu.VMEM
    out_shape = [jax.ShapeDtypeStruct((rows, units), jnp.bfloat16)]
    scratch = [pltpu.VMEM((rows, depth), jnp.bfloat16)]
    if first:
        out_shape.append(pltpu.VMEM(w_up.shape, w_up.dtype))
        scratch += [pltpu.VMEM((rows, units), jnp.float32), pltpu.SemaphoreType.DMA((PARTS,))]
    return pl.pallas_call(
        functools.partial(first_hidden_kernel if first else hidden_kernel, ranges),
        in_specs=[vmem] * (len(pieces) + 1) + [pl.BlockSpec(memory_space=place)],
        out_specs=[vmem] * len(out_shape),
        out_shape=out_shape,
        scratch_shapes=scratch,
        compiler_params=pltpu.CompilerParams(vmem_limit_bytes=max(ROOM, 10 * rows * (depth + units) + 2 * MIB)),
        cost_estimate=pl.CostEstimate(
            flops=4 * rows * depth * units,
            bytes_accessed=2 * rows * (depth + units),
            transcendentals=rows * units,
        ),
    )(*pieces, in_vmem(w_gate), pltpu.with_memory_space_constraint(w_up, place))


def down_kernel(half, groups, place, *refs):
    parts, (weight_ref, out_ref) = refs[:-2], refs[-2:]
    size, units = len(parts) // groups, parts[0].shape[1]
    tile = tile_of(out_ref.shape[1], 512)

    @pl.loop(0, out_ref.shape[1] // tile)
    def _(n):
        columns = pl.ds(pl.multiple_of(n * tile, tile), tile)
        total = jnp.zeros((out_ref.shape[0], tile), jnp.float32)
        for k in range(size):
            owner = lax.rem(place[0] + (size - k), size)
            rows = pl.ds(pl.multiple_of(owner * units, units), units)
            left = []
            for part in parts[k::size]:
                left += [part[-k * half:], part[:-k * half]] if k else [part[...]]
            total += matmul(jnp.concatenate(left, axis=0), weight_ref[0, rows, columns])
        out_ref[:, columns] = total.astype(out_ref.dtype)


def down_slices(groups, half, place, w_down):
    units, width = w_down.shape[1:]
    parts = sum(groups, [])
    rows = sum(parts[0].shape[0] for parts in groups)
    vmem = pl.BlockSpec(memory_space=pltpu.VMEM)
    return pl.pallas_call(
        functools.partial(down_kernel, half, len(groups)),
        in_specs=[pl.BlockSpec(memory_space=pltpu.SMEM)] + [vmem] * (len(parts) + 1),
        out_specs=vmem,
        out_shape=jax.ShapeDtypeStruct((rows, width), jnp.bfloat16),
        compiler_params=pltpu.CompilerParams(vmem_limit_bytes=max(ROOM, 8 * rows * (units + width) + 2 * MIB)),
        cost_estimate=pl.CostEstimate(
            flops=2 * rows * units * width,
            bytes_accessed=2 * rows * (units + width),
            transcendentals=0,
        ),
    )(place, *parts, in_vmem(w_down))


def mix_kernel(blocks, *refs):
    place, weights, pieces, out_ref = refs[0], refs[1], refs[2:-1], refs[-1]
    width = out_ref.shape[1] // blocks
    tile = tile_of(width, 512)
    for k in range(blocks):
        start = lax.rem(place[0] + k, blocks) * width
        for n in range(0, width, tile):
            rows = jnp.concatenate([piece[k, :, n:n + tile] for piece in pieces], axis=0)
            columns = pl.ds(pl.multiple_of(start + n, 128), tile)
            total = lax.dot_general(
                weights[...], rows, (((0,), (0,)), ((), ())), preferred_element_type=jnp.float32
            )
            out_ref[:, columns] = total.astype(out_ref.dtype)


def mixed_rows(weights, pieces, place):
    blocks, half, width = pieces[0].shape
    tokens = weights.shape[1]
    return pl.pallas_call(
        functools.partial(mix_kernel, blocks),
        in_specs=[pl.BlockSpec(memory_space=pltpu.SMEM)]
        + [pl.BlockSpec(memory_space=pltpu.VMEM)] * (len(pieces) + 1),
        out_specs=pl.BlockSpec(memory_space=pltpu.VMEM),
        out_shape=jax.ShapeDtypeStruct((tokens, blocks * width), jnp.bfloat16),
        compiler_params=pltpu.CompilerParams(
            vmem_limit_bytes=4 * blocks * width * (len(pieces) * half + tokens) + 2 * MIB
        ),
    )(place, weights, *pieces)


def on_device(tokens, expert_ids, gate_weights, w_gate, w_up, w_down):
    experts, blocks = lax.axis_size("expert"), lax.axis_size("blk")
    me, mine = lax.axis_index("expert"), lax.axis_index("blk")
    levels = experts // 4
    unit = 2 * CAP
    half = levels * unit
    down_mat = w_down[0]

    place = mine.reshape(1).astype(jnp.int32)
    ids = expert_ids.T
    other_ids = exchanged(ids, CORE, "ids")
    other_tokens = exchanged(tokens, CORE, "tokens")
    chosen, weighting = prepared(
        levels, me.reshape(1).astype(jnp.int32), ids, other_ids, gate_weights.T, tokens, other_tokens
    )
    w_gate, place, weighting, chosen = lax.optimization_barrier((w_gate, place, weighting, chosen))

    def split(rows):
        return [rows[z * unit:(z + 1) * unit] for z in range(levels)]

    def over_blk(piece, name):
        return [shifted(piece, k, name) for k in range(1, blocks)]

    stay, leave = split(chosen[:half]), split(chosen[half:])
    first = over_blk(stay[0], "blk_first")
    for z in range(levels - 1, 0, -1):
        stay[z] = exchanged(stay[z], z * 2 * ROW, "go_stay")
    leave[0] = exchanged(leave[0], ROW, "go_leave")
    early = jnp.concatenate([stay[1], leave[0]], axis=0)
    early, w_gate = lax.optimization_barrier((early, w_gate))
    w_gate = loaded(w_gate)
    leave[1:], w_gate = lax.optimization_barrier((leave[1:], w_gate))
    for z in range(levels - 1, 0, -1):
        leave[z] = exchanged(leave[z], z * 2 * ROW + ROW, "go_leave")
    late = jnp.concatenate(stay[2:], axis=0)
    most = jnp.concatenate([leave[1], *leave[3:]], axis=0)
    early_far, late_far = over_blk(early, "blk_early"), over_blk(late, "blk_late")
    most_far, last_far = over_blk(most, "blk_most"), over_blk(leave[2], "blk_last")
    cut = (levels - 2) * unit
    stay = [(stay[0], 0, unit), (early, 0, unit), (late, 0, cut)]
    for k in range(blocks - 1):
        stay += [(first[k], 0, unit), (early_far[k], 0, unit), (late_far[k], 0, cut)]
    order = [1, *range(3, levels)]
    places = [order.index(z) if z != 2 else None for z in range(1, levels)]

    def leaving(head, most, last):
        rows = [(head, unit, 2 * unit)]
        return rows + [(last, 0, unit) if p is None else (most, p * unit, (p + 1) * unit) for p in places]

    leave = sum([leaving(*arrays) for arrays in zip([early, *early_far], [most, *most_far], [leave[2], *last_far])], [])

    hidden, w_up = hidden_units(stay, w_gate, w_up, True)
    stay = [hidden] + over_blk(hidden, "hidden_stay")
    hidden, = hidden_units(leave, w_gate, w_up, False)
    stay, hidden, w_down = lax.optimization_barrier((stay, hidden, w_down))
    leave = [hidden] + over_blk(hidden, "hidden_leave")
    output = down_slices([stay, leave], half, place, loaded(w_down))
    stay, leave = output[:blocks * half], output[blocks * half:]

    def back(pieces, turn, name):
        received = [pieces[:, z * unit:(z + 1) * unit] for z in range(levels)]
        for z in range(levels - 1, -1, -1):
            mask = z * 2 * ROW + turn
            if mask:
                received[z] = exchanged(received[z], mask, name)
        return received

    def to_owners(slices, name):
        return jnp.stack([slices[0]] + [shifted(slices[k], blocks - k, name) for k in range(1, blocks)])

    def by_blk(output):
        return output.reshape(blocks, half, output.shape[1])

    leave = to_owners(by_blk(leave), "own_leave")
    stay = back(by_blk(stay), 0, "back_stay")
    leave = back(leave, ROW, "back_leave")
    stay = jnp.concatenate(stay, axis=1)
    stay, leave[-1] = lax.optimization_barrier((stay, leave[-1]))
    stay = to_owners(stay, "own_stay")
    leave = jnp.concatenate(leave, axis=1)
    returned = [stay, exchanged(stay, CORE, "pair_stay"), leave, exchanged(leave, CORE, "pair_leave")]
    return mixed_rows(weighting, returned, place)


def solution(mesh):
    return jax.shard_map(
        on_device,
        mesh=mesh,
        in_specs=(
            P(("expert", "blk"), None),
            P(("expert", "blk"), None),
            P(("expert", "blk"), None),
            P("expert", None, "blk"),
            P("expert", None, "blk"),
            P("expert", None, "blk"),
        ),
        out_specs=P(("expert", "blk"), None),
        check_vma=False,
    )
```

```python
import functools

import jax
import jax.numpy as jnp
from jax import lax
from jax.experimental import pallas as pl
from jax.experimental.pallas import tpu as pltpu
from jax.sharding import PartitionSpec as P

CAP = 4
CORE, ROW = 1, 2
MIB = 1 << 20
PARTS = 4
ROOM = 13 * MIB


def exchanged(block, mask, name):
    size = lax.axis_size("expert")
    with jax.named_scope(f"{name}_{mask}"):
        return lax.ppermute(block, "expert", [(i, i ^ mask) for i in range(size)])


def shifted(block, steps, name):
    size = lax.axis_size("blk")
    with jax.named_scope(f"{name}_{steps}"):
        return lax.ppermute(block, "blk", [(i, (i + steps) % size) for i in range(size)])


def matmul(left, right):
    return jnp.dot(left, right, preferred_element_type=jnp.float32)


def tile_of(size, most):
    return max(t for t in range(128, most + 1, 128) if size % t == 0)


def prepare_kernel(levels, place, ids_ref, other_ids_ref, gates_ref, tokens_ref, other_ref, chosen_ref, weights_ref):
    tokens, rows = tokens_ref.shape[0], chosen_ref.shape[0]
    half = rows // 2
    row = lax.broadcasted_iota(jnp.int32, (rows, tokens), 0)
    slot = lax.rem(row, CAP).astype(jnp.float32)
    other_side = lax.rem(row // CAP, 2) == 1
    near = place[0] ^ ((row // half) * ROW + lax.rem(row // (2 * CAP), levels) * (2 * ROW))
    far = near ^ CORE
    earlier = lax.broadcasted_iota(jnp.int32, (tokens, tokens), 0) < lax.broadcasted_iota(jnp.int32, (tokens, tokens), 1)
    earlier = earlier.astype(jnp.float32).astype(jnp.bfloat16)

    def table(ids, labels):
        hits = jnp.zeros((rows, tokens), jnp.float32)
        weights = jnp.zeros((rows, tokens), jnp.float32)
        for j in range(ids.shape[0]):
            match = ids[j:j + 1, :] == labels
            hits = jnp.where(match, 1.0, hits)
            weights = jnp.where(match, gates_ref[j:j + 1, :].astype(jnp.float32), weights)
        before = matmul(hits.astype(jnp.bfloat16), earlier)
        return (hits > 0) & (before == slot), weights

    own, own_weights = table(ids_ref, near)
    other, _ = table(other_ids_ref, near)
    away, away_weights = table(ids_ref, far)
    own_weights = jnp.where(own & ~other_side, own_weights, 0.0)
    away_weights = jnp.where(away & other_side, away_weights, 0.0)
    weights = [own_weights[:half], away_weights[:half], own_weights[half:], away_weights[half:]]
    weights_ref[...] = jnp.concatenate(weights, axis=0).astype(weights_ref.dtype)
    own = jnp.where(own & ~other_side, 1.0, 0.0).astype(jnp.bfloat16)
    other = jnp.where(other & other_side, 1.0, 0.0).astype(jnp.bfloat16)
    tile = tile_of(tokens_ref.shape[1], 1024)
    for n in range(0, tokens_ref.shape[1], tile):
        columns = slice(n, n + tile)
        picked = matmul(own, tokens_ref[:, columns]) + matmul(other, other_ref[:, columns])
        chosen_ref[:, columns] = picked.astype(chosen_ref.dtype)


def prepared(levels, place, ids, other_ids, gates, tokens, other_tokens):
    rows = 4 * levels * CAP
    vmem = pl.BlockSpec(memory_space=pltpu.VMEM)
    return pl.pallas_call(
        functools.partial(prepare_kernel, levels),
        in_specs=[pl.BlockSpec(memory_space=pltpu.SMEM)] + [vmem] * 5,
        out_specs=[vmem, vmem],
        out_shape=[
            jax.ShapeDtypeStruct((rows, tokens.shape[1]), jnp.bfloat16),
            jax.ShapeDtypeStruct((2 * rows, tokens.shape[0]), jnp.bfloat16),
        ],
        compiler_params=pltpu.CompilerParams(vmem_limit_bytes=ROOM),
        cost_estimate=pl.CostEstimate(
            flops=4 * rows * tokens.size, bytes_accessed=4 * (tokens.size + rows * tokens.shape[1]), transcendentals=0
        ),
    )(place, ids, other_ids, gates, tokens, other_tokens)


def parts_of(size, unit):
    return max(p for p in range(1, PARTS + 1) if size % (p * unit) == 0)


def copies_of(source, target, sem, dim):
    count = parts_of(source.shape[dim], 128)
    step = source.shape[dim] // count
    copies = []
    for p in range(count):
        part = (0, pl.ds(p * step, step)) if dim == 1 else (0, slice(None), pl.ds(p * step, step))
        copies.append(pltpu.make_async_copy(source.at[part], target.at[part], sem.at[p]))
    return copies


def load_kernel(count, *refs):
    sources, targets, sem = refs[:count], refs[count:-1], refs[-1]
    copies = []
    for number, (source, target) in enumerate(zip(sources, targets)):
        if len(source.shape) == 2:
            copies.append(pltpu.make_async_copy(source, target, sem.at[number, 0]))
        else:
            copies += copies_of(source, target, sem.at[number], 1)
    for copy in copies:
        copy.start()
    for copy in copies:
        copy.wait()


def loaded(*arrays):
    count = len(arrays)
    return pl.pallas_call(
        functools.partial(load_kernel, count),
        in_specs=[pl.BlockSpec(memory_space=pltpu.HBM)] * count,
        out_specs=[pl.BlockSpec(memory_space=pltpu.VMEM)] * count,
        out_shape=[pltpu.VMEM(array.shape, array.dtype) for array in arrays],
        scratch_shapes=[pltpu.SemaphoreType.DMA((count, PARTS))],
        compiler_params=pltpu.CompilerParams(vmem_limit_bytes=ROOM),
        cost_estimate=pl.CostEstimate(
            flops=0, bytes_accessed=sum(a.size * a.dtype.itemsize for a in arrays), transcendentals=0
        ),
    )(*[pltpu.with_memory_space_constraint(array, pltpu.HBM) for array in arrays])


def in_vmem(weight):
    return pltpu.with_memory_space_constraint(weight, pltpu.VMEM)


def gathered(pieces, ranges, rows_ref):
    rows = [piece[...].astype(jnp.float32)[start:stop] for piece, (start, stop) in zip(pieces, ranges)]
    rows_ref[...] = jnp.concatenate(rows, axis=0).astype(jnp.bfloat16)


def first_hidden_kernel(ranges, *refs):
    count = len(ranges)
    pieces, (gate_ref, up_hbm, out_ref, up_ref, rows_ref, gate_part, sem) = refs[:count], refs[count:]
    copies = copies_of(up_hbm, up_ref, sem, 2)
    for copy in copies:
        copy.start()
    gathered(pieces, ranges, rows_ref)
    tile = out_ref.shape[1] // len(copies)
    parts = [slice(p * tile, (p + 1) * tile) for p in range(len(copies))]
    for columns in parts:
        gate_part[:, columns] = jax.nn.silu(matmul(rows_ref[...], gate_ref[0, :, columns]))
    for columns, copy in zip(parts, copies):
        copy.wait()
        up_part = matmul(rows_ref[...], up_ref[0, :, columns])
        out_ref[:, columns] = (gate_part[:, columns] * up_part).astype(out_ref.dtype)


def hidden_kernel(ranges, *refs):
    count = len(ranges)
    pieces, (gate_ref, up_ref, out_ref, rows_ref) = refs[:count], refs[count:]
    gathered(pieces, ranges, rows_ref)
    tile = tile_of(out_ref.shape[1], 256)

    @pl.loop(0, out_ref.shape[1] // tile)
    def _(n):
        columns = pl.ds(pl.multiple_of(n * tile, tile), tile)
        gate_part = matmul(rows_ref[...], gate_ref[0, :, columns])
        up_part = matmul(rows_ref[...], up_ref[0, :, columns])
        out_ref[:, columns] = (jax.nn.silu(gate_part) * up_part).astype(out_ref.dtype)


def hidden_units(pieces, w_gate, w_up, first):
    depth, units = w_gate.shape[1:]
    ranges = [(start, stop) for _, start, stop in pieces]
    pieces = [piece for piece, _, _ in pieces]
    rows = sum(stop - start for start, stop in ranges)
    vmem = pl.BlockSpec(memory_space=pltpu.VMEM)
    place = pltpu.HBM if first else pltpu.VMEM
    out_shape = [jax.ShapeDtypeStruct((rows, units), jnp.bfloat16)]
    scratch = [pltpu.VMEM((rows, depth), jnp.bfloat16)]
    if first:
        out_shape.append(pltpu.VMEM(w_up.shape, w_up.dtype))
        scratch += [pltpu.VMEM((rows, units), jnp.float32), pltpu.SemaphoreType.DMA((PARTS,))]
    return pl.pallas_call(
        functools.partial(first_hidden_kernel if first else hidden_kernel, ranges),
        in_specs=[vmem] * (len(pieces) + 1) + [pl.BlockSpec(memory_space=place)],
        out_specs=[vmem] * len(out_shape),
        out_shape=out_shape,
        scratch_shapes=scratch,
        compiler_params=pltpu.CompilerParams(vmem_limit_bytes=max(ROOM, 10 * rows * (depth + units) + 2 * MIB)),
        cost_estimate=pl.CostEstimate(
            flops=4 * rows * depth * units,
            bytes_accessed=2 * rows * (depth + units),
            transcendentals=rows * units,
        ),
    )(*pieces, in_vmem(w_gate), pltpu.with_memory_space_constraint(w_up, place))


def down_kernel(half, groups, place, *refs):
    parts, (weight_ref, out_ref) = refs[:-2], refs[-2:]
    size, units = len(parts) // groups, parts[0].shape[1]
    tile = tile_of(out_ref.shape[1], 512)

    @pl.loop(0, out_ref.shape[1] // tile)
    def _(n):
        columns = pl.ds(pl.multiple_of(n * tile, tile), tile)
        total = jnp.zeros((out_ref.shape[0], tile), jnp.float32)
        for k in range(size):
            owner = lax.rem(place[0] + (size - k), size)
            rows = pl.ds(pl.multiple_of(owner * units, units), units)
            left = []
            for part in parts[k::size]:
                left += [part[-k * half:], part[:-k * half]] if k else [part[...]]
            total += matmul(jnp.concatenate(left, axis=0), weight_ref[0, rows, columns])
        out_ref[:, columns] = total.astype(out_ref.dtype)


def down_slices(groups, half, place, w_down):
    units, width = w_down.shape[1:]
    parts = sum(groups, [])
    rows = sum(parts[0].shape[0] for parts in groups)
    vmem = pl.BlockSpec(memory_space=pltpu.VMEM)
    return pl.pallas_call(
        functools.partial(down_kernel, half, len(groups)),
        in_specs=[pl.BlockSpec(memory_space=pltpu.SMEM)] + [vmem] * (len(parts) + 1),
        out_specs=vmem,
        out_shape=jax.ShapeDtypeStruct((rows, width), jnp.bfloat16),
        compiler_params=pltpu.CompilerParams(vmem_limit_bytes=max(ROOM, 8 * rows * (units + width) + 2 * MIB)),
        cost_estimate=pl.CostEstimate(
            flops=2 * rows * units * width,
            bytes_accessed=2 * rows * (units + width),
            transcendentals=0,
        ),
    )(place, *parts, in_vmem(w_down))


def mix_kernel(blocks, *refs):
    place, weights, pieces, out_ref = refs[0], refs[1], refs[2:-1], refs[-1]
    width = out_ref.shape[1] // blocks
    tile = tile_of(width, 512)
    for k in range(blocks):
        start = lax.rem(place[0] + k, blocks) * width
        for n in range(0, width, tile):
            rows = jnp.concatenate([piece[k, :, n:n + tile] for piece in pieces], axis=0)
            columns = pl.ds(pl.multiple_of(start + n, 128), tile)
            total = lax.dot_general(
                weights[...], rows, (((0,), (0,)), ((), ())), preferred_element_type=jnp.float32
            )
            out_ref[:, columns] = total.astype(out_ref.dtype)


def mixed_rows(weights, pieces, place):
    blocks, half, width = pieces[0].shape
    tokens = weights.shape[1]
    return pl.pallas_call(
        functools.partial(mix_kernel, blocks),
        in_specs=[pl.BlockSpec(memory_space=pltpu.SMEM)]
        + [pl.BlockSpec(memory_space=pltpu.VMEM)] * (len(pieces) + 1),
        out_specs=pl.BlockSpec(memory_space=pltpu.VMEM),
        out_shape=jax.ShapeDtypeStruct((tokens, blocks * width), jnp.bfloat16),
        compiler_params=pltpu.CompilerParams(
            vmem_limit_bytes=4 * blocks * width * (len(pieces) * half + tokens) + 2 * MIB
        ),
    )(place, weights, *pieces)


def on_device(tokens, expert_ids, gate_weights, w_gate, w_up, w_down):
    experts, blocks = lax.axis_size("expert"), lax.axis_size("blk")
    me, mine = lax.axis_index("expert"), lax.axis_index("blk")
    levels = experts // 4
    unit = 2 * CAP
    half = levels * unit
    down_mat = w_down[0]

    place = mine.reshape(1).astype(jnp.int32)
    ids = expert_ids.T
    other_ids = exchanged(ids, CORE, "ids")
    other_tokens = exchanged(tokens, CORE, "tokens")
    near_ids, near_gates, near_tokens = loaded(ids, gate_weights.T, tokens)
    chosen, weighting = prepared(
        levels, me.reshape(1).astype(jnp.int32), near_ids, other_ids, near_gates, near_tokens, other_tokens
    )
    w_gate, place, weighting, chosen = lax.optimization_barrier((w_gate, place, weighting, chosen))

    def split(rows):
        return [rows[z * unit:(z + 1) * unit] for z in range(levels)]

    def over_blk(piece, name):
        return [shifted(piece, k, name) for k in range(1, blocks)]

    stay, leave = split(chosen[:half]), split(chosen[half:])
    for z in range(levels - 1, 0, -1):
        stay[z] = exchanged(stay[z], z * 2 * ROW, "go_stay")
    leave[0] = exchanged(leave[0], ROW, "go_leave")
    early = jnp.concatenate([stay[0], stay[1], leave[0]], axis=0)
    late = jnp.concatenate(stay[2:], axis=0)
    early, leave[1:] = lax.optimization_barrier((early, leave[1:]))
    early_far, late_far = over_blk(early, "blk_early"), over_blk(late, "blk_late")
    early_far, leave[2] = lax.optimization_barrier((early_far, leave[2]))
    for z in range(levels - 1, 0, -1):
        leave[z] = exchanged(leave[z], z * 2 * ROW + ROW, "go_leave")
    late, w_gate = lax.optimization_barrier((late, w_gate))
    w_gate, = loaded(w_gate)
    order = [*range(levels - 1, 1, -1)]
    most = jnp.concatenate([leave[z] for z in order], axis=0)
    most, w_gate = lax.optimization_barrier((most, w_gate))
    most_far, last_far = over_blk(most, "blk_most"), over_blk(leave[1], "blk_last")
    cut = (levels - 2) * unit
    stay = sum([[(a, 0, 2 * unit), (b, 0, cut)] for a, b in zip([early, *early_far], [late, *late_far])], [])
    places = [order.index(z) if z != 1 else None for z in range(1, levels)]

    def leaving(head, most, last):
        rows = [(head, 2 * unit, 3 * unit)]
        return rows + [(last, 0, unit) if p is None else (most, p * unit, (p + 1) * unit) for p in places]

    leave = sum([leaving(*arrays) for arrays in zip([early, *early_far], [most, *most_far], [leave[1], *last_far])], [])

    hidden, w_up = hidden_units(stay, w_gate, w_up, True)
    stay = [hidden] + over_blk(hidden, "hidden_stay")
    hidden, = hidden_units(leave, w_gate, w_up, False)
    stay, hidden, w_down = lax.optimization_barrier((stay, hidden, w_down))
    leave = [hidden] + over_blk(hidden, "hidden_leave")
    output = down_slices([stay, leave], half, place, loaded(w_down)[0])
    stay, leave = output[:blocks * half], output[blocks * half:]

    def back(pieces, turn, name):
        received = [pieces[:, z * unit:(z + 1) * unit] for z in range(levels)]
        for z in range(levels - 1, -1, -1):
            mask = z * 2 * ROW + turn
            if mask:
                received[z] = exchanged(received[z], mask, name)
        return received

    def to_owners(slices, name):
        return jnp.stack([slices[0]] + [shifted(slices[k], blocks - k, name) for k in range(1, blocks)])

    def by_blk(output):
        return output.reshape(blocks, half, output.shape[1])

    leave = to_owners(by_blk(leave), "own_leave")
    stay = back(by_blk(stay), 0, "back_stay")
    leave = back(leave, ROW, "back_leave")
    stay = jnp.concatenate(stay, axis=1)
    stay, leave[0] = lax.optimization_barrier((stay, leave[0]))
    stay = to_owners(stay, "own_stay")
    leave = jnp.concatenate(leave, axis=1)
    returned = [stay, exchanged(stay, CORE, "pair_stay"), leave, exchanged(leave, CORE, "pair_leave")]
    return mixed_rows(weighting, returned, place)


def solution(mesh):
    return jax.shard_map(
        on_device,
        mesh=mesh,
        in_specs=(
            P(("expert", "blk"), None),
            P(("expert", "blk"), None),
            P(("expert", "blk"), None),
            P("expert", None, "blk"),
            P("expert", None, "blk"),
            P("expert", None, "blk"),
        ),
        out_specs=P(("expert", "blk"), None),
        check_vma=False,
    )
```

```python
import functools

import jax
import jax.numpy as jnp
from jax import lax
from jax.experimental import pallas as pl
from jax.experimental.pallas import tpu as pltpu
from jax.sharding import PartitionSpec as P

CAP = 4
CORE, ROW = 1, 2
MIB = 1 << 20
PARTS = 4
ROOM = 13 * MIB


def exchanged(block, mask, name):
    size = lax.axis_size("expert")
    with jax.named_scope(f"{name}_{mask}"):
        return lax.ppermute(block, "expert", [(i, i ^ mask) for i in range(size)])


def shifted(block, steps, name):
    size = lax.axis_size("blk")
    with jax.named_scope(f"{name}_{steps}"):
        return lax.ppermute(block, "blk", [(i, (i + steps) % size) for i in range(size)])


def matmul(left, right):
    return jnp.dot(left, right, preferred_element_type=jnp.float32)


def tile_of(size, most):
    return max(t for t in range(128, most + 1, 128) if size % t == 0)


def prepare_kernel(levels, place, ids_ref, other_ids_ref, gates_ref, tokens_ref, other_ref, chosen_ref, weights_ref):
    tokens, rows = tokens_ref.shape[0], chosen_ref.shape[0]
    half = rows // 2
    row = lax.broadcasted_iota(jnp.int32, (rows, tokens), 0)
    slot = lax.rem(row, CAP).astype(jnp.float32)
    other_side = lax.rem(row // CAP, 2) == 1
    near = place[0] ^ ((row // half) * ROW + lax.rem(row // (2 * CAP), levels) * (2 * ROW))
    far = near ^ CORE
    earlier = lax.broadcasted_iota(jnp.int32, (tokens, tokens), 0) < lax.broadcasted_iota(jnp.int32, (tokens, tokens), 1)
    earlier = earlier.astype(jnp.float32).astype(jnp.bfloat16)

    def table(ids, labels):
        hits = jnp.zeros((rows, tokens), jnp.float32)
        weights = jnp.zeros((rows, tokens), jnp.float32)
        for j in range(ids.shape[0]):
            match = ids[j:j + 1, :] == labels
            hits = jnp.where(match, 1.0, hits)
            weights = jnp.where(match, gates_ref[j:j + 1, :].astype(jnp.float32), weights)
        before = matmul(hits.astype(jnp.bfloat16), earlier)
        return (hits > 0) & (before == slot), weights

    own, own_weights = table(ids_ref, near)
    other, _ = table(other_ids_ref, near)
    away, away_weights = table(ids_ref, far)
    own_weights = jnp.where(own & ~other_side, own_weights, 0.0)
    away_weights = jnp.where(away & other_side, away_weights, 0.0)
    weights = [own_weights[:half], away_weights[:half], own_weights[half:], away_weights[half:]]
    weights_ref[...] = jnp.concatenate(weights, axis=0).astype(weights_ref.dtype)
    own = jnp.where(own & ~other_side, 1.0, 0.0).astype(jnp.bfloat16)
    other = jnp.where(other & other_side, 1.0, 0.0).astype(jnp.bfloat16)
    tile = tile_of(tokens_ref.shape[1], 1024)
    for n in range(0, tokens_ref.shape[1], tile):
        columns = slice(n, n + tile)
        picked = matmul(own, tokens_ref[:, columns]) + matmul(other, other_ref[:, columns])
        chosen_ref[:, columns] = picked.astype(chosen_ref.dtype)


def prepared(levels, place, ids, other_ids, gates, tokens, other_tokens):
    rows = 4 * levels * CAP
    vmem = pl.BlockSpec(memory_space=pltpu.VMEM)
    return pl.pallas_call(
        functools.partial(prepare_kernel, levels),
        in_specs=[pl.BlockSpec(memory_space=pltpu.SMEM)] + [vmem] * 5,
        out_specs=[vmem, vmem],
        out_shape=[
            jax.ShapeDtypeStruct((rows, tokens.shape[1]), jnp.bfloat16),
            jax.ShapeDtypeStruct((2 * rows, tokens.shape[0]), jnp.bfloat16),
        ],
        compiler_params=pltpu.CompilerParams(vmem_limit_bytes=ROOM),
        cost_estimate=pl.CostEstimate(
            flops=4 * rows * tokens.size, bytes_accessed=4 * (tokens.size + rows * tokens.shape[1]), transcendentals=0
        ),
    )(place, ids, other_ids, gates, tokens, other_tokens)


def parts_of(size, unit):
    return max(p for p in range(1, PARTS + 1) if size % (p * unit) == 0)


def copies_of(source, target, sem, dim):
    count = parts_of(source.shape[dim], 128)
    step = source.shape[dim] // count
    copies = []
    for p in range(count):
        part = (0, pl.ds(p * step, step)) if dim == 1 else (0, slice(None), pl.ds(p * step, step))
        copies.append(pltpu.make_async_copy(source.at[part], target.at[part], sem.at[p]))
    return copies


def load_kernel(count, *refs):
    sources, targets, sem = refs[:count], refs[count:-1], refs[-1]
    copies = []
    for number, (source, target) in enumerate(zip(sources, targets)):
        if len(source.shape) == 2:
            copies.append(pltpu.make_async_copy(source, target, sem.at[number, 0]))
        else:
            copies += copies_of(source, target, sem.at[number], 1)
    for copy in copies:
        copy.start()
    for copy in copies:
        copy.wait()


def loaded(*arrays):
    count = len(arrays)
    return pl.pallas_call(
        functools.partial(load_kernel, count),
        in_specs=[pl.BlockSpec(memory_space=pltpu.HBM)] * count,
        out_specs=[pl.BlockSpec(memory_space=pltpu.VMEM)] * count,
        out_shape=[pltpu.VMEM(array.shape, array.dtype) for array in arrays],
        scratch_shapes=[pltpu.SemaphoreType.DMA((count, PARTS))],
        compiler_params=pltpu.CompilerParams(vmem_limit_bytes=ROOM),
        cost_estimate=pl.CostEstimate(
            flops=0, bytes_accessed=sum(a.size * a.dtype.itemsize for a in arrays), transcendentals=0
        ),
    )(*[pltpu.with_memory_space_constraint(array, pltpu.HBM) for array in arrays])


def in_vmem(weight):
    return pltpu.with_memory_space_constraint(weight, pltpu.VMEM)


def gathered(pieces, ranges, rows_ref):
    rows = [piece[...].astype(jnp.float32)[start:stop] for piece, (start, stop) in zip(pieces, ranges)]
    rows_ref[...] = jnp.concatenate(rows, axis=0).astype(jnp.bfloat16)


def first_hidden_kernel(ranges, *refs):
    count = len(ranges)
    pieces, (gate_ref, up_hbm, out_ref, up_ref, rows_ref, gate_part, sem) = refs[:count], refs[count:]
    copies = copies_of(up_hbm, up_ref, sem, 2)
    for copy in copies:
        copy.start()
    gathered(pieces, ranges, rows_ref)
    tile = out_ref.shape[1] // len(copies)
    parts = [slice(p * tile, (p + 1) * tile) for p in range(len(copies))]
    for columns in parts:
        gate_part[:, columns] = jax.nn.silu(matmul(rows_ref[...], gate_ref[0, :, columns]))
    for columns, copy in zip(parts, copies):
        copy.wait()
        up_part = matmul(rows_ref[...], up_ref[0, :, columns])
        out_ref[:, columns] = (gate_part[:, columns] * up_part).astype(out_ref.dtype)


def hidden_kernel(ranges, *refs):
    count = len(ranges)
    pieces, (gate_ref, up_ref, out_ref, rows_ref) = refs[:count], refs[count:]
    gathered(pieces, ranges, rows_ref)
    tile = tile_of(out_ref.shape[1], 256)

    @pl.loop(0, out_ref.shape[1] // tile)
    def _(n):
        columns = pl.ds(pl.multiple_of(n * tile, tile), tile)
        gate_part = matmul(rows_ref[...], gate_ref[0, :, columns])
        up_part = matmul(rows_ref[...], up_ref[0, :, columns])
        out_ref[:, columns] = (jax.nn.silu(gate_part) * up_part).astype(out_ref.dtype)


def hidden_units(pieces, w_gate, w_up, first):
    depth, units = w_gate.shape[1:]
    ranges = [(start, stop) for _, start, stop in pieces]
    pieces = [piece for piece, _, _ in pieces]
    rows = sum(stop - start for start, stop in ranges)
    vmem = pl.BlockSpec(memory_space=pltpu.VMEM)
    place = pltpu.HBM if first else pltpu.VMEM
    out_shape = [jax.ShapeDtypeStruct((rows, units), jnp.bfloat16)]
    scratch = [pltpu.VMEM((rows, depth), jnp.bfloat16)]
    if first:
        out_shape.append(pltpu.VMEM(w_up.shape, w_up.dtype))
        scratch += [pltpu.VMEM((rows, units), jnp.float32), pltpu.SemaphoreType.DMA((PARTS,))]
    return pl.pallas_call(
        functools.partial(first_hidden_kernel if first else hidden_kernel, ranges),
        in_specs=[vmem] * (len(pieces) + 1) + [pl.BlockSpec(memory_space=place)],
        out_specs=[vmem] * len(out_shape),
        out_shape=out_shape,
        scratch_shapes=scratch,
        compiler_params=pltpu.CompilerParams(vmem_limit_bytes=max(ROOM, 10 * rows * (depth + units) + 2 * MIB)),
        cost_estimate=pl.CostEstimate(
            flops=4 * rows * depth * units,
            bytes_accessed=2 * rows * (depth + units),
            transcendentals=rows * units,
        ),
    )(*pieces, in_vmem(w_gate), pltpu.with_memory_space_constraint(w_up, place))


def down_kernel(half, groups, place, *refs):
    parts, (weight_ref, out_ref) = refs[:-2], refs[-2:]
    size, units = len(parts) // groups, parts[0].shape[1]
    tile = tile_of(out_ref.shape[1], 512)

    @pl.loop(0, out_ref.shape[1] // tile)
    def _(n):
        columns = pl.ds(pl.multiple_of(n * tile, tile), tile)
        total = jnp.zeros((out_ref.shape[0], tile), jnp.float32)
        for k in range(size):
            owner = lax.rem(place[0] + (size - k), size)
            rows = pl.ds(pl.multiple_of(owner * units, units), units)
            left = []
            for part in parts[k::size]:
                left += [part[-k * half:], part[:-k * half]] if k else [part[...]]
            total += matmul(jnp.concatenate(left, axis=0), weight_ref[0, rows, columns])
        out_ref[:, columns] = total.astype(out_ref.dtype)


def down_slices(groups, half, place, w_down):
    units, width = w_down.shape[1:]
    parts = sum(groups, [])
    rows = sum(parts[0].shape[0] for parts in groups)
    vmem = pl.BlockSpec(memory_space=pltpu.VMEM)
    return pl.pallas_call(
        functools.partial(down_kernel, half, len(groups)),
        in_specs=[pl.BlockSpec(memory_space=pltpu.SMEM)] + [vmem] * (len(parts) + 1),
        out_specs=vmem,
        out_shape=jax.ShapeDtypeStruct((rows, width), jnp.bfloat16),
        compiler_params=pltpu.CompilerParams(vmem_limit_bytes=max(ROOM, 8 * rows * (units + width) + 2 * MIB)),
        cost_estimate=pl.CostEstimate(
            flops=2 * rows * units * width,
            bytes_accessed=2 * rows * (units + width),
            transcendentals=0,
        ),
    )(place, *parts, in_vmem(w_down))


def mix_kernel(blocks, *refs):
    place, weights, pieces, out_ref = refs[0], refs[1], refs[2:-1], refs[-1]
    width = out_ref.shape[1] // blocks
    tile = tile_of(width, 512)
    for k in range(blocks):
        start = lax.rem(place[0] + k, blocks) * width
        for n in range(0, width, tile):
            rows = jnp.concatenate([piece[k, :, n:n + tile] for piece in pieces], axis=0)
            columns = pl.ds(pl.multiple_of(start + n, 128), tile)
            total = lax.dot_general(
                weights[...], rows, (((0,), (0,)), ((), ())), preferred_element_type=jnp.float32
            )
            out_ref[:, columns] = total.astype(out_ref.dtype)


def mixed_rows(weights, pieces, place):
    blocks, half, width = pieces[0].shape
    tokens = weights.shape[1]
    return pl.pallas_call(
        functools.partial(mix_kernel, blocks),
        in_specs=[pl.BlockSpec(memory_space=pltpu.SMEM)]
        + [pl.BlockSpec(memory_space=pltpu.VMEM)] * (len(pieces) + 1),
        out_specs=pl.BlockSpec(memory_space=pltpu.VMEM),
        out_shape=jax.ShapeDtypeStruct((tokens, blocks * width), jnp.bfloat16),
        compiler_params=pltpu.CompilerParams(
            vmem_limit_bytes=4 * blocks * width * (len(pieces) * half + tokens) + 2 * MIB
        ),
    )(place, weights, *pieces)


def on_device(tokens, expert_ids, gate_weights, w_gate, w_up, w_down):
    experts, blocks = lax.axis_size("expert"), lax.axis_size("blk")
    me, mine = lax.axis_index("expert"), lax.axis_index("blk")
    levels = experts // 4
    unit = 2 * CAP
    half = levels * unit
    down_mat = w_down[0]

    place = mine.reshape(1).astype(jnp.int32)
    ids = expert_ids.T
    other_ids = exchanged(ids, CORE, "ids")
    other_tokens = exchanged(tokens, CORE, "tokens")
    near_ids, near_gates, near_tokens = loaded(ids, gate_weights.T, tokens)
    chosen, weighting = prepared(
        levels, me.reshape(1).astype(jnp.int32), near_ids, other_ids, near_gates, near_tokens, other_tokens
    )
    w_gate, place, weighting, chosen = lax.optimization_barrier((w_gate, place, weighting, chosen))

    def split(rows):
        return [rows[z * unit:(z + 1) * unit] for z in range(levels)]

    def over_blk(piece, name):
        return [shifted(piece, k, name) for k in range(1, blocks)]

    stay, leave = split(chosen[:half]), split(chosen[half:])
    for z in range(levels - 1, 0, -1):
        stay[z] = exchanged(stay[z], z * 2 * ROW, "go_stay")
    leave[0] = exchanged(leave[0], ROW, "go_leave")
    early = jnp.concatenate([stay[0], stay[1], leave[0]], axis=0)
    late = jnp.concatenate(stay[2:], axis=0)
    early, leave[1:] = lax.optimization_barrier((early, leave[1:]))
    early_far, late_far = over_blk(early, "blk_early"), over_blk(late, "blk_late")
    for z in [1, *range(levels - 1, 2, -1)]:
        leave[z] = exchanged(leave[z], z * 2 * ROW + ROW, "go_leave")
    early_far, leave[1], leave[2] = lax.optimization_barrier((early_far, leave[1], leave[2]))
    leave[2] = exchanged(leave[2], 2 * 2 * ROW + ROW, "go_leave")
    late, w_gate = lax.optimization_barrier((late, w_gate))
    w_gate, = loaded(w_gate)
    order = [*range(levels - 1, 1, -1)]
    most = jnp.concatenate([leave[z] for z in order], axis=0)
    most, w_gate = lax.optimization_barrier((most, w_gate))
    most_far, last_far = over_blk(most, "blk_most"), over_blk(leave[1], "blk_last")
    cut = (levels - 2) * unit
    stay = sum([[(a, 0, 2 * unit), (b, 0, cut)] for a, b in zip([early, *early_far], [late, *late_far])], [])
    places = [order.index(z) if z != 1 else None for z in range(1, levels)]

    def leaving(head, most, last):
        rows = [(head, 2 * unit, 3 * unit)]
        return rows + [(last, 0, unit) if p is None else (most, p * unit, (p + 1) * unit) for p in places]

    leave = sum([leaving(*arrays) for arrays in zip([early, *early_far], [most, *most_far], [leave[1], *last_far])], [])

    hidden, w_up = hidden_units(stay, w_gate, w_up, True)
    stay = [hidden] + over_blk(hidden, "hidden_stay")
    hidden, = hidden_units(leave, w_gate, w_up, False)
    stay, hidden, w_down = lax.optimization_barrier((stay, hidden, w_down))
    leave = [hidden] + over_blk(hidden, "hidden_leave")
    output = down_slices([stay, leave], half, place, loaded(w_down)[0])
    stay, leave = output[:blocks * half], output[blocks * half:]

    def back(pieces, turn, name):
        received = [pieces[:, z * unit:(z + 1) * unit] for z in range(levels)]
        for z in range(levels - 1, -1, -1):
            mask = z * 2 * ROW + turn
            if mask:
                received[z] = exchanged(received[z], mask, name)
        return received

    def to_owners(slices, name):
        return jnp.stack([slices[0]] + [shifted(slices[k], blocks - k, name) for k in range(1, blocks)])

    def by_blk(output):
        return output.reshape(blocks, half, output.shape[1])

    leave = to_owners(by_blk(leave), "own_leave")
    stay = back(by_blk(stay), 0, "back_stay")
    leave = back(leave, ROW, "back_leave")
    stay = jnp.concatenate(stay, axis=1)
    stay = to_owners(stay, "own_stay")
    leave = jnp.concatenate(leave, axis=1)
    returned = [stay, exchanged(stay, CORE, "pair_stay"), leave, exchanged(leave, CORE, "pair_leave")]
    return mixed_rows(weighting, returned, place)


def solution(mesh):
    return jax.shard_map(
        on_device,
        mesh=mesh,
        in_specs=(
            P(("expert", "blk"), None),
            P(("expert", "blk"), None),
            P(("expert", "blk"), None),
            P("expert", None, "blk"),
            P("expert", None, "blk"),
            P("expert", None, "blk"),
        ),
        out_specs=P(("expert", "blk"), None),
        check_vma=False,
    )
```

```python
import functools

import jax
import jax.numpy as jnp
from jax import lax
from jax.experimental import pallas as pl
from jax.experimental.pallas import tpu as pltpu
from jax.sharding import PartitionSpec as P

CAP = 4
CORE, ROW = 1, 2
MIB = 1 << 20
PARTS = 4
ROOM = 13 * MIB


def exchanged(block, mask, name):
    size = lax.axis_size("expert")
    with jax.named_scope(f"{name}_{mask}"):
        return lax.ppermute(block, "expert", [(i, i ^ mask) for i in range(size)])


def shifted(block, steps, name):
    size = lax.axis_size("blk")
    with jax.named_scope(f"{name}_{steps}"):
        return lax.ppermute(block, "blk", [(i, (i + steps) % size) for i in range(size)])


def matmul(left, right):
    return jnp.dot(left, right, preferred_element_type=jnp.float32)


def tile_of(size, most):
    return max(t for t in range(128, most + 1, 128) if size % t == 0)


def prepare_kernel(levels, place, ids_ref, other_ids_ref, gates_ref, tokens_ref, other_ref, chosen_ref, weights_ref):
    tokens, rows = tokens_ref.shape[0], chosen_ref.shape[0]
    half = rows // 2
    row = lax.broadcasted_iota(jnp.int32, (rows, tokens), 0)
    slot = lax.rem(row, CAP).astype(jnp.float32)
    other_side = lax.rem(row // CAP, 2) == 1
    near = place[0] ^ ((row // half) * ROW + lax.rem(row // (2 * CAP), levels) * (2 * ROW))
    far = near ^ CORE
    earlier = lax.broadcasted_iota(jnp.int32, (tokens, tokens), 0) < lax.broadcasted_iota(jnp.int32, (tokens, tokens), 1)
    earlier = earlier.astype(jnp.float32).astype(jnp.bfloat16)

    def table(ids, labels):
        hits = jnp.zeros((rows, tokens), jnp.float32)
        weights = jnp.zeros((rows, tokens), jnp.float32)
        for j in range(ids.shape[0]):
            match = ids[j:j + 1, :] == labels
            hits = jnp.where(match, 1.0, hits)
            weights = jnp.where(match, gates_ref[j:j + 1, :].astype(jnp.float32), weights)
        before = matmul(hits.astype(jnp.bfloat16), earlier)
        return (hits > 0) & (before == slot), weights

    own, own_weights = table(ids_ref, near)
    other, _ = table(other_ids_ref, near)
    away, away_weights = table(ids_ref, far)
    own_weights = jnp.where(own & ~other_side, own_weights, 0.0)
    away_weights = jnp.where(away & other_side, away_weights, 0.0)
    weights = [own_weights[:half], away_weights[:half], own_weights[half:], away_weights[half:]]
    weights_ref[...] = jnp.concatenate(weights, axis=0).astype(weights_ref.dtype)
    own = jnp.where(own & ~other_side, 1.0, 0.0).astype(jnp.bfloat16)
    other = jnp.where(other & other_side, 1.0, 0.0).astype(jnp.bfloat16)
    tile = tile_of(tokens_ref.shape[1], 1024)
    for n in range(0, tokens_ref.shape[1], tile):
        columns = slice(n, n + tile)
        picked = matmul(own, tokens_ref[:, columns]) + matmul(other, other_ref[:, columns])
        chosen_ref[:, columns] = picked.astype(chosen_ref.dtype)


def prepared(levels, place, ids, other_ids, gates, tokens, other_tokens):
    rows = 4 * levels * CAP
    vmem = pl.BlockSpec(memory_space=pltpu.VMEM)
    return pl.pallas_call(
        functools.partial(prepare_kernel, levels),
        in_specs=[pl.BlockSpec(memory_space=pltpu.SMEM)] + [vmem] * 5,
        out_specs=[vmem, vmem],
        out_shape=[
            jax.ShapeDtypeStruct((rows, tokens.shape[1]), jnp.bfloat16),
            jax.ShapeDtypeStruct((2 * rows, tokens.shape[0]), jnp.bfloat16),
        ],
        compiler_params=pltpu.CompilerParams(vmem_limit_bytes=ROOM),
        cost_estimate=pl.CostEstimate(
            flops=4 * rows * tokens.size, bytes_accessed=4 * (tokens.size + rows * tokens.shape[1]), transcendentals=0
        ),
    )(place, ids, other_ids, gates, tokens, other_tokens)


def parts_of(size, unit):
    return max(p for p in range(1, PARTS + 1) if size % (p * unit) == 0)


def copies_of(source, target, sem, dim):
    count = parts_of(source.shape[dim], 128)
    step = source.shape[dim] // count
    copies = []
    for p in range(count):
        part = (0, pl.ds(p * step, step)) if dim == 1 else (0, slice(None), pl.ds(p * step, step))
        copies.append(pltpu.make_async_copy(source.at[part], target.at[part], sem.at[p]))
    return copies


def load_kernel(count, *refs):
    sources, targets, sem = refs[:count], refs[count:-1], refs[-1]
    copies = []
    for number, (source, target) in enumerate(zip(sources, targets)):
        if len(source.shape) == 2:
            copies.append(pltpu.make_async_copy(source, target, sem.at[number, 0]))
        else:
            copies += copies_of(source, target, sem.at[number], 1)
    for copy in copies:
        copy.start()
    for copy in copies:
        copy.wait()


def loaded(*arrays):
    count = len(arrays)
    return pl.pallas_call(
        functools.partial(load_kernel, count),
        in_specs=[pl.BlockSpec(memory_space=pltpu.HBM)] * count,
        out_specs=[pl.BlockSpec(memory_space=pltpu.VMEM)] * count,
        out_shape=[pltpu.VMEM(array.shape, array.dtype) for array in arrays],
        scratch_shapes=[pltpu.SemaphoreType.DMA((count, PARTS))],
        compiler_params=pltpu.CompilerParams(vmem_limit_bytes=ROOM),
        cost_estimate=pl.CostEstimate(
            flops=0, bytes_accessed=sum(a.size * a.dtype.itemsize for a in arrays), transcendentals=0
        ),
    )(*[pltpu.with_memory_space_constraint(array, pltpu.HBM) for array in arrays])


def in_vmem(weight):
    return pltpu.with_memory_space_constraint(weight, pltpu.VMEM)


def gathered(pieces, ranges, rows_ref):
    rows = [piece[...].astype(jnp.float32)[start:stop] for piece, (start, stop) in zip(pieces, ranges)]
    rows_ref[...] = jnp.concatenate(rows, axis=0).astype(jnp.bfloat16)


def first_hidden_kernel(ranges, *refs):
    count = len(ranges)
    pieces, (gate_ref, up_hbm, out_ref, up_ref, rows_ref, gate_part, sem) = refs[:count], refs[count:]
    copies = copies_of(up_hbm, up_ref, sem, 2)
    for copy in copies:
        copy.start()
    gathered(pieces, ranges, rows_ref)
    tile = out_ref.shape[1] // len(copies)
    parts = [slice(p * tile, (p + 1) * tile) for p in range(len(copies))]
    for columns in parts:
        gate_part[:, columns] = jax.nn.silu(matmul(rows_ref[...], gate_ref[0, :, columns]))
    for columns, copy in zip(parts, copies):
        copy.wait()
        up_part = matmul(rows_ref[...], up_ref[0, :, columns])
        out_ref[:, columns] = (gate_part[:, columns] * up_part).astype(out_ref.dtype)


def hidden_kernel(ranges, *refs):
    count = len(ranges)
    pieces, (gate_ref, up_ref, out_ref, rows_ref) = refs[:count], refs[count:]
    gathered(pieces, ranges, rows_ref)
    tile = tile_of(out_ref.shape[1], 256)

    @pl.loop(0, out_ref.shape[1] // tile)
    def _(n):
        columns = pl.ds(pl.multiple_of(n * tile, tile), tile)
        gate_part = matmul(rows_ref[...], gate_ref[0, :, columns])
        up_part = matmul(rows_ref[...], up_ref[0, :, columns])
        out_ref[:, columns] = (jax.nn.silu(gate_part) * up_part).astype(out_ref.dtype)


def hidden_units(pieces, w_gate, w_up, first):
    depth, units = w_gate.shape[1:]
    ranges = [(start, stop) for _, start, stop in pieces]
    pieces = [piece for piece, _, _ in pieces]
    rows = sum(stop - start for start, stop in ranges)
    vmem = pl.BlockSpec(memory_space=pltpu.VMEM)
    place = pltpu.HBM if first else pltpu.VMEM
    out_shape = [jax.ShapeDtypeStruct((rows, units), jnp.bfloat16)]
    scratch = [pltpu.VMEM((rows, depth), jnp.bfloat16)]
    if first:
        out_shape.append(pltpu.VMEM(w_up.shape, w_up.dtype))
        scratch += [pltpu.VMEM((rows, units), jnp.float32), pltpu.SemaphoreType.DMA((PARTS,))]
    return pl.pallas_call(
        functools.partial(first_hidden_kernel if first else hidden_kernel, ranges),
        in_specs=[vmem] * (len(pieces) + 1) + [pl.BlockSpec(memory_space=place)],
        out_specs=[vmem] * len(out_shape),
        out_shape=out_shape,
        scratch_shapes=scratch,
        compiler_params=pltpu.CompilerParams(vmem_limit_bytes=max(ROOM, 10 * rows * (depth + units) + 2 * MIB)),
        cost_estimate=pl.CostEstimate(
            flops=4 * rows * depth * units,
            bytes_accessed=2 * rows * (depth + units),
            transcendentals=rows * units,
        ),
    )(*pieces, in_vmem(w_gate), pltpu.with_memory_space_constraint(w_up, place))


def down_kernel(half, groups, place, *refs):
    parts, (weight_ref, out_ref) = refs[:-2], refs[-2:]
    size, units = len(parts) // groups, parts[0].shape[1]
    tile = tile_of(out_ref.shape[1], 512)

    @pl.loop(0, out_ref.shape[1] // tile)
    def _(n):
        columns = pl.ds(pl.multiple_of(n * tile, tile), tile)
        total = jnp.zeros((out_ref.shape[0], tile), jnp.float32)
        for k in range(size):
            owner = lax.rem(place[0] + (size - k), size)
            rows = pl.ds(pl.multiple_of(owner * units, units), units)
            left = []
            for part in parts[k::size]:
                left += [part[-k * half:], part[:-k * half]] if k else [part[...]]
            total += matmul(jnp.concatenate(left, axis=0), weight_ref[0, rows, columns])
        out_ref[:, columns] = total.astype(out_ref.dtype)


def down_slices(groups, half, place, w_down):
    units, width = w_down.shape[1:]
    parts = sum(groups, [])
    rows = sum(parts[0].shape[0] for parts in groups)
    vmem = pl.BlockSpec(memory_space=pltpu.VMEM)
    return pl.pallas_call(
        functools.partial(down_kernel, half, len(groups)),
        in_specs=[pl.BlockSpec(memory_space=pltpu.SMEM)] + [vmem] * (len(parts) + 1),
        out_specs=vmem,
        out_shape=jax.ShapeDtypeStruct((rows, width), jnp.bfloat16),
        compiler_params=pltpu.CompilerParams(vmem_limit_bytes=max(ROOM, 8 * rows * (units + width) + 2 * MIB)),
        cost_estimate=pl.CostEstimate(
            flops=2 * rows * units * width,
            bytes_accessed=2 * rows * (units + width),
            transcendentals=0,
        ),
    )(place, *parts, in_vmem(w_down))


def mix_kernel(blocks, *refs):
    place, weights, pieces, out_ref = refs[0], refs[1], refs[2:-1], refs[-1]
    width = out_ref.shape[1] // blocks
    tile = tile_of(width, 512)
    for k in range(blocks):
        start = lax.rem(place[0] + k, blocks) * width
        for n in range(0, width, tile):
            rows = jnp.concatenate([piece[k, :, n:n + tile] for piece in pieces], axis=0)
            columns = pl.ds(pl.multiple_of(start + n, 128), tile)
            total = lax.dot_general(
                weights[...], rows, (((0,), (0,)), ((), ())), preferred_element_type=jnp.float32
            )
            out_ref[:, columns] = total.astype(out_ref.dtype)


def mixed_rows(weights, pieces, place):
    blocks, half, width = pieces[0].shape
    tokens = weights.shape[1]
    return pl.pallas_call(
        functools.partial(mix_kernel, blocks),
        in_specs=[pl.BlockSpec(memory_space=pltpu.SMEM)]
        + [pl.BlockSpec(memory_space=pltpu.VMEM)] * (len(pieces) + 1),
        out_specs=pl.BlockSpec(memory_space=pltpu.VMEM),
        out_shape=jax.ShapeDtypeStruct((tokens, blocks * width), jnp.bfloat16),
        compiler_params=pltpu.CompilerParams(
            vmem_limit_bytes=4 * blocks * width * (len(pieces) * half + tokens) + 2 * MIB
        ),
    )(place, weights, *pieces)


def on_device(tokens, expert_ids, gate_weights, w_gate, w_up, w_down):
    experts, blocks = lax.axis_size("expert"), lax.axis_size("blk")
    me, mine = lax.axis_index("expert"), lax.axis_index("blk")
    levels = experts // 4
    unit = 2 * CAP
    half = levels * unit
    down_mat = w_down[0]

    place = mine.reshape(1).astype(jnp.int32)
    ids = expert_ids.T
    other_ids = exchanged(ids, CORE, "ids")
    other_tokens = exchanged(tokens, CORE, "tokens")
    near_ids, near_gates, near_tokens = loaded(ids, gate_weights.T, tokens)
    chosen, weighting = prepared(
        levels, me.reshape(1).astype(jnp.int32), near_ids, other_ids, near_gates, near_tokens, other_tokens
    )
    w_gate, place, weighting, chosen = lax.optimization_barrier((w_gate, place, weighting, chosen))

    def split(rows):
        return [rows[z * unit:(z + 1) * unit] for z in range(levels)]

    def over_blk(piece, name):
        return [shifted(piece, k, name) for k in range(1, blocks)]

    stay, leave = split(chosen[:half]), split(chosen[half:])
    for z in range(levels - 1, 0, -1):
        stay[z] = exchanged(stay[z], z * 2 * ROW, "go_stay")
    leave[0] = exchanged(leave[0], ROW, "go_leave")
    early = jnp.concatenate([stay[0], stay[1], leave[0]], axis=0)
    late = jnp.concatenate(stay[2:], axis=0)
    early, leave[1:] = lax.optimization_barrier((early, leave[1:]))
    early_far, late_far = over_blk(early, "blk_early"), over_blk(late, "blk_late")
    for z in [1, *range(levels - 1, 2, -1)]:
        leave[z] = exchanged(leave[z], z * 2 * ROW + ROW, "go_leave")
    early_far, leave[1], leave[2] = lax.optimization_barrier((early_far, leave[1], leave[2]))
    leave[2] = exchanged(leave[2], 2 * 2 * ROW + ROW, "go_leave")
    late, w_gate = lax.optimization_barrier((late, w_gate))
    w_gate, = loaded(w_gate)
    order = [*range(levels - 1, 1, -1)]
    most = jnp.concatenate([leave[z] for z in order], axis=0)
    most, w_gate = lax.optimization_barrier((most, w_gate))
    most_far, last_far = over_blk(most, "blk_most"), over_blk(leave[1], "blk_last")
    cut = (levels - 2) * unit
    stay = sum([[(a, 0, 2 * unit), (b, 0, cut)] for a, b in zip([early, *early_far], [late, *late_far])], [])
    places = [order.index(z) if z != 1 else None for z in range(1, levels)]

    def leaving(head, most, last):
        rows = [(head, 2 * unit, 3 * unit)]
        return rows + [(last, 0, unit) if p is None else (most, p * unit, (p + 1) * unit) for p in places]

    leave = sum([leaving(*arrays) for arrays in zip([early, *early_far], [most, *most_far], [leave[1], *last_far])], [])

    hidden, w_up = hidden_units(stay, w_gate, w_up, True)
    stay = [hidden] + over_blk(hidden, "hidden_stay")
    hidden, = hidden_units(leave, w_gate, w_up, False)
    stay, hidden, w_down = lax.optimization_barrier((stay, hidden, w_down))
    leave = [hidden] + over_blk(hidden, "hidden_leave")
    output = down_slices([stay, leave], half, place, loaded(w_down)[0])
    stay, leave = output[:blocks * half], output[blocks * half:]

    def back(pieces, turn, name):
        received = [pieces[:, z * unit:(z + 1) * unit] for z in range(levels)]
        for z in range(levels - 1, -1, -1):
            mask = z * 2 * ROW + turn
            if mask:
                received[z] = exchanged(received[z], mask, name)
        return received

    def to_owners(slices, name):
        return jnp.stack([slices[0]] + [shifted(slices[k], blocks - k, name) for k in range(1, blocks)])

    def by_blk(output):
        return output.reshape(blocks, half, output.shape[1])

    stay = to_owners(by_blk(stay), "own_stay")
    leave = back(by_blk(leave), ROW, "back_leave")
    stay = [stay[:, z * unit:(z + 1) * unit] for z in range(levels)]
    leave[0], stay[2] = lax.optimization_barrier((leave[0], stay[2]))
    leave[1], stay[-1] = lax.optimization_barrier((leave[1], stay[-1]))
    for z in range(levels - 1, 0, -1):
        stay[z] = exchanged(stay[z], z * 2 * ROW, "back_stay")
    leave = jnp.concatenate(leave, axis=1)
    leave = to_owners(leave, "own_leave")
    stay = jnp.concatenate(stay, axis=1)
    returned = [stay, exchanged(stay, CORE, "pair_stay"), leave, exchanged(leave, CORE, "pair_leave")]
    return mixed_rows(weighting, returned, place)


def solution(mesh):
    return jax.shard_map(
        on_device,
        mesh=mesh,
        in_specs=(
            P(("expert", "blk"), None),
            P(("expert", "blk"), None),
            P(("expert", "blk"), None),
            P("expert", None, "blk"),
            P("expert", None, "blk"),
            P("expert", None, "blk"),
        ),
        out_specs=P(("expert", "blk"), None),
        check_vma=False,
    )
```

```python
import functools

import jax
import jax.numpy as jnp
from jax import lax
from jax.experimental import pallas as pl
from jax.experimental.pallas import tpu as pltpu
from jax.sharding import PartitionSpec as P

CAP = 4
CORE, ROW = 1, 2
MIB = 1 << 20
PARTS = 4
ROOM = 13 * MIB


def exchanged(block, mask, name):
    size = lax.axis_size("expert")
    with jax.named_scope(f"{name}_{mask}"):
        return lax.ppermute(block, "expert", [(i, i ^ mask) for i in range(size)])


def shifted(block, steps, name):
    size = lax.axis_size("blk")
    with jax.named_scope(f"{name}_{steps}"):
        return lax.ppermute(block, "blk", [(i, (i + steps) % size) for i in range(size)])


def matmul(left, right):
    return jnp.dot(left, right, preferred_element_type=jnp.float32)


def tile_of(size, most):
    return max(t for t in range(128, most + 1, 128) if size % t == 0)


def prepare_kernel(levels, place, ids_ref, other_ids_ref, gates_ref, tokens_ref, other_ref, chosen_ref, weights_ref):
    tokens, rows = tokens_ref.shape[0], chosen_ref.shape[0]
    half = rows // 2
    row = lax.broadcasted_iota(jnp.int32, (rows, tokens), 0)
    slot = lax.rem(row, CAP).astype(jnp.float32)
    other_side = lax.rem(row // CAP, 2) == 1
    near = place[0] ^ ((row // half) * ROW + lax.rem(row // (2 * CAP), levels) * (2 * ROW))
    far = near ^ CORE
    earlier = lax.broadcasted_iota(jnp.int32, (tokens, tokens), 0) < lax.broadcasted_iota(jnp.int32, (tokens, tokens), 1)
    earlier = earlier.astype(jnp.float32).astype(jnp.bfloat16)

    def table(ids, labels):
        hits = jnp.zeros((rows, tokens), jnp.float32)
        weights = jnp.zeros((rows, tokens), jnp.float32)
        for j in range(ids.shape[0]):
            match = ids[j:j + 1, :] == labels
            hits = jnp.where(match, 1.0, hits)
            weights = jnp.where(match, gates_ref[j:j + 1, :].astype(jnp.float32), weights)
        before = matmul(hits.astype(jnp.bfloat16), earlier)
        return (hits > 0) & (before == slot), weights

    own, own_weights = table(ids_ref, near)
    other, _ = table(other_ids_ref, near)
    away, away_weights = table(ids_ref, far)
    own_weights = jnp.where(own & ~other_side, own_weights, 0.0)
    away_weights = jnp.where(away & other_side, away_weights, 0.0)
    weights = [own_weights[:half], away_weights[:half], own_weights[half:], away_weights[half:]]
    weights_ref[...] = jnp.concatenate(weights, axis=0).astype(weights_ref.dtype)
    own = jnp.where(own & ~other_side, 1.0, 0.0).astype(jnp.bfloat16)
    other = jnp.where(other & other_side, 1.0, 0.0).astype(jnp.bfloat16)
    tile = tile_of(tokens_ref.shape[1], 1024)
    for n in range(0, tokens_ref.shape[1], tile):
        columns = slice(n, n + tile)
        picked = matmul(own, tokens_ref[:, columns]) + matmul(other, other_ref[:, columns])
        chosen_ref[:, columns] = picked.astype(chosen_ref.dtype)


def prepared(levels, place, ids, other_ids, gates, tokens, other_tokens):
    rows = 4 * levels * CAP
    vmem = pl.BlockSpec(memory_space=pltpu.VMEM)
    return pl.pallas_call(
        functools.partial(prepare_kernel, levels),
        in_specs=[pl.BlockSpec(memory_space=pltpu.SMEM)] + [vmem] * 5,
        out_specs=[vmem, vmem],
        out_shape=[
            jax.ShapeDtypeStruct((rows, tokens.shape[1]), jnp.bfloat16),
            jax.ShapeDtypeStruct((2 * rows, tokens.shape[0]), jnp.bfloat16),
        ],
        compiler_params=pltpu.CompilerParams(vmem_limit_bytes=ROOM),
        cost_estimate=pl.CostEstimate(
            flops=4 * rows * tokens.size, bytes_accessed=4 * (tokens.size + rows * tokens.shape[1]), transcendentals=0
        ),
    )(place, ids, other_ids, gates, tokens, other_tokens)


def parts_of(size, unit):
    return max(p for p in range(1, PARTS + 1) if size % (p * unit) == 0)


def copies_of(source, target, sem, dim):
    count = parts_of(source.shape[dim], 128)
    step = source.shape[dim] // count
    copies = []
    for p in range(count):
        part = (0, pl.ds(p * step, step)) if dim == 1 else (0, slice(None), pl.ds(p * step, step))
        copies.append(pltpu.make_async_copy(source.at[part], target.at[part], sem.at[p]))
    return copies


def load_kernel(count, *refs):
    sources, targets, sem = refs[:count], refs[count:-1], refs[-1]
    copies = []
    for number, (source, target) in enumerate(zip(sources, targets)):
        if len(source.shape) == 2:
            copies.append(pltpu.make_async_copy(source, target, sem.at[number, 0]))
        else:
            copies += copies_of(source, target, sem.at[number], 1)
    for copy in copies:
        copy.start()
    for copy in copies:
        copy.wait()


def loaded(*arrays):
    count = len(arrays)
    return pl.pallas_call(
        functools.partial(load_kernel, count),
        in_specs=[pl.BlockSpec(memory_space=pltpu.HBM)] * count,
        out_specs=[pl.BlockSpec(memory_space=pltpu.VMEM)] * count,
        out_shape=[pltpu.VMEM(array.shape, array.dtype) for array in arrays],
        scratch_shapes=[pltpu.SemaphoreType.DMA((count, PARTS))],
        compiler_params=pltpu.CompilerParams(vmem_limit_bytes=ROOM),
        cost_estimate=pl.CostEstimate(
            flops=0, bytes_accessed=sum(a.size * a.dtype.itemsize for a in arrays), transcendentals=0
        ),
    )(*[pltpu.with_memory_space_constraint(array, pltpu.HBM) for array in arrays])


def in_vmem(weight):
    return pltpu.with_memory_space_constraint(weight, pltpu.VMEM)


def gathered(pieces, ranges, rows_ref):
    rows = [piece[...].astype(jnp.float32)[start:stop] for piece, (start, stop) in zip(pieces, ranges)]
    rows_ref[...] = jnp.concatenate(rows, axis=0).astype(jnp.bfloat16)


def first_hidden_kernel(ranges, *refs):
    count = len(ranges)
    pieces, (gate_ref, up_hbm, out_ref, up_ref, rows_ref, gate_part, sem) = refs[:count], refs[count:]
    copies = copies_of(up_hbm, up_ref, sem, 2)
    for copy in copies:
        copy.start()
    gathered(pieces, ranges, rows_ref)
    tile = out_ref.shape[1] // len(copies)
    parts = [slice(p * tile, (p + 1) * tile) for p in range(len(copies))]
    for columns in parts:
        gate_part[:, columns] = jax.nn.silu(matmul(rows_ref[...], gate_ref[0, :, columns]))
    for columns, copy in zip(parts, copies):
        copy.wait()
        up_part = matmul(rows_ref[...], up_ref[0, :, columns])
        out_ref[:, columns] = (gate_part[:, columns] * up_part).astype(out_ref.dtype)


def hidden_kernel(ranges, *refs):
    count = len(ranges)
    pieces, (gate_ref, up_ref, out_ref, rows_ref) = refs[:count], refs[count:]
    gathered(pieces, ranges, rows_ref)
    tile = tile_of(out_ref.shape[1], 256)

    @pl.loop(0, out_ref.shape[1] // tile)
    def _(n):
        columns = pl.ds(pl.multiple_of(n * tile, tile), tile)
        gate_part = matmul(rows_ref[...], gate_ref[0, :, columns])
        up_part = matmul(rows_ref[...], up_ref[0, :, columns])
        out_ref[:, columns] = (jax.nn.silu(gate_part) * up_part).astype(out_ref.dtype)


def hidden_units(pieces, w_gate, w_up, first):
    depth, units = w_gate.shape[1:]
    ranges = [(start, stop) for _, start, stop in pieces]
    pieces = [piece for piece, _, _ in pieces]
    rows = sum(stop - start for start, stop in ranges)
    vmem = pl.BlockSpec(memory_space=pltpu.VMEM)
    place = pltpu.HBM if first else pltpu.VMEM
    out_shape = [jax.ShapeDtypeStruct((rows, units), jnp.bfloat16)]
    scratch = [pltpu.VMEM((rows, depth), jnp.bfloat16)]
    if first:
        out_shape.append(pltpu.VMEM(w_up.shape, w_up.dtype))
        scratch += [pltpu.VMEM((rows, units), jnp.float32), pltpu.SemaphoreType.DMA((PARTS,))]
    return pl.pallas_call(
        functools.partial(first_hidden_kernel if first else hidden_kernel, ranges),
        in_specs=[vmem] * (len(pieces) + 1) + [pl.BlockSpec(memory_space=place)],
        out_specs=[vmem] * len(out_shape),
        out_shape=out_shape,
        scratch_shapes=scratch,
        compiler_params=pltpu.CompilerParams(vmem_limit_bytes=max(ROOM, 10 * rows * (depth + units) + 2 * MIB)),
        cost_estimate=pl.CostEstimate(
            flops=4 * rows * depth * units,
            bytes_accessed=2 * rows * (depth + units),
            transcendentals=rows * units,
        ),
    )(*pieces, in_vmem(w_gate), pltpu.with_memory_space_constraint(w_up, place))


def down_kernel(half, groups, place, *refs):
    parts, (weight_ref, out_ref) = refs[:-2], refs[-2:]
    size, units = len(parts) // groups, parts[0].shape[1]
    tile = tile_of(out_ref.shape[1], 512)

    @pl.loop(0, out_ref.shape[1] // tile)
    def _(n):
        columns = pl.ds(pl.multiple_of(n * tile, tile), tile)
        total = jnp.zeros((out_ref.shape[0], tile), jnp.float32)
        for k in range(size):
            owner = lax.rem(place[0] + (size - k), size)
            rows = pl.ds(pl.multiple_of(owner * units, units), units)
            left = []
            for part in parts[k::size]:
                left += [part[-k * half:], part[:-k * half]] if k else [part[...]]
            total += matmul(jnp.concatenate(left, axis=0), weight_ref[0, rows, columns])
        out_ref[:, columns] = total.astype(out_ref.dtype)


def down_slices(groups, half, place, w_down):
    units, width = w_down.shape[1:]
    parts = sum(groups, [])
    rows = sum(parts[0].shape[0] for parts in groups)
    vmem = pl.BlockSpec(memory_space=pltpu.VMEM)
    return pl.pallas_call(
        functools.partial(down_kernel, half, len(groups)),
        in_specs=[pl.BlockSpec(memory_space=pltpu.SMEM)] + [vmem] * (len(parts) + 1),
        out_specs=vmem,
        out_shape=jax.ShapeDtypeStruct((rows, width), jnp.bfloat16),
        compiler_params=pltpu.CompilerParams(vmem_limit_bytes=max(ROOM, 8 * rows * (units + width) + 2 * MIB)),
        cost_estimate=pl.CostEstimate(
            flops=2 * rows * units * width,
            bytes_accessed=2 * rows * (units + width),
            transcendentals=0,
        ),
    )(place, *parts, in_vmem(w_down))


def mix_kernel(blocks, *refs):
    place, weights, pieces, out_ref = refs[0], refs[1], refs[2:-1], refs[-1]
    width = out_ref.shape[1] // blocks
    tile = tile_of(width, 512)
    for k in range(blocks):
        start = lax.rem(place[0] + k, blocks) * width
        for n in range(0, width, tile):
            rows = jnp.concatenate([piece[k, :, n:n + tile] for piece in pieces], axis=0)
            columns = pl.ds(pl.multiple_of(start + n, 128), tile)
            total = lax.dot_general(
                weights[...], rows, (((0,), (0,)), ((), ())), preferred_element_type=jnp.float32
            )
            out_ref[:, columns] = total.astype(out_ref.dtype)


def mixed_rows(weights, pieces, place):
    blocks, half, width = pieces[0].shape
    tokens = weights.shape[1]
    return pl.pallas_call(
        functools.partial(mix_kernel, blocks),
        in_specs=[pl.BlockSpec(memory_space=pltpu.SMEM)]
        + [pl.BlockSpec(memory_space=pltpu.VMEM)] * (len(pieces) + 1),
        out_specs=pl.BlockSpec(memory_space=pltpu.VMEM),
        out_shape=jax.ShapeDtypeStruct((tokens, blocks * width), jnp.bfloat16),
        compiler_params=pltpu.CompilerParams(
            vmem_limit_bytes=4 * blocks * width * (len(pieces) * half + tokens) + 2 * MIB
        ),
    )(place, weights, *pieces)


def on_device(tokens, expert_ids, gate_weights, w_gate, w_up, w_down):
    experts, blocks = lax.axis_size("expert"), lax.axis_size("blk")
    me, mine = lax.axis_index("expert"), lax.axis_index("blk")
    levels = experts // 4
    unit = 2 * CAP
    half = levels * unit
    down_mat = w_down[0]

    place = mine.reshape(1).astype(jnp.int32)
    ids = expert_ids.T
    other_ids = exchanged(ids, CORE, "ids")
    other_tokens = exchanged(tokens, CORE, "tokens")
    near_ids, near_gates, near_tokens = loaded(ids, gate_weights.T, tokens)
    chosen, weighting = prepared(
        levels, me.reshape(1).astype(jnp.int32), near_ids, other_ids, near_gates, near_tokens, other_tokens
    )
    w_gate, place, weighting, chosen = lax.optimization_barrier((w_gate, place, weighting, chosen))

    def split(rows):
        return [rows[z * unit:(z + 1) * unit] for z in range(levels)]

    def over_blk(piece, name):
        return [shifted(piece, k, name) for k in range(1, blocks)]

    stay, leave = split(chosen[:half]), split(chosen[half:])
    for z in range(levels - 1, 0, -1):
        stay[z] = exchanged(stay[z], z * 2 * ROW, "go_stay")
    leave[0] = exchanged(leave[0], ROW, "go_leave")
    early = jnp.concatenate([stay[0], stay[1], leave[0]], axis=0)
    late = jnp.concatenate(stay[2:], axis=0)
    early, leave[1:] = lax.optimization_barrier((early, leave[1:]))
    early_far, late_far = over_blk(early, "blk_early"), over_blk(late, "blk_late")
    for z in [1, *range(levels - 1, 2, -1)]:
        leave[z] = exchanged(leave[z], z * 2 * ROW + ROW, "go_leave")
    early_far, leave[1], leave[2] = lax.optimization_barrier((early_far, leave[1], leave[2]))
    leave[2] = exchanged(leave[2], 2 * 2 * ROW + ROW, "go_leave")
    late, w_gate = lax.optimization_barrier((late, w_gate))
    w_gate, = loaded(w_gate)
    order = [*range(levels - 1, 1, -1)]
    most = jnp.concatenate([leave[z] for z in order], axis=0)
    most, w_gate = lax.optimization_barrier((most, w_gate))
    most_far, last_far = over_blk(most, "blk_most"), over_blk(leave[1], "blk_last")
    cut = (levels - 2) * unit
    stay = sum([[(a, 0, 2 * unit), (b, 0, cut)] for a, b in zip([early, *early_far], [late, *late_far])], [])
    places = [order.index(z) if z != 1 else None for z in range(1, levels)]

    def leaving(head, most, last):
        rows = [(head, 2 * unit, 3 * unit)]
        return rows + [(last, 0, unit) if p is None else (most, p * unit, (p + 1) * unit) for p in places]

    leave = sum([leaving(*arrays) for arrays in zip([early, *early_far], [most, *most_far], [leave[1], *last_far])], [])

    hidden, w_up = hidden_units(stay, w_gate, w_up, True)
    stay = [hidden] + over_blk(hidden, "hidden_stay")
    hidden, = hidden_units(leave, w_gate, w_up, False)
    stay, hidden, w_down = lax.optimization_barrier((stay, hidden, w_down))
    leave = [hidden] + over_blk(hidden, "hidden_leave")
    output = down_slices([stay, leave], half, place, loaded(w_down)[0])
    stay, leave = output[:blocks * half], output[blocks * half:]

    def back(pieces, turn, name):
        received = [pieces[:, z * unit:(z + 1) * unit] for z in range(levels)]
        for z in range(levels - 1, -1, -1):
            mask = z * 2 * ROW + turn
            if mask:
                received[z] = exchanged(received[z], mask, name)
        return received

    def to_owners(slices, name):
        return jnp.stack([slices[0]] + [shifted(slices[k], blocks - k, name) for k in range(1, blocks)])

    def by_blk(output):
        return output.reshape(blocks, half, output.shape[1])

    stay, leave = by_blk(stay), by_blk(leave)
    rear = [leave[:, z * unit:(z + 1) * unit] for z in range(2, levels)]
    for z in range(levels - 1, 1, -1):
        rear[z - 2] = exchanged(rear[z - 2], z * 2 * ROW + ROW, "back_leave")
    front = to_owners(jnp.concatenate([stay, leave[:, :2 * unit]], axis=1), "own_front")
    front = [front[:, z * unit:(z + 1) * unit] for z in range(levels + 2)]
    light = [front[1], front[levels], front[levels + 1]]
    light, rear[-1] = lax.optimization_barrier((light, rear[-1]))
    front[1], front[levels:] = light[0], light[1:]
    for z in range(levels - 1, 0, -1):
        front[z] = exchanged(front[z], z * 2 * ROW, "back_stay")
    for z in range(2):
        front[levels + z] = exchanged(front[levels + z], z * 2 * ROW + ROW, "back_leave")
    rear, front[2] = lax.optimization_barrier((rear, front[2]))
    rear = to_owners(jnp.concatenate(rear, axis=1), "own_rear")
    stay = jnp.concatenate(front[:levels], axis=1)
    leave = jnp.concatenate([*front[levels:], rear], axis=1)
    returned = [stay, exchanged(stay, CORE, "pair_stay"), leave, exchanged(leave, CORE, "pair_leave")]
    return mixed_rows(weighting, returned, place)


def solution(mesh):
    return jax.shard_map(
        on_device,
        mesh=mesh,
        in_specs=(
            P(("expert", "blk"), None),
            P(("expert", "blk"), None),
            P(("expert", "blk"), None),
            P("expert", None, "blk"),
            P("expert", None, "blk"),
            P("expert", None, "blk"),
        ),
        out_specs=P(("expert", "blk"), None),
        check_vma=False,
    )
```

```python
import functools

import jax
import jax.numpy as jnp
from jax import lax
from jax.experimental import pallas as pl
from jax.experimental.pallas import tpu as pltpu
from jax.sharding import PartitionSpec as P

CAP = 4
CORE, ROW = 1, 2
MIB = 1 << 20
PARTS = 4
ROOM = 13 * MIB


def exchanged(block, mask, name):
    size = lax.axis_size("expert")
    with jax.named_scope(f"{name}_{mask}"):
        return lax.ppermute(block, "expert", [(i, i ^ mask) for i in range(size)])


def shifted(block, steps, name):
    size = lax.axis_size("blk")
    with jax.named_scope(f"{name}_{steps}"):
        return lax.ppermute(block, "blk", [(i, (i + steps) % size) for i in range(size)])


def matmul(left, right):
    return jnp.dot(left, right, preferred_element_type=jnp.float32)


def tile_of(size, most):
    return max(t for t in range(128, most + 1, 128) if size % t == 0)


def prepare_kernel(levels, place, ids_ref, other_ids_ref, gates_ref, tokens_ref, other_ref, chosen_ref, weights_ref):
    tokens, rows = tokens_ref.shape[0], chosen_ref.shape[0]
    half = rows // 2
    row = lax.broadcasted_iota(jnp.int32, (rows, tokens), 0)
    slot = lax.rem(row, CAP).astype(jnp.float32)
    other_side = lax.rem(row // CAP, 2) == 1
    near = place[0] ^ ((row // half) * ROW + lax.rem(row // (2 * CAP), levels) * (2 * ROW))
    far = near ^ CORE
    earlier = lax.broadcasted_iota(jnp.int32, (tokens, tokens), 0) < lax.broadcasted_iota(jnp.int32, (tokens, tokens), 1)
    earlier = earlier.astype(jnp.float32).astype(jnp.bfloat16)

    def table(ids, labels):
        hits = jnp.zeros((rows, tokens), jnp.float32)
        weights = jnp.zeros((rows, tokens), jnp.float32)
        for j in range(ids.shape[0]):
            match = ids[j:j + 1, :] == labels
            hits = jnp.where(match, 1.0, hits)
            weights = jnp.where(match, gates_ref[j:j + 1, :].astype(jnp.float32), weights)
        before = matmul(hits.astype(jnp.bfloat16), earlier)
        return (hits > 0) & (before == slot), weights

    own, own_weights = table(ids_ref, near)
    other, _ = table(other_ids_ref, near)
    away, away_weights = table(ids_ref, far)
    own_weights = jnp.where(own & ~other_side, own_weights, 0.0)
    away_weights = jnp.where(away & other_side, away_weights, 0.0)
    weights = [own_weights[:half], away_weights[:half], own_weights[half:], away_weights[half:]]
    weights_ref[...] = jnp.concatenate(weights, axis=0).astype(weights_ref.dtype)
    own = jnp.where(own & ~other_side, 1.0, 0.0).astype(jnp.bfloat16)
    other = jnp.where(other & other_side, 1.0, 0.0).astype(jnp.bfloat16)
    tile = tile_of(tokens_ref.shape[1], 1024)
    for n in range(0, tokens_ref.shape[1], tile):
        columns = slice(n, n + tile)
        picked = matmul(own, tokens_ref[:, columns]) + matmul(other, other_ref[:, columns])
        chosen_ref[:, columns] = picked.astype(chosen_ref.dtype)


def prepared(levels, place, ids, other_ids, gates, tokens, other_tokens):
    rows = 4 * levels * CAP
    vmem = pl.BlockSpec(memory_space=pltpu.VMEM)
    return pl.pallas_call(
        functools.partial(prepare_kernel, levels),
        in_specs=[pl.BlockSpec(memory_space=pltpu.SMEM)] + [vmem] * 5,
        out_specs=[vmem, vmem],
        out_shape=[
            jax.ShapeDtypeStruct((rows, tokens.shape[1]), jnp.bfloat16),
            jax.ShapeDtypeStruct((2 * rows, tokens.shape[0]), jnp.bfloat16),
        ],
        compiler_params=pltpu.CompilerParams(vmem_limit_bytes=ROOM),
        cost_estimate=pl.CostEstimate(
            flops=4 * rows * tokens.size, bytes_accessed=4 * (tokens.size + rows * tokens.shape[1]), transcendentals=0
        ),
    )(place, ids, other_ids, gates, tokens, other_tokens)


def parts_of(size, unit):
    return max(p for p in range(1, PARTS + 1) if size % (p * unit) == 0)


def copies_of(source, target, sem, dim):
    count = parts_of(source.shape[dim], 128)
    step = source.shape[dim] // count
    copies = []
    for p in range(count):
        part = (0, pl.ds(p * step, step)) if dim == 1 else (0, slice(None), pl.ds(p * step, step))
        copies.append(pltpu.make_async_copy(source.at[part], target.at[part], sem.at[p]))
    return copies


def column_copies(source, target, sem, start):
    count = parts_of(source.shape[1], 128)
    step = source.shape[1] // count
    copies = []
    for p in range(count):
        rows = pl.ds(p * step, step)
        part = source.at[0, rows, pl.ds(start, target.shape[2])]
        copies.append(pltpu.make_async_copy(part, target.at[0, rows], sem.at[p]))
    return copies


def down_tile(width):
    return tile_of(width, 512)


def first_columns(width):
    tile = down_tile(width)
    return (width // tile + 1) // 2 * tile


def first_kernel(source, target, sem):
    copies = column_copies(source, target, sem, 0)
    for copy in copies:
        copy.start()
    for copy in copies:
        copy.wait()


def first_loaded(weight):
    shape = (1, weight.shape[1], first_columns(weight.shape[2]))
    return pl.pallas_call(
        first_kernel,
        in_specs=[pl.BlockSpec(memory_space=pltpu.HBM)],
        out_specs=pl.BlockSpec(memory_space=pltpu.VMEM),
        out_shape=pltpu.VMEM(shape, weight.dtype),
        scratch_shapes=[pltpu.SemaphoreType.DMA((PARTS,))],
        compiler_params=pltpu.CompilerParams(vmem_limit_bytes=ROOM),
        cost_estimate=pl.CostEstimate(
            flops=0, bytes_accessed=shape[1] * shape[2] * weight.dtype.itemsize, transcendentals=0
        ),
    )(pltpu.with_memory_space_constraint(weight, pltpu.HBM))


def load_kernel(count, *refs):
    sources, targets, sem = refs[:count], refs[count:-1], refs[-1]
    copies = []
    for number, (source, target) in enumerate(zip(sources, targets)):
        if len(source.shape) == 2:
            copies.append(pltpu.make_async_copy(source, target, sem.at[number, 0]))
        else:
            copies += copies_of(source, target, sem.at[number], 1)
    for copy in copies:
        copy.start()
    for copy in copies:
        copy.wait()


def loaded(*arrays):
    count = len(arrays)
    return pl.pallas_call(
        functools.partial(load_kernel, count),
        in_specs=[pl.BlockSpec(memory_space=pltpu.HBM)] * count,
        out_specs=[pl.BlockSpec(memory_space=pltpu.VMEM)] * count,
        out_shape=[pltpu.VMEM(array.shape, array.dtype) for array in arrays],
        scratch_shapes=[pltpu.SemaphoreType.DMA((count, PARTS))],
        compiler_params=pltpu.CompilerParams(vmem_limit_bytes=ROOM),
        cost_estimate=pl.CostEstimate(
            flops=0, bytes_accessed=sum(a.size * a.dtype.itemsize for a in arrays), transcendentals=0
        ),
    )(*[pltpu.with_memory_space_constraint(array, pltpu.HBM) for array in arrays])


def in_vmem(weight):
    return pltpu.with_memory_space_constraint(weight, pltpu.VMEM)


def gathered(pieces, ranges, rows_ref):
    rows = [piece[...].astype(jnp.float32)[start:stop] for piece, (start, stop) in zip(pieces, ranges)]
    rows_ref[...] = jnp.concatenate(rows, axis=0).astype(jnp.bfloat16)


def first_hidden_kernel(ranges, *refs):
    count = len(ranges)
    pieces, (gate_ref, up_hbm, out_ref, up_ref, rows_ref, gate_part, sem) = refs[:count], refs[count:]
    copies = copies_of(up_hbm, up_ref, sem, 2)
    for copy in copies:
        copy.start()
    gathered(pieces, ranges, rows_ref)
    tile = out_ref.shape[1] // len(copies)
    parts = [slice(p * tile, (p + 1) * tile) for p in range(len(copies))]
    for columns in parts:
        gate_part[:, columns] = jax.nn.silu(matmul(rows_ref[...], gate_ref[0, :, columns]))
    for columns, copy in zip(parts, copies):
        copy.wait()
        up_part = matmul(rows_ref[...], up_ref[0, :, columns])
        out_ref[:, columns] = (gate_part[:, columns] * up_part).astype(out_ref.dtype)


def hidden_kernel(ranges, *refs):
    count = len(ranges)
    pieces, (gate_ref, up_ref, out_ref, rows_ref) = refs[:count], refs[count:]
    gathered(pieces, ranges, rows_ref)
    tile = tile_of(out_ref.shape[1], 256)

    @pl.loop(0, out_ref.shape[1] // tile)
    def _(n):
        columns = pl.ds(pl.multiple_of(n * tile, tile), tile)
        gate_part = matmul(rows_ref[...], gate_ref[0, :, columns])
        up_part = matmul(rows_ref[...], up_ref[0, :, columns])
        out_ref[:, columns] = (jax.nn.silu(gate_part) * up_part).astype(out_ref.dtype)


def hidden_units(pieces, w_gate, w_up, first):
    depth, units = w_gate.shape[1:]
    ranges = [(start, stop) for _, start, stop in pieces]
    pieces = [piece for piece, _, _ in pieces]
    rows = sum(stop - start for start, stop in ranges)
    vmem = pl.BlockSpec(memory_space=pltpu.VMEM)
    place = pltpu.HBM if first else pltpu.VMEM
    out_shape = [jax.ShapeDtypeStruct((rows, units), jnp.bfloat16)]
    scratch = [pltpu.VMEM((rows, depth), jnp.bfloat16)]
    if first:
        out_shape.append(pltpu.VMEM(w_up.shape, w_up.dtype))
        scratch += [pltpu.VMEM((rows, units), jnp.float32), pltpu.SemaphoreType.DMA((PARTS,))]
    return pl.pallas_call(
        functools.partial(first_hidden_kernel if first else hidden_kernel, ranges),
        in_specs=[vmem] * (len(pieces) + 1) + [pl.BlockSpec(memory_space=place)],
        out_specs=[vmem] * len(out_shape),
        out_shape=out_shape,
        scratch_shapes=scratch,
        compiler_params=pltpu.CompilerParams(vmem_limit_bytes=max(ROOM, 10 * rows * (depth + units) + 2 * MIB)),
        cost_estimate=pl.CostEstimate(
            flops=4 * rows * depth * units,
            bytes_accessed=2 * rows * (depth + units),
            transcendentals=rows * units,
        ),
    )(*pieces, in_vmem(w_gate), pltpu.with_memory_space_constraint(w_up, place))


def down_kernel(half, groups, place, *refs):
    parts, (first_ref, weight_hbm, out_ref, rest_ref, sem) = refs[:-5], refs[-5:]
    size, units = len(parts) // groups, parts[0].shape[1]
    tile, first = down_tile(out_ref.shape[1]), first_ref.shape[2]
    copies = column_copies(weight_hbm, rest_ref, sem, first)
    for copy in copies:
        copy.start()

    def columns_of(weight_ref, start):
        @pl.loop(0, weight_ref.shape[2] // tile)
        def _(n):
            columns = pl.ds(pl.multiple_of(n * tile, tile), tile)
            total = jnp.zeros((out_ref.shape[0], tile), jnp.float32)
            for k in range(size):
                owner = lax.rem(place[0] + (size - k), size)
                rows = pl.ds(pl.multiple_of(owner * units, units), units)
                left = []
                for part in parts[k::size]:
                    left += [part[-k * half:], part[:-k * half]] if k else [part[...]]
                total += matmul(jnp.concatenate(left, axis=0), weight_ref[0, rows, columns])
            out_ref[:, pl.ds(pl.multiple_of(start + n * tile, tile), tile)] = total.astype(out_ref.dtype)

    columns_of(first_ref, 0)
    for copy in copies:
        copy.wait()
    columns_of(rest_ref, first)


def down_slices(groups, half, place, first, w_down):
    units, width = w_down.shape[1:]
    parts = sum(groups, [])
    rows = sum(parts[0].shape[0] for parts in groups)
    rest = (1, units, width - first.shape[2])
    vmem = pl.BlockSpec(memory_space=pltpu.VMEM)
    limit = max(ROOM, 8 * rows * (units + width) + 2 * MIB) + 2 * rest[1] * rest[2]
    return pl.pallas_call(
        functools.partial(down_kernel, half, len(groups)),
        in_specs=[pl.BlockSpec(memory_space=pltpu.SMEM)]
        + [vmem] * (len(parts) + 1)
        + [pl.BlockSpec(memory_space=pltpu.HBM)],
        out_specs=vmem,
        out_shape=jax.ShapeDtypeStruct((rows, width), jnp.bfloat16),
        scratch_shapes=[pltpu.VMEM(rest, w_down.dtype), pltpu.SemaphoreType.DMA((PARTS,))],
        compiler_params=pltpu.CompilerParams(vmem_limit_bytes=limit),
        cost_estimate=pl.CostEstimate(
            flops=2 * rows * units * width,
            bytes_accessed=2 * rows * (units + width),
            transcendentals=0,
        ),
    )(place, *parts, in_vmem(first), pltpu.with_memory_space_constraint(w_down, pltpu.HBM))


def mix_kernel(blocks, *refs):
    place, weights, pieces, out_ref = refs[0], refs[1], refs[2:-1], refs[-1]
    width = out_ref.shape[1] // blocks
    tile = tile_of(width, 512)
    for k in range(blocks):
        start = lax.rem(place[0] + k, blocks) * width
        for n in range(0, width, tile):
            rows = jnp.concatenate([piece[k, :, n:n + tile] for piece in pieces], axis=0)
            columns = pl.ds(pl.multiple_of(start + n, 128), tile)
            total = lax.dot_general(
                weights[...], rows, (((0,), (0,)), ((), ())), preferred_element_type=jnp.float32
            )
            out_ref[:, columns] = total.astype(out_ref.dtype)


def mixed_rows(weights, pieces, place):
    blocks, half, width = pieces[0].shape
    tokens = weights.shape[1]
    return pl.pallas_call(
        functools.partial(mix_kernel, blocks),
        in_specs=[pl.BlockSpec(memory_space=pltpu.SMEM)]
        + [pl.BlockSpec(memory_space=pltpu.VMEM)] * (len(pieces) + 1),
        out_specs=pl.BlockSpec(memory_space=pltpu.VMEM),
        out_shape=jax.ShapeDtypeStruct((tokens, blocks * width), jnp.bfloat16),
        compiler_params=pltpu.CompilerParams(
            vmem_limit_bytes=4 * blocks * width * (len(pieces) * half + tokens) + 2 * MIB
        ),
    )(place, weights, *pieces)


def on_device(tokens, expert_ids, gate_weights, w_gate, w_up, w_down):
    experts, blocks = lax.axis_size("expert"), lax.axis_size("blk")
    me, mine = lax.axis_index("expert"), lax.axis_index("blk")
    levels = experts // 4
    unit = 2 * CAP
    half = levels * unit
    down_mat = w_down[0]

    place = mine.reshape(1).astype(jnp.int32)
    ids = expert_ids.T
    other_ids = exchanged(ids, CORE, "ids")
    other_tokens = exchanged(tokens, CORE, "tokens")
    near_ids, near_gates, near_tokens = loaded(ids, gate_weights.T, tokens)
    chosen, weighting = prepared(
        levels, me.reshape(1).astype(jnp.int32), near_ids, other_ids, near_gates, near_tokens, other_tokens
    )
    w_gate, place, weighting, chosen = lax.optimization_barrier((w_gate, place, weighting, chosen))

    def split(rows):
        return [rows[z * unit:(z + 1) * unit] for z in range(levels)]

    def over_blk(piece, name):
        return [shifted(piece, k, name) for k in range(1, blocks)]

    stay, leave = split(chosen[:half]), split(chosen[half:])
    for z in range(levels - 1, 0, -1):
        stay[z] = exchanged(stay[z], z * 2 * ROW, "go_stay")
    leave[0] = exchanged(leave[0], ROW, "go_leave")
    early = jnp.concatenate([stay[0], stay[1], leave[0]], axis=0)
    late = jnp.concatenate(stay[2:], axis=0)
    early, leave[1:] = lax.optimization_barrier((early, leave[1:]))
    early_far, late_far = over_blk(early, "blk_early"), over_blk(late, "blk_late")
    for z in [1, *range(levels - 1, 2, -1)]:
        leave[z] = exchanged(leave[z], z * 2 * ROW + ROW, "go_leave")
    early_far, leave[1], leave[2] = lax.optimization_barrier((early_far, leave[1], leave[2]))
    leave[2] = exchanged(leave[2], 2 * 2 * ROW + ROW, "go_leave")
    late, w_gate = lax.optimization_barrier((late, w_gate))
    w_gate, = loaded(w_gate)
    order = [*range(levels - 1, 1, -1)]
    most = jnp.concatenate([leave[z] for z in order], axis=0)
    most, w_gate = lax.optimization_barrier((most, w_gate))
    most_far, last_far = over_blk(most, "blk_most"), over_blk(leave[1], "blk_last")
    cut = (levels - 2) * unit
    stay = sum([[(a, 0, 2 * unit), (b, 0, cut)] for a, b in zip([early, *early_far], [late, *late_far])], [])
    places = [order.index(z) if z != 1 else None for z in range(1, levels)]

    def leaving(head, most, last):
        rows = [(head, 2 * unit, 3 * unit)]
        return rows + [(last, 0, unit) if p is None else (most, p * unit, (p + 1) * unit) for p in places]

    leave = sum([leaving(*arrays) for arrays in zip([early, *early_far], [most, *most_far], [leave[1], *last_far])], [])

    hidden, w_up = hidden_units(stay, w_gate, w_up, True)
    stay = [hidden] + over_blk(hidden, "hidden_stay")
    hidden, = hidden_units(leave, w_gate, w_up, False)
    stay, hidden, w_down = lax.optimization_barrier((stay, hidden, w_down))
    leave = [hidden] + over_blk(hidden, "hidden_leave")
    output = down_slices([stay, leave], half, place, first_loaded(w_down), w_down)
    stay, leave = output[:blocks * half], output[blocks * half:]

    def back(pieces, turn, name):
        received = [pieces[:, z * unit:(z + 1) * unit] for z in range(levels)]
        for z in range(levels - 1, -1, -1):
            mask = z * 2 * ROW + turn
            if mask:
                received[z] = exchanged(received[z], mask, name)
        return received

    def to_owners(slices, name):
        return jnp.stack([slices[0]] + [shifted(slices[k], blocks - k, name) for k in range(1, blocks)])

    def by_blk(output):
        return output.reshape(blocks, half, output.shape[1])

    stay, leave = by_blk(stay), by_blk(leave)
    rear = [leave[:, z * unit:(z + 1) * unit] for z in range(2, levels)]
    for z in range(levels - 1, 1, -1):
        rear[z - 2] = exchanged(rear[z - 2], z * 2 * ROW + ROW, "back_leave")
    front = to_owners(jnp.concatenate([stay, leave[:, :2 * unit]], axis=1), "own_front")
    front = [front[:, z * unit:(z + 1) * unit] for z in range(levels + 2)]
    light = [front[1], front[levels], front[levels + 1]]
    light, rear[-1] = lax.optimization_barrier((light, rear[-1]))
    front[1], front[levels:] = light[0], light[1:]
    for z in range(levels - 1, 0, -1):
        front[z] = exchanged(front[z], z * 2 * ROW, "back_stay")
    for z in range(2):
        front[levels + z] = exchanged(front[levels + z], z * 2 * ROW + ROW, "back_leave")
    rear, front[2] = lax.optimization_barrier((rear, front[2]))
    rear = to_owners(jnp.concatenate(rear, axis=1), "own_rear")
    stay = jnp.concatenate(front[:levels], axis=1)
    leave = jnp.concatenate([*front[levels:], rear], axis=1)
    returned = [stay, exchanged(stay, CORE, "pair_stay"), leave, exchanged(leave, CORE, "pair_leave")]
    return mixed_rows(weighting, returned, place)


def solution(mesh):
    return jax.shard_map(
        on_device,
        mesh=mesh,
        in_specs=(
            P(("expert", "blk"), None),
            P(("expert", "blk"), None),
            P(("expert", "blk"), None),
            P("expert", None, "blk"),
            P("expert", None, "blk"),
            P("expert", None, "blk"),
        ),
        out_specs=P(("expert", "blk"), None),
        check_vma=False,
    )
```

```python
import functools

import jax
import jax.numpy as jnp
from jax import lax
from jax.experimental import pallas as pl
from jax.experimental.pallas import tpu as pltpu
from jax.sharding import PartitionSpec as P

CAP = 4
CORE, ROW = 1, 2
MIB = 1 << 20
PARTS = 4
ROOM = 13 * MIB


def exchanged(block, mask, name):
    size = lax.axis_size("expert")
    with jax.named_scope(f"{name}_{mask}"):
        return lax.ppermute(block, "expert", [(i, i ^ mask) for i in range(size)])


def shifted(block, steps, name):
    size = lax.axis_size("blk")
    with jax.named_scope(f"{name}_{steps}"):
        return lax.ppermute(block, "blk", [(i, (i + steps) % size) for i in range(size)])


def matmul(left, right):
    return jnp.dot(left, right, preferred_element_type=jnp.float32)


def tile_of(size, most):
    return max(t for t in range(128, most + 1, 128) if size % t == 0)


def prepare_kernel(levels, place, ids_ref, other_ids_ref, gates_ref, tokens_ref, other_ref, chosen_ref, weights_ref):
    tokens, rows = tokens_ref.shape[0], chosen_ref.shape[0]
    half = rows // 2
    row = lax.broadcasted_iota(jnp.int32, (rows, tokens), 0)
    slot = lax.rem(row, CAP).astype(jnp.float32)
    other_side = lax.rem(row // CAP, 2) == 1
    near = place[0] ^ ((row // half) * ROW + lax.rem(row // (2 * CAP), levels) * (2 * ROW))
    far = near ^ CORE
    earlier = lax.broadcasted_iota(jnp.int32, (tokens, tokens), 0) < lax.broadcasted_iota(jnp.int32, (tokens, tokens), 1)
    earlier = earlier.astype(jnp.float32).astype(jnp.bfloat16)

    def table(ids, labels):
        hits = jnp.zeros((rows, tokens), jnp.float32)
        weights = jnp.zeros((rows, tokens), jnp.float32)
        for j in range(ids.shape[0]):
            match = ids[j:j + 1, :] == labels
            hits = jnp.where(match, 1.0, hits)
            weights = jnp.where(match, gates_ref[j:j + 1, :].astype(jnp.float32), weights)
        before = matmul(hits.astype(jnp.bfloat16), earlier)
        return (hits > 0) & (before == slot), weights

    own, own_weights = table(ids_ref, near)
    other, _ = table(other_ids_ref, near)
    away, away_weights = table(ids_ref, far)
    own_weights = jnp.where(own & ~other_side, own_weights, 0.0)
    away_weights = jnp.where(away & other_side, away_weights, 0.0)
    weights = [own_weights[:half], away_weights[:half], own_weights[half:], away_weights[half:]]
    weights_ref[...] = jnp.concatenate(weights, axis=0).astype(weights_ref.dtype)
    own = jnp.where(own & ~other_side, 1.0, 0.0).astype(jnp.bfloat16)
    other = jnp.where(other & other_side, 1.0, 0.0).astype(jnp.bfloat16)
    tile = tile_of(tokens_ref.shape[1], 1024)
    for n in range(0, tokens_ref.shape[1], tile):
        columns = slice(n, n + tile)
        picked = matmul(own, tokens_ref[:, columns]) + matmul(other, other_ref[:, columns])
        chosen_ref[:, columns] = picked.astype(chosen_ref.dtype)


def prepared(levels, place, ids, other_ids, gates, tokens, other_tokens):
    rows = 4 * levels * CAP
    vmem = pl.BlockSpec(memory_space=pltpu.VMEM)
    return pl.pallas_call(
        functools.partial(prepare_kernel, levels),
        in_specs=[pl.BlockSpec(memory_space=pltpu.SMEM)] + [vmem] * 5,
        out_specs=[vmem, vmem],
        out_shape=[
            jax.ShapeDtypeStruct((rows, tokens.shape[1]), jnp.bfloat16),
            jax.ShapeDtypeStruct((2 * rows, tokens.shape[0]), jnp.bfloat16),
        ],
        compiler_params=pltpu.CompilerParams(vmem_limit_bytes=ROOM),
        cost_estimate=pl.CostEstimate(
            flops=4 * rows * tokens.size, bytes_accessed=4 * (tokens.size + rows * tokens.shape[1]), transcendentals=0
        ),
    )(place, ids, other_ids, gates, tokens, other_tokens)


def parts_of(size, unit):
    return max(p for p in range(1, PARTS + 1) if size % (p * unit) == 0)


def copies_of(source, target, sem, dim):
    count = parts_of(source.shape[dim], 128)
    step = source.shape[dim] // count
    copies = []
    for p in range(count):
        part = (0, pl.ds(p * step, step)) if dim == 1 else (0, slice(None), pl.ds(p * step, step))
        copies.append(pltpu.make_async_copy(source.at[part], target.at[part], sem.at[p]))
    return copies


def column_copies(source, target, sem, start):
    count = parts_of(source.shape[1], 128)
    step = source.shape[1] // count
    copies = []
    for p in range(count):
        rows = pl.ds(p * step, step)
        part = source.at[0, rows, pl.ds(start, target.shape[2])]
        copies.append(pltpu.make_async_copy(part, target.at[0, rows], sem.at[p]))
    return copies


def down_tile(width):
    return tile_of(width, 512)


def first_columns(width):
    tile = down_tile(width)
    return (2 * (width // tile) + 2) // 3 * tile


def first_kernel(source, target, sem):
    copies = column_copies(source, target, sem, 0)
    for copy in copies:
        copy.start()
    for copy in copies:
        copy.wait()


def first_loaded(weight):
    shape = (1, weight.shape[1], first_columns(weight.shape[2]))
    return pl.pallas_call(
        first_kernel,
        in_specs=[pl.BlockSpec(memory_space=pltpu.HBM)],
        out_specs=pl.BlockSpec(memory_space=pltpu.VMEM),
        out_shape=pltpu.VMEM(shape, weight.dtype),
        scratch_shapes=[pltpu.SemaphoreType.DMA((PARTS,))],
        compiler_params=pltpu.CompilerParams(vmem_limit_bytes=ROOM),
        cost_estimate=pl.CostEstimate(
            flops=0, bytes_accessed=shape[1] * shape[2] * weight.dtype.itemsize, transcendentals=0
        ),
    )(pltpu.with_memory_space_constraint(weight, pltpu.HBM))


def load_kernel(count, *refs):
    sources, targets, sem = refs[:count], refs[count:-1], refs[-1]
    copies = []
    for number, (source, target) in enumerate(zip(sources, targets)):
        if len(source.shape) == 2:
            copies.append(pltpu.make_async_copy(source, target, sem.at[number, 0]))
        else:
            copies += copies_of(source, target, sem.at[number], 1)
    for copy in copies:
        copy.start()
    for copy in copies:
        copy.wait()


def loaded(*arrays):
    count = len(arrays)
    return pl.pallas_call(
        functools.partial(load_kernel, count),
        in_specs=[pl.BlockSpec(memory_space=pltpu.HBM)] * count,
        out_specs=[pl.BlockSpec(memory_space=pltpu.VMEM)] * count,
        out_shape=[pltpu.VMEM(array.shape, array.dtype) for array in arrays],
        scratch_shapes=[pltpu.SemaphoreType.DMA((count, PARTS))],
        compiler_params=pltpu.CompilerParams(vmem_limit_bytes=ROOM),
        cost_estimate=pl.CostEstimate(
            flops=0, bytes_accessed=sum(a.size * a.dtype.itemsize for a in arrays), transcendentals=0
        ),
    )(*[pltpu.with_memory_space_constraint(array, pltpu.HBM) for array in arrays])


def in_vmem(weight):
    return pltpu.with_memory_space_constraint(weight, pltpu.VMEM)


def gathered(pieces, ranges, rows_ref):
    rows = [piece[...].astype(jnp.float32)[start:stop] for piece, (start, stop) in zip(pieces, ranges)]
    rows_ref[...] = jnp.concatenate(rows, axis=0).astype(jnp.bfloat16)


def first_hidden_kernel(ranges, *refs):
    count = len(ranges)
    pieces, (gate_ref, up_hbm, out_ref, up_ref, rows_ref, gate_part, sem) = refs[:count], refs[count:]
    copies = copies_of(up_hbm, up_ref, sem, 2)
    for copy in copies:
        copy.start()
    gathered(pieces, ranges, rows_ref)
    tile = out_ref.shape[1] // len(copies)
    parts = [slice(p * tile, (p + 1) * tile) for p in range(len(copies))]
    for columns in parts:
        gate_part[:, columns] = jax.nn.silu(matmul(rows_ref[...], gate_ref[0, :, columns]))
    for columns, copy in zip(parts, copies):
        copy.wait()
        up_part = matmul(rows_ref[...], up_ref[0, :, columns])
        out_ref[:, columns] = (gate_part[:, columns] * up_part).astype(out_ref.dtype)


def hidden_kernel(ranges, *refs):
    count = len(ranges)
    pieces, (gate_ref, up_ref, out_ref, rows_ref) = refs[:count], refs[count:]
    gathered(pieces, ranges, rows_ref)
    tile = tile_of(out_ref.shape[1], 256)

    @pl.loop(0, out_ref.shape[1] // tile)
    def _(n):
        columns = pl.ds(pl.multiple_of(n * tile, tile), tile)
        gate_part = matmul(rows_ref[...], gate_ref[0, :, columns])
        up_part = matmul(rows_ref[...], up_ref[0, :, columns])
        out_ref[:, columns] = (jax.nn.silu(gate_part) * up_part).astype(out_ref.dtype)


def hidden_units(pieces, w_gate, w_up, first):
    depth, units = w_gate.shape[1:]
    ranges = [(start, stop) for _, start, stop in pieces]
    pieces = [piece for piece, _, _ in pieces]
    rows = sum(stop - start for start, stop in ranges)
    vmem = pl.BlockSpec(memory_space=pltpu.VMEM)
    place = pltpu.HBM if first else pltpu.VMEM
    out_shape = [jax.ShapeDtypeStruct((rows, units), jnp.bfloat16)]
    scratch = [pltpu.VMEM((rows, depth), jnp.bfloat16)]
    if first:
        out_shape.append(pltpu.VMEM(w_up.shape, w_up.dtype))
        scratch += [pltpu.VMEM((rows, units), jnp.float32), pltpu.SemaphoreType.DMA((PARTS,))]
    return pl.pallas_call(
        functools.partial(first_hidden_kernel if first else hidden_kernel, ranges),
        in_specs=[vmem] * (len(pieces) + 1) + [pl.BlockSpec(memory_space=place)],
        out_specs=[vmem] * len(out_shape),
        out_shape=out_shape,
        scratch_shapes=scratch,
        compiler_params=pltpu.CompilerParams(vmem_limit_bytes=max(ROOM, 10 * rows * (depth + units) + 2 * MIB)),
        cost_estimate=pl.CostEstimate(
            flops=4 * rows * depth * units,
            bytes_accessed=2 * rows * (depth + units),
            transcendentals=rows * units,
        ),
    )(*pieces, in_vmem(w_gate), pltpu.with_memory_space_constraint(w_up, place))


def down_kernel(half, groups, place, *refs):
    parts, (first_ref, weight_hbm, out_ref, rest_ref, sem) = refs[:-5], refs[-5:]
    size, units = len(parts) // groups, parts[0].shape[1]
    tile, first = down_tile(out_ref.shape[1]), first_ref.shape[2]
    copies = column_copies(weight_hbm, rest_ref, sem, first)
    for copy in copies:
        copy.start()

    def columns_of(weight_ref, start):
        @pl.loop(0, weight_ref.shape[2] // tile)
        def _(n):
            columns = pl.ds(pl.multiple_of(n * tile, tile), tile)
            total = jnp.zeros((out_ref.shape[0], tile), jnp.float32)
            for k in range(size):
                owner = lax.rem(place[0] + (size - k), size)
                rows = pl.ds(pl.multiple_of(owner * units, units), units)
                left = []
                for part in parts[k::size]:
                    left += [part[-k * half:], part[:-k * half]] if k else [part[...]]
                total += matmul(jnp.concatenate(left, axis=0), weight_ref[0, rows, columns])
            out_ref[:, pl.ds(pl.multiple_of(start + n * tile, tile), tile)] = total.astype(out_ref.dtype)

    columns_of(first_ref, 0)
    for copy in copies:
        copy.wait()
    columns_of(rest_ref, first)


def down_slices(groups, half, place, first, w_down):
    units, width = w_down.shape[1:]
    parts = sum(groups, [])
    rows = sum(parts[0].shape[0] for parts in groups)
    rest = (1, units, width - first.shape[2])
    vmem = pl.BlockSpec(memory_space=pltpu.VMEM)
    limit = max(ROOM, 8 * rows * (units + width) + 2 * MIB) + 2 * rest[1] * rest[2]
    return pl.pallas_call(
        functools.partial(down_kernel, half, len(groups)),
        in_specs=[pl.BlockSpec(memory_space=pltpu.SMEM)]
        + [vmem] * (len(parts) + 1)
        + [pl.BlockSpec(memory_space=pltpu.HBM)],
        out_specs=vmem,
        out_shape=jax.ShapeDtypeStruct((rows, width), jnp.bfloat16),
        scratch_shapes=[pltpu.VMEM(rest, w_down.dtype), pltpu.SemaphoreType.DMA((PARTS,))],
        compiler_params=pltpu.CompilerParams(vmem_limit_bytes=limit),
        cost_estimate=pl.CostEstimate(
            flops=2 * rows * units * width,
            bytes_accessed=2 * rows * (units + width),
            transcendentals=0,
        ),
    )(place, *parts, in_vmem(first), pltpu.with_memory_space_constraint(w_down, pltpu.HBM))


def mix_kernel(blocks, *refs):
    place, weights, pieces, out_ref = refs[0], refs[1], refs[2:-1], refs[-1]
    width = out_ref.shape[1] // blocks
    tile = tile_of(width, 512)
    for k in range(blocks):
        start = lax.rem(place[0] + k, blocks) * width
        for n in range(0, width, tile):
            rows = jnp.concatenate([piece[k, :, n:n + tile] for piece in pieces], axis=0)
            columns = pl.ds(pl.multiple_of(start + n, 128), tile)
            total = lax.dot_general(
                weights[...], rows, (((0,), (0,)), ((), ())), preferred_element_type=jnp.float32
            )
            out_ref[:, columns] = total.astype(out_ref.dtype)


def mixed_rows(weights, pieces, place):
    blocks, half, width = pieces[0].shape
    tokens = weights.shape[1]
    return pl.pallas_call(
        functools.partial(mix_kernel, blocks),
        in_specs=[pl.BlockSpec(memory_space=pltpu.SMEM)]
        + [pl.BlockSpec(memory_space=pltpu.VMEM)] * (len(pieces) + 1),
        out_specs=pl.BlockSpec(memory_space=pltpu.VMEM),
        out_shape=jax.ShapeDtypeStruct((tokens, blocks * width), jnp.bfloat16),
        compiler_params=pltpu.CompilerParams(
            vmem_limit_bytes=4 * blocks * width * (len(pieces) * half + tokens) + 2 * MIB
        ),
    )(place, weights, *pieces)


def on_device(tokens, expert_ids, gate_weights, w_gate, w_up, w_down):
    experts, blocks = lax.axis_size("expert"), lax.axis_size("blk")
    me, mine = lax.axis_index("expert"), lax.axis_index("blk")
    levels = experts // 4
    unit = 2 * CAP
    half = levels * unit
    down_mat = w_down[0]

    place = mine.reshape(1).astype(jnp.int32)
    ids = expert_ids.T
    other_ids = exchanged(ids, CORE, "ids")
    other_tokens = exchanged(tokens, CORE, "tokens")
    near_ids, near_gates, near_tokens = loaded(ids, gate_weights.T, tokens)
    chosen, weighting = prepared(
        levels, me.reshape(1).astype(jnp.int32), near_ids, other_ids, near_gates, near_tokens, other_tokens
    )
    w_gate, place, weighting, chosen = lax.optimization_barrier((w_gate, place, weighting, chosen))

    def split(rows):
        return [rows[z * unit:(z + 1) * unit] for z in range(levels)]

    def over_blk(piece, name):
        return [shifted(piece, k, name) for k in range(1, blocks)]

    stay, leave = split(chosen[:half]), split(chosen[half:])
    for z in range(levels - 1, 0, -1):
        stay[z] = exchanged(stay[z], z * 2 * ROW, "go_stay")
    leave[0] = exchanged(leave[0], ROW, "go_leave")
    early = jnp.concatenate([stay[0], stay[1], leave[0]], axis=0)
    late = jnp.concatenate(stay[2:], axis=0)
    early, leave[1:] = lax.optimization_barrier((early, leave[1:]))
    early_far, late_far = over_blk(early, "blk_early"), over_blk(late, "blk_late")
    for z in [1, *range(levels - 1, 2, -1)]:
        leave[z] = exchanged(leave[z], z * 2 * ROW + ROW, "go_leave")
    early_far, leave[1], leave[2] = lax.optimization_barrier((early_far, leave[1], leave[2]))
    leave[2] = exchanged(leave[2], 2 * 2 * ROW + ROW, "go_leave")
    late, w_gate = lax.optimization_barrier((late, w_gate))
    w_gate, = loaded(w_gate)
    order = [*range(levels - 1, 1, -1)]
    most = jnp.concatenate([leave[z] for z in order], axis=0)
    most, w_gate = lax.optimization_barrier((most, w_gate))
    most_far, last_far = over_blk(most, "blk_most"), over_blk(leave[1], "blk_last")
    cut = (levels - 2) * unit
    stay = sum([[(a, 0, 2 * unit), (b, 0, cut)] for a, b in zip([early, *early_far], [late, *late_far])], [])
    places = [order.index(z) if z != 1 else None for z in range(1, levels)]

    def leaving(head, most, last):
        rows = [(head, 2 * unit, 3 * unit)]
        return rows + [(last, 0, unit) if p is None else (most, p * unit, (p + 1) * unit) for p in places]

    leave = sum([leaving(*arrays) for arrays in zip([early, *early_far], [most, *most_far], [leave[1], *last_far])], [])

    hidden, w_up = hidden_units(stay, w_gate, w_up, True)
    stay = [hidden] + over_blk(hidden, "hidden_stay")
    hidden, = hidden_units(leave, w_gate, w_up, False)
    stay, hidden, w_down = lax.optimization_barrier((stay, hidden, w_down))
    leave = [hidden] + over_blk(hidden, "hidden_leave")
    output = down_slices([stay, leave], half, place, first_loaded(w_down), w_down)
    stay, leave = output[:blocks * half], output[blocks * half:]

    def back(pieces, turn, name):
        received = [pieces[:, z * unit:(z + 1) * unit] for z in range(levels)]
        for z in range(levels - 1, -1, -1):
            mask = z * 2 * ROW + turn
            if mask:
                received[z] = exchanged(received[z], mask, name)
        return received

    def to_owners(slices, name):
        return jnp.stack([slices[0]] + [shifted(slices[k], blocks - k, name) for k in range(1, blocks)])

    def by_blk(output):
        return output.reshape(blocks, half, output.shape[1])

    stay, leave = by_blk(stay), by_blk(leave)
    rear = [leave[:, z * unit:(z + 1) * unit] for z in range(2, levels)]
    for z in range(levels - 1, 1, -1):
        rear[z - 2] = exchanged(rear[z - 2], z * 2 * ROW + ROW, "back_leave")
    front = to_owners(jnp.concatenate([stay, leave[:, :2 * unit]], axis=1), "own_front")
    front = [front[:, z * unit:(z + 1) * unit] for z in range(levels + 2)]
    light = [front[1], front[levels], front[levels + 1]]
    light, rear[-1] = lax.optimization_barrier((light, rear[-1]))
    front[1], front[levels:] = light[0], light[1:]
    for z in range(levels - 1, 0, -1):
        front[z] = exchanged(front[z], z * 2 * ROW, "back_stay")
    for z in range(2):
        front[levels + z] = exchanged(front[levels + z], z * 2 * ROW + ROW, "back_leave")
    rear, front[2] = lax.optimization_barrier((rear, front[2]))
    rear = to_owners(jnp.concatenate(rear, axis=1), "own_rear")
    stay = jnp.concatenate(front[:levels], axis=1)
    leave = jnp.concatenate([*front[levels:], rear], axis=1)
    returned = [stay, exchanged(stay, CORE, "pair_stay"), leave, exchanged(leave, CORE, "pair_leave")]
    return mixed_rows(weighting, returned, place)


def solution(mesh):
    return jax.shard_map(
        on_device,
        mesh=mesh,
        in_specs=(
            P(("expert", "blk"), None),
            P(("expert", "blk"), None),
            P(("expert", "blk"), None),
            P("expert", None, "blk"),
            P("expert", None, "blk"),
            P("expert", None, "blk"),
        ),
        out_specs=P(("expert", "blk"), None),
        check_vma=False,
    )
```
